32 devices in a mesh: dp: 4 (over z), row: 4 (over y, core), col: 2 (over x).
Axes of the slice: x: 2, y: 2, z: 4, core: 2. Of those that a mesh axis runs over, the one named last changes fastest.
Arguments:
- hidden_in: bfloat16 [1536, 16384], P('col', ('dp', 'row')), may hold values from -6 to 6
- grad_out: bfloat16 [1536, 16384], P('col', ('dp', 'row')), may hold values from -6 to 6
- lengths: int32 [4, 3], P('dp'), may hold values from 512 to 2048, as said below
- norm_gain: bfloat16 [1536], replicated, may hold values from 0.5 to 1.5
- inner_proj: bfloat16 [3072, 2, 1536], P('col', None, 'row'), may hold values from -0.15625 to 0.15625
- state_proj: bfloat16 [1536, 256], P('row'), may hold values from -0.15625 to 0.15625
- step_proj: bfloat16 [48, 1536], P('col', 'row'), may hold values from -0.15625 to 0.15625
- conv_inner: bfloat16 [4, 3072], P(None, 'col'), may hold values from -3 to 3
- conv_inner_bias: bfloat16 [3072], P('col'), may hold values from -3 to 3
- conv_state: bfloat16 [4, 256], replicated, may hold values from -3 to 3
- conv_state_bias: bfloat16 [256], replicated, may hold values from -3 to 3
- step_bias: float32 [48], P('col'), may hold values from -5 to -1
- decay_log: float32 [48], P('col'), may hold values from -5 to 2.5
- skip_gain: float32 [48], P('col'), may hold values from 0.5 to 1.5
- gate_gain: bfloat16 [3072], P('col'), may hold values from 0.5 to 1.5
- out_proj: bfloat16 [3072, 1536], P('col', 'row'), may hold values from -0.109375 to 0.109375
Outputs:
- block_out: bfloat16 [1536, 16384], P('col', ('dp', 'row'))
- grad_in: bfloat16 [1536, 16384], P('col', ('dp', 'row'))
- grad_norm_gain: float32 [1536], replicated
- grad_inner_proj: float32 [3072, 2, 1536], P('col', None, ('dp', 'row'))
- grad_state_proj: float32 [1536, 256], replicated
- grad_step_proj: float32 [48, 1536], P('col', ('dp', 'row'))
- grad_conv_inner: float32 [4, 3072], replicated
- grad_inner_bias: float32 [3072], replicated
- grad_conv_state: float32 [4, 256], replicated
- grad_state_bias: float32 [256], replicated
- grad_step_bias: float32 [48], replicated
- grad_decay_log: float32 [48], replicated
- grad_skip_gain: float32 [48], replicated
- grad_gate_gain: float32 [3072], replicated
- grad_out_proj: float32 [3072, 1536], P('col', ('dp', 'row'))
The draws below stay inside these ranges and needn't reach their ends.
Inputs may be any that keep to these rules, and one draw needn't show every extreme that they name: In every group one length, at a place drawn from the seed, is exactly 2048; the other lengths lie between 512 and 1024, so a group's lengths sum to at most 4096.
All inputs are finite; a program needn't handle non-finite values.
Results may differ from the reference program's by a relative error of at most 0.012.
The reference program's roundings to bfloat16 on the way (of `normed` and `gated`) count: a program that leaves them out, or rounds other values in their place, can miss the bound.
Values may be sent and summed in bfloat16 or wider, within the bound.
A program may use at most 320 MiB of HBM per device.

```python
import jax
import jax.numpy as jnp
from jax import lax

D = 1536
HEADS = 48
HEADDIM = 64
STATE = 128
INNER = 3072
CONV = 4
SPAN = 256
LEN_MAX = 2048
LEN_MIN = 512
GROUP_TOK = 4096
SEQS = 3
TOKENS = 16384
N_DP = 4
N_COL = 2


def draw_lengths(key, part):
    key = jax.random.fold_in(key, 11)
    first, second, third = jax.random.split(key, 3)
    others = jax.random.randint(first, (N_DP, SEQS), LEN_MIN, LEN_MAX // 2 + 1)
    where_long = jax.random.randint(second, (N_DP,), 0, SEQS)
    forced_group = jax.random.randint(third, (), 0, N_DP)
    index = jnp.arange(SEQS)[None, :]
    groups = jnp.arange(N_DP)[:, None]
    short_spot = (index == ((where_long + 1) % SEQS)[:, None]) & (groups == forced_group)
    result = jnp.where(short_spot, LEN_MIN, others)
    result = jnp.where(index == where_long[:, None], LEN_MAX, result)
    return result.astype(jnp.int32)


def block_levels(own_key, extent, shards, smallest, top_value):
    level, own = 1.0, jax.random.fold_in(own_key, 6)
    for dim, blocks in shards:
        heights = jnp.exp(jax.random.uniform(jax.random.fold_in(own, dim), (blocks,), jnp.float32, smallest / len(shards), top_value / len(shards)))
        level = level * jnp.repeat(heights, extent[dim] // blocks).reshape([-1 if axis == dim else 1 for axis in range(len(extent))])
    return level


def scatter_about(stream_key, extent, scale, reach, shards=(), held_as=jnp.bfloat16):
    loudness = block_levels(stream_key, extent, shards, -0.22, 0.18) if shards else 1.0
    entries = jax.random.normal(stream_key, extent, jnp.float32) * scale * loudness
    return jnp.minimum(jnp.maximum(entries, -reach), reach).astype(held_as)


def setup_inputs(seed: int = 0) -> dict:
    key_list = jax.random.split(jax.random.key(seed), 17)
    return {
        "hidden_in": scatter_about(key_list[0], (D, TOKENS), 1.0, 6.0, ((0, 2), (1, 16))),
        "grad_out": scatter_about(key_list[1], (D, TOKENS), 1.0, 6.0, ((0, 2), (1, 16))),
        "lengths": draw_lengths(jax.random.fold_in(key_list[16], 71), 0),
        "norm_gain": jnp.clip(1.0 + 0.1 * jax.random.normal(key_list[3], (D,), jnp.float32), 0.5, 1.5).astype(jnp.bfloat16),
        "inner_proj": scatter_about(key_list[4], (INNER, 2, D), D ** -0.5, 0.15625, ((0, 2), (2, 4))),
        "state_proj": scatter_about(key_list[5], (D, 2 * STATE), D ** -0.5, 0.15625, ((0, 4),)),
        "step_proj": scatter_about(key_list[6], (HEADS, D), D ** -0.5, 0.15625, ((0, 2), (1, 4))),
        "conv_inner": scatter_about(key_list[7], (CONV, INNER), CONV ** -0.5, 3.0, ((1, 2),)),
        "conv_inner_bias": scatter_about(key_list[8], (INNER,), 0.5, 3.0, ((0, 2),)),
        "conv_state": scatter_about(key_list[9], (CONV, 2 * STATE), CONV ** -0.5, 3.0),
        "conv_state_bias": scatter_about(key_list[10], (2 * STATE,), 0.5, 3.0),
        "step_bias": jnp.clip(-5.0 + 4.0 * jax.random.uniform(key_list[11], (HEADS,), jnp.float32) ** block_levels(key_list[11], (HEADS,), ((0, 2),), -0.2, 0.2), -5.0, -1.0),
        "decay_log": jnp.clip(-5.0 + 7.5 * jax.random.uniform(key_list[12], (HEADS,), jnp.float32) ** block_levels(key_list[12], (HEADS,), ((0, 2),), -0.2, 0.2), -5.0, 2.5),
        "skip_gain": jnp.clip(0.5 + 1.0 * jax.random.uniform(key_list[13], (HEADS,), jnp.float32) ** block_levels(key_list[13], (HEADS,), ((0, 2),), -0.2, 0.2), 0.5, 1.5),
        "gate_gain": jnp.clip(1.0 + 0.1 * jax.random.normal(key_list[14], (INNER,), jnp.float32), 0.5, 1.5).astype(jnp.bfloat16),
        "out_proj": scatter_about(key_list[15], (INNER, D), INNER ** -0.5, 0.109375, ((0, 2), (1, 4))),
    }


EPS = 1e-05
PRECISE = lax.Precision.HIGHEST

@jax.custom_vjp
def low(v):
    return lax.optimization_barrier(v.astype(jnp.bfloat16)).astype(jnp.float32)

@jax.custom_vjp
def low_back(v):
    return v

def low_keep(v):
    return (low(v), None)

def low_pass(kept, grad):
    return (grad,)

def back_keep(v):
    return (v, None)

def back_low(kept, grad):
    return (low(grad),)
low.defvjp(low_keep, low_pass)
low_back.defvjp(back_keep, back_low)

def causal_conv(padded, taps, bias, padded_segment, segment):
    count = segment.shape[0]
    total = bias
    for index in range(taps.shape[0]):
        same = (padded_segment[index:index + count] == segment).astype(jnp.float32)
        total = total + taps[index] * padded[index:index + count] * same[:, None]
    return total

def span_step(state, pieces, rate, skip):
    values, keys_b, keys_c, steps, segment, before = pieces
    size = segment.shape[0]
    logs = steps * rate
    cums = jnp.cumsum(logs, axis=0)
    order = jnp.arange(size)
    same = ((segment[:, None] == segment[None, :]) & (order[:, None] >= order[None, :])).astype(jnp.float32)
    mask = same[:, :, None, None]
    diffs = cums[:, None] - cums[None, :]
    decay = jnp.exp(jnp.where(mask > 0, diffs, 0.0)) * mask
    scores = jnp.einsum('ign,jgn->ijg', keys_c, keys_b, precision=PRECISE)
    mixing = scores[:, :, :, None] * decay * steps[None]
    inner = jnp.einsum('ijgk,jgkp->igkp', mixing, values, precision=PRECISE)
    carry = (segment == before).astype(jnp.float32)
    entry = jnp.exp(cums) * carry[:, None, None]
    outer = jnp.einsum('ign,gkpn->igkp', keys_c, state, precision=PRECISE) * entry[..., None]
    result = inner + outer + skip[None, :, :, None] * values
    last_same = (segment == segment[size - 1]).astype(jnp.float32)
    tail = jnp.exp(cums[size - 1][None] - cums) * last_same[:, None, None] * steps
    weighted = values * tail[..., None]
    fresh = jnp.einsum('jgkp,jgn->gkpn', weighted, keys_b, precision=PRECISE)
    kept = state * (jnp.exp(cums[size - 1]) * carry[size - 1])[:, :, None, None]
    return (fresh + kept, result)

def scan_spans(state, values, keys_b, keys_c, steps, segment, before, rate, skip, size):
    count = values.shape[0] // size
    ends = segment.reshape(count, size)[:, size - 1]
    befores = jnp.concatenate([jnp.reshape(before, (1,)), ends[:count - 1]]).astype(jnp.int32)

    def step(carry_state, pieces):
        return span_step(carry_state, pieces, rate, skip)
    pieces = (values.reshape((count, size) + values.shape[1:]), keys_b.reshape((count, size) + keys_b.shape[1:]), keys_c.reshape((count, size) + keys_c.shape[1:]), steps.reshape((count, size) + steps.shape[1:]), segment.reshape(count, size), befores)
    final, outputs = lax.scan(jax.checkpoint(step), state, pieces)
    return (final, outputs.reshape((count * size,) + outputs.shape[2:]))

def group_forward(group_x, group_lengths, params):
    n_gain, w_inner, w_state, w_step, c_inner, c_inner_b, c_state, c_state_b, s_bias, d_log, s_gain, g_gain, w_out = params
    ends = jnp.cumsum(group_lengths).astype(jnp.int32)
    places = jnp.arange(GROUP_TOK, dtype=jnp.int32)
    segment = lax.optimization_barrier(jnp.sum((places[:, None] >= ends[None, :]).astype(jnp.int32), axis=1)).astype(jnp.int32)
    live = (places < ends[SEQS - 1]).astype(jnp.float32)
    rstd_in = lax.rsqrt(lax.optimization_barrier(jnp.mean(group_x * group_x, axis=-1, keepdims=True)) + EPS)
    normed = low(group_x * rstd_in * n_gain)
    gate_z = low_back(jnp.dot(normed, w_inner[:, 0, :].T, precision=PRECISE))
    x_in = low_back(jnp.dot(normed, w_inner[:, 1, :].T, precision=PRECISE))
    bc_in = jnp.dot(normed, w_state, precision=PRECISE)
    dt_in = low_back(jnp.dot(normed, w_step.T, precision=PRECISE))
    copies = low_back(jnp.broadcast_to(bc_in, (N_COL,) + bc_in.shape))
    padded_segment = jnp.concatenate([jnp.full((CONV - 1,), -1, dtype=jnp.int32), segment])
    x_pad = jnp.concatenate([jnp.zeros((CONV - 1, INNER), jnp.float32), x_in])
    x_conv = jax.nn.silu(causal_conv(x_pad, c_inner, c_inner_b, padded_segment, segment))
    bc_pad = jnp.concatenate([jnp.zeros((N_COL, CONV - 1, 2 * STATE), jnp.float32), copies], axis=1)
    bc_conv = jax.nn.silu(jax.vmap(lambda e: causal_conv(e, c_state, c_state_b, padded_segment, segment))(bc_pad))
    steps = jax.nn.softplus(dt_in + s_bias)
    rate = -jnp.exp(d_log)
    per_group = HEADS // N_COL
    values = x_conv.reshape(GROUP_TOK, N_COL, per_group, HEADDIM)
    keys_b = jnp.transpose(bc_conv[:, :, :STATE], (1, 0, 2))
    keys_c = jnp.transpose(bc_conv[:, :, STATE:], (1, 0, 2))
    start = jnp.zeros((N_COL, per_group, HEADDIM, STATE), jnp.float32)
    _, outputs = scan_spans(start, values, keys_b, keys_c, steps.reshape(GROUP_TOK, N_COL, per_group), segment, jnp.int32(-1), rate.reshape(N_COL, per_group), s_gain.reshape(N_COL, per_group), SPAN)
    y_all = outputs.reshape(GROUP_TOK, INNER)
    gz = y_all * jax.nn.silu(gate_z)
    rstd_gate = lax.rsqrt(lax.optimization_barrier(jnp.mean(gz * gz, axis=-1, keepdims=True)) + EPS)
    gated = low(gz * rstd_gate * g_gain)
    mixed = low_back(jnp.dot(gated, w_out, precision=PRECISE))
    return group_x + live[:, None] * mixed

def reference(hidden_in, grad_out, lengths, norm_gain, inner_proj, state_proj, step_proj, conv_inner, conv_inner_bias, conv_state, conv_state_bias, step_bias, decay_log, skip_gain, gate_gain, out_proj):
    params = tuple((v.astype(jnp.float32) for v in (norm_gain, inner_proj, state_proj, step_proj, conv_inner, conv_inner_bias, conv_state, conv_state_bias, step_bias, decay_log, skip_gain, gate_gain, out_proj)))
    hidden_f = hidden_in.astype(jnp.float32)

    def forward(values, weights):
        groups = values.T.reshape(N_DP, GROUP_TOK, D)

        def one(pair):
            return group_forward(pair[0], pair[1], weights)
        return lax.map(jax.checkpoint(one), (groups, lengths)).reshape(TOKENS, D).T
    result, pull = jax.vjp(forward, hidden_f, params)
    grad_x, grads = pull(grad_out.astype(jnp.float32))
    return (result.astype(jnp.bfloat16), grad_x.astype(jnp.bfloat16), grads[0], grads[1], grads[2], grads[3], grads[4], grads[5], grads[6], grads[7], grads[8], grads[9], grads[10], grads[11], grads[12])
```

```python
import functools

import jax
import jax.numpy as jnp
from jax import lax
from jax.experimental import pallas as pl
from jax.experimental.pallas import tpu as pltpu
from jax.sharding import PartitionSpec as P

HEADDIM = 64
STATE = 128
CONV = 4
Q = 128
EPS = 1e-05
LOG2E = 1.4426950408889634
F32 = jnp.float32
BF16 = jnp.bfloat16
HIGHEST = lax.Precision.HIGHEST
MESH = pl.DeviceIdType.MESH
VMEM_LIMIT = 56 * 1024 * 1024
CUM, STEP, ENTRY, TAIL, DEC, SIG = range(6)


def nn(a, b, precision=None):
    return lax.dot_general(a, b, (((1,), (0,)), ((), ())), precision=precision, preferred_element_type=F32)


def nt(a, b, precision=None):
    return lax.dot_general(a, b, (((1,), (1,)), ((), ())), precision=precision, preferred_element_type=F32)


def tn(a, b, precision=None):
    return lax.dot_general(a, b, (((0,), (0,)), ((), ())), precision=precision, preferred_element_type=F32)


def halves(v):
    high = v.astype(BF16)
    return high, (v - high.astype(F32)).astype(BF16)


def nn3(a, b):
    (ah, al), (bh, bl) = halves(a), halves(b)
    return nn(jnp.concatenate([ah, ah, al], 1), jnp.concatenate([bh, bl, bh], 0))


def nt3(a, b):
    (ah, al), (bh, bl) = halves(a), halves(b)
    return nt(jnp.concatenate([ah, ah, al], 1), jnp.concatenate([bh, bl, bh], 1))


def sigm(v):
    return 0.5 + 0.5 * jnp.tanh(0.5 * v)


def iota(shape, dim):
    return lax.broadcasted_iota(jnp.int32, shape, dim)


def segment_of(place, ends):
    total = (place >= ends[0]).astype(jnp.int32)
    for end in ends[1:]:
        total = total + (place >= end).astype(jnp.int32)
    return jnp.where(place < 0, -1, total)


def chunk_of(c):
    return pl.ds(pl.multiple_of(c * Q, Q), Q)


def shift_masks(place, ends):
    segment = segment_of(place, ends)
    return [(segment_of(place - d, ends) == segment).astype(F32) for d in range(1, CONV)]


def shifted_right(now, earlier, d, lane):
    return pltpu.roll(jnp.where(lane >= Q - d, earlier, now), d, 1)


def shifted_left(now, later, d, lane):
    return pltpu.roll(jnp.where(lane < d, later, now), Q - d, 1)


def conv_tile(now, earlier, taps, masks, lane):
    total = taps(CONV) + taps(CONV - 1) * now
    for d in range(1, CONV):
        total = total + taps(CONV - 1 - d) * (shifted_right(now, earlier, d, lane) * masks[d - 1])
    return total


def spread(rows_ref, out):
    cols = jnp.transpose(rows_ref[...])
    for k in range(out.shape[0]):
        out[k] = jnp.broadcast_to(cols[:, k : k + 1], out.shape[1:])


def thirds(v):
    high, rest = v.astype(BF16), v
    rest = rest - high.astype(F32)
    middle = rest.astype(BF16)
    return jnp.concatenate([high, middle, (rest - middle.astype(F32)).astype(BF16)], -1)


def times_flags(v, flags):
    return nn(thirds(v), jnp.concatenate([flags.astype(BF16)] * 3, 0))


def stacked(v, count):
    return jnp.concatenate([v[:, c * Q : (c + 1) * Q] for c in range(count)], 0)


def scalars(lengths_ref, rows):
    ends = [lengths_ref[0, 0]]
    for k in range(1, lengths_ref.shape[1]):
        ends.append(ends[-1] + lengths_ref[0, k])
    return lax.axis_index("row") * rows, ends


def enter_kernel(nc, hb, place_ref, xin_ref, bcin_ref, dt_ref, heads_ref, taps8_ref, bctaps8_ref, wait_ref,
                 u_ref, ubc_ref, bc_ref, rows_ref, scores_ref, y_ref, fresh_ref, final_ref, pass_ref, hpar_ref, state, taps_ref, bctaps_ref):
    base, ends = scalars(place_ref, nc * Q)
    wide = iota((HEADDIM, Q), 1)
    block = pl.program_id(0)
    spread(taps8_ref, taps_ref)

    @pl.when(block == 0)
    def _():
        spread(bctaps8_ref, bctaps_ref)
        lane = iota((1, Q), 1)
        row, col = iota((Q, Q), 0), iota((Q, Q), 1)

        def body(c, _):
            masks = shift_masks(base + c * Q + lane, ends)
            for part in range(2 * STATE // HEADDIM):
                at = slice(part * HEADDIM, (part + 1) * HEADDIM)
                u = conv_tile(bcin_ref[at, chunk_of(c + 1)], bcin_ref[at, chunk_of(c)], lambda k: bctaps_ref[k, at, :], masks, wide)
                ubc_ref[at, chunk_of(c)] = u
                bc_ref[at, chunk_of(c)] = u * sigm(u)
            start = base + c * Q
            same = (segment_of(start + row, ends) == segment_of(start + col, ends)) & (row >= col)
            score = nn3(jnp.transpose(bc_ref[STATE:, chunk_of(c)]), bc_ref[:STATE, chunk_of(c)])
            scores_ref[c] = jnp.where(same, score, 0.0)
            return 0

        lax.fori_loop(0, nc, body, 0, unroll=2)

        nb = dt_ref.shape[0]
        by_head = jnp.transpose(heads_ref[...])[:, :8]
        for n in range(nb):
            own = by_head[n * hb : (n + 1) * hb]
            hpar_ref[n] = own if hb == 8 else jnp.concatenate([own, jnp.zeros((8 - hb, 8), F32)], 0)
        raw = jnp.concatenate([dt_ref[n] + hpar_ref[n, :, 0:1] for n in range(nb)], 0)
        rate = jnp.concatenate([-jnp.exp(hpar_ref[n, :, 1:2]) for n in range(nb)], 0)
        small = jnp.exp(-jnp.abs(raw))
        steps = jnp.maximum(raw, 0.0) + jnp.log1p(small)
        sig = jnp.where(raw >= 0, 1.0, small) / (1.0 + small)
        each = nb * 8
        cums = times_flags(stacked(steps * rate * LOG2E, nc), row <= col)
        whole_sum = jnp.zeros((each, 1), F32)
        for c in range(nc):
            at = slice(c * Q, (c + 1) * Q)
            start = base + c * Q
            segment = segment_of(start + lane, ends)
            before = segment_of(start - 1, ends)
            after = segment_of(start + Q - 1, ends)
            cum = cums[c * each : (c + 1) * each]
            last = cum[:, Q - 1 : Q]
            entry = jnp.exp2(cum) * (segment == before).astype(F32)
            tail = jnp.exp2(last - cum) * (segment == after).astype(F32)
            decay = jnp.broadcast_to(jnp.exp2(last), (each, Q)) * (before == after).astype(F32)
            for n in range(nb):
                part = slice(n * 8, (n + 1) * 8)
                rows_ref[n, CUM, :, at] = cum[part]
                rows_ref[n, STEP, :, at] = steps[part, at]
                rows_ref[n, ENTRY, :, at] = entry[part]
                rows_ref[n, TAIL, :, at] = tail[part]
                rows_ref[n, DEC, :, at] = decay[part]
                rows_ref[n, SIG, :, at] = sig[part, at]
            whole_sum = whole_sum + last
        end = segment_of(base + nc * Q - 1, ends)
        keep = jnp.broadcast_to(jnp.exp2(whole_sum), (each, Q)) * (segment_of(base - 1, ends) == end).astype(F32)
        for n in range(nb):
            pass_ref[n] = keep[n * 8 : (n + 1) * 8]

    state[...] = jnp.zeros_like(state)

    def chunk(c, _):
        now = chunk_of(c)
        masks = shift_masks(base + c * Q + iota((1, Q), 1), ends)
        cum8 = rows_ref[block, CUM, :, now]
        cols = jnp.transpose(cum8)
        weighted = []
        for h in range(hb):
            at = slice(h * HEADDIM, (h + 1) * HEADDIM)
            hr = slice(h, h + 1)
            u = conv_tile(xin_ref[at, chunk_of(c + 1)], xin_ref[at, now], lambda k: taps_ref[k, at, :], masks, wide)
            u_ref[at, now] = u
            x = u * sigm(u)
            moved = x * rows_ref[block, STEP, hr, now]
            decay = jnp.exp2(jnp.minimum(cols[:, hr] - cum8[hr, :], 0.0))
            mixing = (decay * scores_ref[c]).astype(BF16)
            y_ref[at, now] = nt(moved.astype(BF16), mixing) + hpar_ref[block, hr, 2:3] * x
            weighted.append((moved * rows_ref[block, TAIL, hr, now]).astype(BF16))
        fresh = nt(jnp.concatenate(weighted, 0), bc_ref[:STATE, now].astype(BF16))
        fresh_ref[c] = fresh
        for h in range(hb):
            at = slice(h * HEADDIM, (h + 1) * HEADDIM)
            state[at, :] = state[at, :] * rows_ref[block, DEC, h : h + 1, now] + fresh[at, :]
        return 0

    lax.fori_loop(0, nc, chunk, 0, unroll=2)
    final_ref[...] = state[...].astype(BF16)


def across_kernel(nc, hb, y_ref, fresh_ref, start_ref, bc_ref, rows_ref, z_ref, gg_ref, gate8_ref,
                  y_out, states_ref, stat_ref, state, gate_ref):
    first = pl.program_id(0) == 0

    @pl.when(first)
    def _():
        stat_ref[...] = jnp.zeros_like(stat_ref)

    state[...] = start_ref[...]
    spread(gate8_ref, gate_ref)

    def chunk(c, _):
        states_ref[c] = state[...]
        outer = nn3(state[...], bc_ref[STATE:, chunk_of(c)])
        square = jnp.zeros((8, Q), F32)
        cross = jnp.zeros((8, Q), F32)
        for h in range(hb):
            at = slice(h * HEADDIM, (h + 1) * HEADDIM)
            y = y_ref[at, chunk_of(c)] + outer[at, :] * rows_ref[0, ENTRY, h : h + 1, chunk_of(c)]
            y_out[at, chunk_of(c)] = y
            z = z_ref[at, chunk_of(c)]
            gz = y * (z * sigm(z))
            other = gz * gate_ref[0, at, :] * gg_ref[at, chunk_of(c)]
            squared = gz * gz
            for k in range(HEADDIM // 8):
                square = square + squared[k * 8 : (k + 1) * 8]
                cross = cross + other[k * 8 : (k + 1) * 8]
            state[at, :] = state[at, :] * rows_ref[0, DEC, h : h + 1, chunk_of(c)] + fresh_ref[c, at, :]
        stat_ref[0, :, chunk_of(c)] += square
        stat_ref[1, :, chunk_of(c)] += cross
        return 0

    lax.fori_loop(0, nc, chunk, 0, unroll=2)


def lane_sums(v):
    return nt(jnp.ones((8, 2 * Q), BF16), jnp.concatenate(halves(v), 1))


def gate_kernel(nc, hb, y_ref, z_ref, gg_ref, tok_ref, gate8_ref, bc_ref, rows_ref,
                gated_ref, gz_ref, gy_ref, adj_ref, first_ref, ggate_ref, adjoint, gsum, gate_ref):
    spread(gate8_ref, gate_ref)
    adjoint[...] = jnp.zeros_like(adjoint)
    gsum[...] = jnp.zeros_like(gsum)

    def chunk(k, _):
        c = nc - 1 - k
        rstd = tok_ref[0:1, chunk_of(c)]
        pull = tok_ref[1:2, chunk_of(c)]
        lifted = []
        for h in range(hb):
            at = slice(h * HEADDIM, (h + 1) * HEADDIM)
            y, z, gg = y_ref[at, chunk_of(c)], z_ref[at, chunk_of(c)], gg_ref[at, chunk_of(c)]
            s = sigm(z)
            silu = z * s
            gz = y * silu
            gate = gate_ref[0, at, :]
            gzr = gz * rstd
            gated_ref[at, chunk_of(c)] = (gzr * gate).astype(BF16)
            gsum[at, :] += gzr * gg
            ggz = rstd * (gate * gg) - gz * pull
            gy = ggz * silu
            gz_ref[at, chunk_of(c)] = (ggz * y * (s * (1.0 + z * (1.0 - s)))).astype(BF16)
            gy_ref[at, chunk_of(c)] = gy
            lifted.append(gy * rows_ref[0, ENTRY, h : h + 1, chunk_of(c)])
        adj = nt3(jnp.concatenate(lifted, 0), bc_ref[STATE:, chunk_of(c)])
        adj_ref[c] = adj
        for h in range(hb):
            at = slice(h * HEADDIM, (h + 1) * HEADDIM)
            adjoint[at, :] = adjoint[at, :] * rows_ref[0, DEC, h : h + 1, chunk_of(c)] + adj[at, :]
        return 0

    lax.fori_loop(0, nc, chunk, 0, unroll=2)
    first_ref[...] = adjoint[...].astype(BF16)
    ggate_ref[...] = lane_sums(gsum[...])


def conv_back(gu, later, taps, masks, lane):
    moved = [gu]
    total = taps(CONV - 1) * gu
    for d in range(1, CONV):
        part = shifted_left(gu * masks[d - 1], later * masks[CONV - 1 + d - 1], d, lane)
        moved.append(part)
        total = total + taps(CONV - 1 - d) * part
    return total, moved


def conv_rim(gu, taps, masks, lane, rim_in):
    total = jnp.zeros_like(gu)
    sums = []
    for d in range(1, CONV):
        part = pltpu.roll(jnp.where(lane < d, gu * masks[d - 1], 0.0), Q - d, 1)
        total = total + taps(CONV - 1 - d) * part
        sums.append(rim_in * part)
    return total, sums


def back_masks(base, c, ends):
    lane = iota((1, Q), 1)
    return shift_masks(base + c * Q + lane, ends) + shift_masks(base + (c + 1) * Q + lane, ends)


def total_rows(v):
    return jnp.sum(v, 0, keepdims=True)


def early_sums(early, n_dp, grads, outs, come1, come2, come3, sems):
    half = grads[0].shape[0] // 2
    views = []
    for k, (a, at, width) in enumerate(early["pieces"]):
        columns = pl.ds(at, width)
        views.append((grads[a].at[pl.ds(0, half), columns], grads[a].at[pl.ds(half, half), columns], come1.at[k], come2.at[k], come3.at[k],
                      outs[a].at[:, columns]))
    return RowSums(n_dp, views, sems)


def sent_sums(early, n_dp, grads, outs, *refs):
    sums = early_sums(early, n_dp, grads, outs, *refs)
    groups = early["groups"]
    for t in range(early["steps"]):
        @pl.when(pl.program_id(0) == t)
        def _():
            if t == 0:
                meet(sums.partners())
            for stage, lag in ((sums.along, 2), (sums.across, 1), (sums.pair, 0), (sums.finish, 3)):
                if 0 <= t - lag < len(groups):
                    for p in groups[t - lag]:
                        stage(p)


def end_sums(early, n_dp, grads, outs, *refs):
    sums = early_sums(early, n_dp, grads, outs, *refs)
    groups, steps = early["groups"], early["steps"]

    @pl.when(pl.program_id(0) == steps - 1)
    def _():
        for t in range(steps, len(groups) + 3):
            for stage, lag in ((sums.along, 2), (sums.across, 1), (sums.finish, 3)):
                if 0 <= t - lag < len(groups):
                    for p in groups[t - lag]:
                        stage(p)
        for p in range(len(early["pieces"])):
            sums.first(p).wait_send()
            sums.sent(p)


def back_kernel(nc, hb, heads, early, n_dp, place_ref, u_ref, xin_ref, gy_ref, y_ref, states_ref, adj_ref, start_ref, bc_ref, scores_ref,
                rows_ref, hpar_ref, taps8_ref, *refs):
    refs = list(refs)
    take = lambda count: [refs.pop(0) for _ in range(count)]
    arrays = 2 if early else 0
    grads = take(arrays)
    gx_ref, gxlast_ref, rim_ref, gtaps_ref, gdt_ref, gscores, gbct, hsum_ref = take(8)
    sums_out = take(arrays)
    adjoint, gnext, tapsum, hrow, taps_ref, ends_at = take(6)
    if early:
        sent_sums(early, n_dp, grads, sums_out, *refs)
    spread(taps8_ref, taps_ref)
    base, ends = scalars(place_ref, nc * Q)
    wide = iota((HEADDIM, Q), 1)
    block = pl.program_id(0)

    @pl.when(block == 0)
    def _():
        hsum_ref[...] = jnp.zeros_like(hsum_ref)
        gscores[...] = jnp.zeros_like(gscores)
        gbct[...] = jnp.zeros_like(gbct)
        hrow[...] = jnp.zeros_like(hrow)

    adjoint[...] = start_ref[...]
    gnext[...] = jnp.zeros_like(gnext)
    tapsum[...] = jnp.zeros_like(tapsum)

    def chunk(k, _):
        c = nc - 1 - k
        now = chunk_of(c)
        masks = back_masks(base, c, ends)
        from_later = nn(adjoint[...].astype(BF16), bc_ref[:STATE, now].astype(BF16))
        cum8 = rows_ref[0, CUM, :, now]
        cols = jnp.transpose(cum8)
        lifted, weighted = [], []
        for h in range(hb):
            at = slice(h * HEADDIM, (h + 1) * HEADDIM)
            hr = slice(h, h + 1)
            u = u_ref[at, now]
            gy = gy_ref[at, now]
            s = sigm(u)
            x = u * s
            step = rows_ref[0, STEP, hr, now]
            tail = rows_ref[0, TAIL, hr, now]
            moved = x * step
            moved_low = moved.astype(BF16)
            gy_low = gy.astype(BF16)
            decay = jnp.exp2(jnp.minimum(cols[:, hr] - cum8[hr, :], 0.0))
            gmix = tn(gy_low, moved_low)
            gscores[c] += gmix * decay
            gmoved = nn(gy_low, (decay * scores_ref[c]).astype(BF16))
            later = from_later[at, :] * tail
            lifted.append((gy * rows_ref[0, ENTRY, hr, now]).astype(BF16))
            weighted.append((moved * tail).astype(BF16))
            skip = hpar_ref[0, hr, 2:3]
            taken = gy_low.astype(F32) * (y_ref[at, now] - skip * x) - moved_low.astype(F32) * gmoved
            hrow[0, block, hr, now] = total_rows(taken)
            hrow[1, block, hr, now] = total_rows(moved * later)
            hrow[2, block, hr, now] = total_rows(adjoint[at, :] * states_ref[c, at, :]) * rows_ref[0, DEC, hr, now]
            gmoved = gmoved + later
            hrow[3, block, hr, now] = total_rows(x * gmoved)
            hrow[4, block, hr, now] = total_rows(x * gy)
            gx = gmoved * step + skip * gy
            gu = gx * (s * (1.0 + u * (1.0 - s)))
            gin, shifts = conv_back(gu, gnext[at, :], lambda k: taps_ref[k, at, :], masks, wide)
            gnext[at, :] = gu
            gx_ref[at, now] = gin.astype(BF16)

            ends_at[jnp.minimum(k, 1), at, :] = gin
            xin = xin_ref[at, chunk_of(c + 1)]
            for d in range(CONV):
                tapsum[d, at, :] += xin * shifts[d]
            tapsum[CONV, at, :] += gu
        gbct[STATE:, now] += tn(states_ref[c].astype(BF16), jnp.concatenate(lifted, 0))
        gbct[:STATE, now] += tn(adjoint[...].astype(BF16), jnp.concatenate(weighted, 0))
        for h in range(hb):
            at = slice(h * HEADDIM, (h + 1) * HEADDIM)
            adjoint[at, :] = adjoint[at, :] * rows_ref[0, DEC, h : h + 1, now] + adj_ref[c, at, :]
        return 0

    lax.fori_loop(0, nc, chunk, 0, unroll=2)

    gxlast_ref[...] = ends_at[0]
    masks = back_masks(base, 0, ends)
    for h in range(hb):
        at = slice(h * HEADDIM, (h + 1) * HEADDIM)
        rim, sums = conv_rim(gnext[at, :], lambda k: taps_ref[k, at, :], masks, wide, xin_ref[at, :Q])
        rim_ref[at, :] = rim.astype(BF16)
        for d in range(1, CONV):
            tapsum[d, at, :] += sums[d - 1]
    gtaps_ref[...] = jnp.concatenate([lane_sums(tapsum[d])[0:1] for d in range(CONV + 1)] + [jnp.zeros((7 - CONV, hb * HEADDIM), F32)], 0)

    row, col = iota((Q, Q), 0), iota((Q, Q), 1)
    glogs = (times_flags(stacked(hrow[0, block], nc), row >= col) + times_flags(stacked(hrow[1, block], nc), row < col)
             + times_flags(stacked(hrow[2, block], nc), row >= 0))
    rate = -jnp.exp(hpar_ref[0, :, 1:2])
    total = [jnp.zeros((8, Q), F32) for _ in range(3)]
    for c in range(nc):
        at = slice(c * Q, (c + 1) * Q)
        glog = glogs[c * 8 : (c + 1) * 8] * rate
        gdt = (hrow[3, block, :, at] + glog) * rows_ref[0, SIG, :, at]
        gdt_ref[0, :, at] = gdt
        total[0] = total[0] + gdt
        total[1] = total[1] + glog * rows_ref[0, STEP, :, at]
        total[2] = total[2] + hrow[4, block, :, at]
    sums = times_flags(jnp.concatenate(total, 0), row >= 0)
    first = lax.axis_index("col") * heads + block * hb
    lane = iota((1, Q), 1)
    for k in range(3):
        for h in range(hb):
            hsum_ref[k : k + 1, :] += jnp.where(lane == first + h, sums[k * 8 + h : k * 8 + h + 1, :], 0.0)

    if early:
        end_sums(early, n_dp, grads, sums_out, *refs)


def state_kernel(nc, place_ref, bc_ref, ubc_ref, bcin_ref, bctaps8_ref, gscores_in, gbct_in,
                 gbc_ref, gbclast_ref, bcrim_ref, gbctaps_ref, gnext, tapsum, bctaps_ref, ends_at):
    spread(bctaps8_ref, bctaps_ref)
    base, ends = scalars(place_ref, nc * Q)
    row, col = iota((Q, Q), 0), iota((Q, Q), 1)
    wide = iota((HEADDIM, Q), 1)
    gnext[...] = jnp.zeros_like(gnext)
    tapsum[...] = jnp.zeros_like(tapsum)
    tiles = [slice(k * HEADDIM, (k + 1) * HEADDIM) for k in range(2 * STATE // HEADDIM)]

    def body(k, _):
        c = nc - 1 - k
        now = chunk_of(c)
        start = base + c * Q
        same = (segment_of(start + row, ends) == segment_of(start + col, ends)) & (row >= col)
        gscore = jnp.where(same, gscores_in[c], 0.0)
        masks = back_masks(base, c, ends)
        inter = gbct_in[:, now]
        g_c = inter[STATE:] + nt3(bc_ref[:STATE, now], gscore)
        g_b = inter[:STATE] + nn3(bc_ref[STATE:, now], gscore)
        g_bc = jnp.concatenate([g_b, g_c], 0)
        for at in tiles:
            u = ubc_ref[at, now]
            s = sigm(u)
            gu = g_bc[at] * (s * (1.0 + u * (1.0 - s)))
            gin, shifts = conv_back(gu, gnext[at, :], lambda k: bctaps_ref[k, at, :], masks, wide)
            gnext[at, :] = gu
            gbc_ref[at, now] = gin.astype(BF16)

            ends_at[jnp.minimum(k, 1), at, :] = gin
            xin = bcin_ref[at, chunk_of(c + 1)]
            for d in range(CONV):
                tapsum[d, at, :] += xin * shifts[d]
            tapsum[CONV, at, :] += gu
        return 0

    lax.fori_loop(0, nc, body, 0)
    gbclast_ref[...] = ends_at[0]
    masks = back_masks(base, 0, ends)
    for at in tiles:
        rim, more = conv_rim(gnext[at, :], lambda k: bctaps_ref[k, at, :], masks, wide, bcin_ref[at, :Q])
        bcrim_ref[at, :] = rim.astype(BF16)
        for d in range(1, CONV):
            tapsum[d, at, :] += more[d - 1]
    for d in range(CONV + 1):
        gbctaps_ref[:, d * 2 * STATE : (d + 1) * 2 * STATE] = lane_sums(tapsum[d])


def whole(*shape):
    return pl.BlockSpec(shape, lambda n: (0,) * len(shape))


def params():
    return pltpu.CompilerParams(vmem_limit_bytes=VMEM_LIMIT)


SMEM = pl.BlockSpec(memory_space=pltpu.SMEM)


def shape(dtype, *dims):
    return jax.ShapeDtypeStruct(dims, dtype)


def after(value, *others):
    return lax.optimization_barrier((value,) + others)[0]


def moved(value, axis, steps):
    n = lax.axis_size(axis)
    return lax.ppermute(value, axis, [(k, (k + steps) % n) for k in range(n)])


def swapped(value, axis, bit):
    n = lax.axis_size(axis)
    return lax.ppermute(value, axis, [(k, k ^ bit) for k in range(n)])


def col_sum(value):
    if lax.axis_size("col") == 2:
        return value + swapped(value, "col", 1)
    return lax.psum(value, "col")


def from_before(value, steps):
    n = lax.axis_size("row")
    pairs = [(k, k + steps) for k in range(max(0, -steps), min(n, n - steps))]
    return lax.ppermute(value, "row", pairs)


def chained(state, keep, hb, direction):
    nb, inner = keep.shape[0], state.shape[0]
    flat = keep.reshape(nb * 8, Q)
    high, low = halves(flat)
    packed = jnp.concatenate([state, high, low], axis=0)
    total, decay = None, None
    for k in range(1, lax.axis_size("row")):
        part = from_before(packed, direction * k)
        passing = part[inner : inner + nb * 8].astype(F32) + part[inner + nb * 8 :].astype(F32)
        passing = jnp.repeat(passing.reshape(nb, 8, Q)[:, :hb].reshape(nb * hb, Q), HEADDIM, axis=0)
        part = part[:inner].astype(F32)
        total = part if total is None else total + decay * part
        decay = passing if decay is None else decay * passing
    return total


def sum_stages(n_row):
    order, bits = [0], []
    bit = n_row // 2
    while bit:
        order = [k + bit for k in order] + order
        bits.insert(0, bit)
        bit //= 2
    return order, bits


def far(source, target, sems, k, axis, place):
    return pltpu.make_async_remote_copy(
        src_ref=source, dst_ref=target, send_sem=sems.at[0, k], recv_sem=sems.at[1, k],
        device_id={axis: place}, device_id_type=MESH)


def meet(partners):
    barrier = pltpu.get_barrier_semaphore()
    for axis, place in partners:
        pl.semaphore_signal(barrier, inc=1, device_id={axis: place}, device_id_type=MESH)
    pl.semaphore_wait(barrier, len(partners))


class RowSums:
    def __init__(self, n_dp, pieces, sems):
        self.row, dp = lax.axis_index("row"), lax.axis_index("dp")
        self.n_dp, self.pieces, self.sems = n_dp, pieces, sems
        self.dps = [lax.rem(dp + k, n_dp) for k in range(n_dp)]
        self.quarter = pieces[0][3].shape[0]
        self.block = self.quarter // n_dp
        self.per = n_dp + 1

    def partners(self):
        return [("row", self.row ^ 1), ("row", self.row ^ 2)] + [("dp", d) for d in self.dps[1:]]

    def first(self, p):
        send, _, come1, _, _, _ = self.pieces[p]
        return far(send, come1, self.sems, p * self.per, "row", self.row ^ 1)

    def second(self, p):
        _, _, come1, come2, _, _ = self.pieces[p]
        return far(come1.at[pl.ds(0, self.quarter)], come2, self.sems, p * self.per + 1, "row", self.row ^ 2)

    def third(self, p):
        _, _, _, come2, come3, _ = self.pieces[p]
        block = self.block
        return [far(come2.at[pl.ds(k * block, block)], come3.at[pl.ds((k - 1) * block, block)], self.sems, p * self.per + 1 + k, "dp", self.dps[k])
                for k in range(self.n_dp - 1, 0, -1)]

    def pair(self, p):
        self.first(p).start()

    def across(self, p):
        _, kept, come1, _, _, _ = self.pieces[p]
        self.first(p).wait_recv()
        add_rows(come1, 0, kept, 0, self.quarter)
        self.second(p).start()
        add_rows(come1, self.quarter, kept, self.quarter, self.quarter)

    def along(self, p):
        _, _, come1, come2, _, _ = self.pieces[p]
        self.second(p).wait_recv()
        add_rows(come2, 0, come1, self.quarter, self.quarter)
        for copy in self.third(p):
            copy.start()

    def finish(self, p):
        _, _, _, come2, come3, out = self.pieces[p]
        for copy in self.third(p):
            copy.wait_recv()

        def body(i, _):
            at = i * 32
            total = come2[pl.ds(at, 32), :].astype(F32)
            for k in range(1, self.n_dp):
                total = total + come3[pl.ds((k - 1) * self.block + at, 32), :].astype(F32)
            out[pl.ds(at, 32), :] = total
            return 0

        lax.fori_loop(0, self.block // 32, body, 0, unroll=True)

    def sent(self, p):
        self.second(p).wait_send()
        for copy in self.third(p):
            copy.wait_send()


def add_rows(out, out_at, other, other_at, count):
    def body(i, _):
        at = i * 32
        out[pl.ds(out_at + at, 32), :] = (
            out[pl.ds(out_at + at, 32), :].astype(F32) + other[pl.ds(other_at + at, 32), :].astype(F32)).astype(out.dtype)
        return 0

    lax.fori_loop(0, count // 32, body, 0, unroll=4)


def close_kernel(n_row, n_dp, n_col, sources, pieces, has_gn, fused, *refs):
    refs = list(refs)
    take = lambda count: [refs.pop(0) for _ in range(count)]
    lefts = take(1 + max(left for left, _, _ in sources))
    if fused:
        nc, hb, n_late = fused
        lengths_ref, = take(1)
        rows_given = take(3)
    else:
        gbd, = take(1)
        rows_given = take(4)
    if has_gn:
        gain8, rstd8 = take(2)
    else:
        stat, gain_row = take(2)
    later_given = take(n_late if fused else 2 + len(sources) - 3 + (5 if has_gn else 0))
    outs = take(len(sources))
    state_out, small_out, stat_out = take(3)
    if has_gn:
        grad_in, = take(1)
    come1, come2, come3 = take(len(sources)), take(len(sources)), take(len(sources))
    grad_slots, = take(1)
    later_held = take(len(later_given))
    small_a, small_b, small_c, state_a, state_b = take(5)
    sems_grad, sems_small, sems_state, sems_other, sems_local, small = take(6)
    if has_gn:
        gn_sum, gn, gn_come, gain, gsum, stat = take(6)
    if fused:
        gbd, gbctaps, gbclast, rim_bc, rims, gnext, tapsum, bctaps, ends_at, sems_rim = take(10)
        rows_given = rows_given[:2] + [gbctaps] + rows_given[2:]

    loads = [pltpu.make_async_copy(source, held, sems_local.at[k]) for k, (source, held) in enumerate(zip(later_given, later_held))]
    for load in loads:
        load.start()
    loaded = set()

    def held(k):
        if k not in loaded:
            loads[k].wait()
            loaded.add(k)
        return later_held[k]

    row, dp, col = lax.axis_index("row"), lax.axis_index("dp"), lax.axis_index("col")
    dps = [lax.rem(dp + k, n_dp) for k in range(n_dp)]
    cols = [lax.rem(col + k, n_col) for k in range(n_col)]
    rows = lefts[0].shape[0]
    half, quarter = rows // 2, rows // 4
    block = quarter // n_dp
    count = len(pieces)
    slots = grad_slots.shape[0]
    views = []
    for p, (a, at, width) in enumerate(pieces):
        columns, mine = pl.ds(at, width), grad_slots.at[p % slots, :, pl.ds(0, width)]
        views.append((mine.at[pl.ds(0, half)], mine.at[pl.ds(half, half)], come1[a].at[:, columns], come2[a].at[:, columns],
                      come3[a].at[:, columns], outs[a].at[:, columns]))
    sums = RowSums(n_dp, views, sems_grad)
    ahead, behind = lax.rem(row + 1, n_row), lax.rem(row + n_row - 1, n_row)
    meet(sums.partners() + [("col", c) for c in cols[1:]] + ([("row", ahead), ("row", behind)] if fused else []))
    started = []

    def start(copy):
        copy.start()
        started.append(copy)
        return copy

    def make(p):
        a, at, width = pieces[p]
        left, first_row, right = sources[a]
        if p >= slots:
            sums.first(p - slots).wait_send()
        right = gbd if right is None else held(right)
        value = right[first_row + at : min(first_row + at + width, right.shape[0]), :]
        if value.shape[0] < width:
            value = jnp.concatenate([value, jnp.zeros((width - value.shape[0], value.shape[1]), BF16)], 0)
        for part in range(2):
            rows_here = slice(part * half, (part + 1) * half)
            grad_slots[p % slots, rows_here, :width] = nt(lefts[left][rows_here, :], value).astype(BF16)
            if part == 0:
                sums.pair(p)

    group = lambda r: pl.ds(pl.multiple_of(r * (n_dp * block), 16), n_dp * block)
    here = pl.ds(pl.multiple_of((row * n_dp + dp) * block, 16), block)
    n0 = n_col - 1
    n1 = n0 + n_dp - 1
    later = {"others": []}

    def send_rim():
        later["rim"] = start(far(held(7), rims.at[pl.ds(0, held(7).shape[0])], sems_rim, 0, "row", behind))

    def add_rim(target, last, at, count):
        tokens = target.shape[1]
        come = jnp.where(row < n_row - 1, rims[at : at + count, :].astype(F32), 0.0)
        target[:count, tokens - Q :] = (last[...] + come).astype(BF16)

    def take_rim():
        later["rim"].wait_recv()
        add_rim(held(0), held(8), 0, held(8).shape[0])

    def state_back():
        bc, ubc, bcin, bctaps8, gscores, gbct, gdt = (held(k) for k in range(9, 16))
        state_kernel(nc, lengths_ref, bc, ubc, bcin, bctaps8, gscores, gbct, gbd, gbclast, rim_bc, gbctaps, gnext, tapsum, bctaps, ends_at)
        channels = held(8).shape[0]
        later["rim_bc"] = start(far(rim_bc, rims.at[pl.ds(channels, 2 * STATE)], sems_rim, 1, "row", behind))
        steps = [gdt[n, :hb, :] for n in range(gdt.shape[0])]
        rest = gbd.shape[0] - 2 * STATE - hb * gdt.shape[0]
        gbd[2 * STATE :, :] = jnp.concatenate(steps + [jnp.zeros((rest, gdt.shape[2]), F32)], 0).astype(BF16)

    def take_rim_bc():
        later["rim_bc"].wait_recv()
        add_rim(gbd, gbclast, held(8).shape[0], 2 * STATE)

    def product(place, unit):
        gx, gz, x4, z4, bd4 = (held(k) for k in range(5))
        each = x4.shape[2]
        index = place * (n_row // 2) + unit
        gn_sum[unit * each : (unit + 1) * each, :] = tn(x4[index], gx[...]) + tn(z4[index], gz[...]) + tn(bd4[index], gbd[: bd4.shape[1], :])

    def prepare(k, place):
        hx = held(5)
        width = gn_sum.shape[0]
        rstd = rstd8[0:1, :]

        def body(i, total):
            at = pl.ds(i * 16, 16)
            there = pl.ds(pl.multiple_of(place * width + i * 16, 16), 16)
            pushed = gn_sum[at, :]
            if k == 0:
                gn[at, :] = pushed.astype(BF16)
            product = hx[there, Q:].astype(F32) * pushed
            scaled = product * rstd
            summed = scaled[:, :128]
            for tile in range(1, scaled.shape[1] // 128):
                summed = summed + scaled[:, tile * 128 : (tile + 1) * 128]
            gsum[at, :] = summed
            product = product * gain[0, there, 0:1]
            return total + product[:8] + product[8:]

        total = lax.fori_loop(0, width // 16, body, jnp.zeros((8, rstd.shape[1]), F32), unroll=2)
        total = rstd * total_rows(total)
        stat[...] = total if k == 0 else stat[...] + total
        small[6:7, pl.ds(pl.multiple_of(place * width, 128), width)] = lane_sums(gsum[...])[0:1]

    def begin_rows():
        channels = rows_given[0].shape[1]
        small[0 : CONV + 1, :channels] = rows_given[0][0 : CONV + 1, :]
        small[CONV + 1 : CONV + 2, :channels] = rows_given[1][0:1, :]
        small[7:8, : rows_given[2].shape[1]] = rows_given[2][0:1, :]
        for k in range(3):
            small[8:9, k * 128 : (k + 1) * 128] = rows_given[3][k : k + 1, :]

    def begin():
        small[...] = jnp.zeros_like(small)
        if has_gn:
            spread(gain8, gain)
        else:
            small[6:7, : gain_row.shape[1]] = gain_row[...]
        if not fused:
            begin_rows()

    def send_norm():
        if fused:
            begin()
        prepare(0, 1 - col)
        later["others"].append(start(far(gn, gn_come, sems_other, 0, "col", cols[1])))

    def send_small():
        if fused:
            begin_rows()
        if has_gn:
            prepare(1, col)
        later["small1"] = start(far(small, small_a.at[0], sems_small, 0, "row", row ^ 1))
        later["others"] += [start(far(stat, stat_out.at[col], sems_other, k, "col", cols[k])) for k in range(1, n_col)]
        stat_out[col] = stat[...]

    def small_pair():
        later["small1"].wait_recv()
        small_a[1] = small[...] + small_a[0]
        later["small2"] = start(far(small_a.at[1], small_b.at[0], sems_small, 1, "row", row ^ 2))

    def small_dp():
        later["small2"].wait_recv()
        small_b[1] = small_a[1] + small_b[0]
        later["small3"] = [start(far(small_b.at[1], small_c.at[k], sems_small, 1 + k, "dp", dps[k])) for k in range(1, n_dp)]

    def small_col():
        for copy in later["small3"]:
            copy.wait_recv()
        total = small_b[1]
        for k in range(1, n_dp):
            total = total + small_c[k]
        small_out[col] = total
        later["small4"] = [start(far(small_out.at[col], small_out.at[col], sems_small, n_dp + k, "col", cols[k])) for k in range(1, n_col)]

    def state_col():
        state_a[0] = outs[0][:, : state_a.shape[2]]
        later["state1"] = [start(far(state_a.at[0], state_a.at[k], sems_state, k - 1, "col", cols[k])) for k in range(1, n_col)]

    def state_dp():
        for copy in later["state1"]:
            copy.wait_recv()
        total = state_a[0]
        for k in range(1, n_col):
            total = total + state_a[k]
        state_b[...] = total.astype(state_b.dtype)
        state_out[here, :] = state_b[...]
        later["state2"] = [start(far(state_b, state_out.at[here], sems_state, n0 + k - 1, "dp", dps[k])) for k in range(1, n_dp)]

    def state_row():
        for copy in later["state2"]:
            copy.wait_recv()
        later["state3"] = start(far(state_out.at[group(row)], state_out.at[group(row)], sems_state, n1, "row", row ^ 2))

    def state_pair():
        later["state3"].wait_recv()
        later["state4"] = [start(far(state_out.at[group(r)], state_out.at[group(r)], sems_state, n1 + 1 + k, "row", row ^ 1))
                           for k, r in enumerate((row, row ^ 2))]

    def norm_back():
        for copy in later["others"]:
            copy.wait_recv()
        if not has_gn:
            return
        hx, grad_out = held(5), held(6)
        rstd = rstd8[0:1, :]
        total = stat_out[0]
        for k in range(1, n_col):
            total = total + stat_out[k]
        own = gn_sum.shape[0]
        width = n_col * own
        pull = (rstd * rstd) * (total / width)

        def body(i, _):
            at = pl.ds(i * 16, 16)
            there = pl.ds(pl.multiple_of(col * own + i * 16, 16), 16)
            pushed = gn_sum[at, :] + gn_come[at, :].astype(F32)
            grad_in[at, :] = (grad_out[at, :].astype(F32) + (rstd * gain[0, there, 0:1]) * pushed
                              - hx[there, Q:].astype(F32) * pull).astype(BF16)
            return 0

        lax.fori_loop(0, own // 16, body, 0, unroll=2)

    ahead_of = {}
    if fused:
        ahead_of = {4: [take_rim_bc], 6: [take_rim]}
        extra = {0: [send_rim], 1: [state_back], 7: [lambda: product(1 - col, 0)], 8: [lambda: product(1 - col, 1), send_norm],
                 9: [lambda: product(col, 0), state_col], 10: [lambda: product(col, 1), send_small], 11: [state_dp, small_pair],
                 12: [state_row, small_dp], 13: [state_pair, small_col], 15: [norm_back]}
    elif has_gn:
        extra = {1: [lambda: product(1 - col, 0)], 2: [lambda: product(1 - col, 1), send_norm], 4: [lambda: product(col, 0)],
                 6: [lambda: product(col, 1), send_small], 7: [state_col], 8: [small_pair], 9: [state_dp], 10: [small_dp], 11: [state_row],
                 12: [small_col], 13: [state_pair, norm_back]}
    else:
        extra = {1: [send_small], 3: [small_pair], 4: [small_dp], 5: [small_col], 7: [state_col], 8: [state_dp], 9: [state_row],
                 10: [state_pair], 11: [norm_back]}
    for step in extra.get(0, ()):
        step()
    make(0)
    if not fused:
        begin()
    for t in range(1, max(count + 6, 16)):
        if 0 <= t - 1 < count:
            sums.across(t - 1)
        for step in ahead_of.get(t, ()):
            step()
        if t < count:
            make(t)
        if 0 <= t - 3 < count:
            sums.along(t - 3)
        if 0 <= t - 5 < count:
            sums.finish(t - 5)
        for step in extra.get(t, ()):
            step()
    for copy in later["small4"] + later["state4"]:
        copy.wait_recv()
    for k in range(len(loads)):
        held(k)
    for copy in started:
        copy.wait_send()
    for p in range(count):
        if p + slots >= count:
            sums.first(p).wait_send()
        sums.sent(p)


def close(sources, pieces, lefts, gbd, given, gn, plain, later, fused=()):
    n_row, n_dp, n_col = (lax.axis_size(axis) for axis in ("row", "dp", "col"))
    assert n_row == 4
    rows, tokens = lefts[0].shape
    widths = [max(at + width for a, at, width in pieces if a == k) for k in range(len(sources))]
    half, quarter, block = rows // 2, rows // 4, rows // 4 // n_dp
    vmem, anywhere = pl.BlockSpec(memory_space=pltpu.VMEM), pl.BlockSpec(memory_space=pl.ANY)
    has_gn = gn is not None
    here = rows // n_col
    given = list(given)
    small = (16, max(rows, given[1 if fused else 0].shape[1]))
    channels = given[1].shape[1]
    extra = list(gn) if has_gn else list(plain)
    out = pl.pallas_call(
        functools.partial(close_kernel, n_row, n_dp, n_col, sources, pieces, has_gn, fused),
        in_specs=[vmem] * len(lefts) + ([SMEM] + [vmem] * 3 if fused else [vmem] * 5) + [vmem] * len(extra) + [anywhere] * len(later),
        out_specs=[vmem] * (len(sources) + 3 + has_gn),
        out_shape=[shape(F32, block, width) for width in widths]
        + [shape(BF16, rows, 2 * STATE), shape(F32, n_col, *small), shape(F32, n_col, 1, tokens)] + [shape(BF16, here, tokens)] * has_gn,
        scratch_shapes=[pltpu.VMEM((half, width), BF16) for width in widths] + [pltpu.VMEM((quarter, width), BF16) for width in widths]
        + [pltpu.VMEM(((n_dp - 1) * block, width), BF16) for width in widths]
        + [pltpu.VMEM((min(3 if fused else 4, len(pieces)), rows, max(width for _, _, width in pieces)), BF16)]
        + [pltpu.VMEM(value.shape, value.dtype) for value in later]
        + [pltpu.VMEM((2,) + small, F32), pltpu.VMEM((2,) + small, F32), pltpu.VMEM((n_dp,) + small, F32),
           pltpu.VMEM((n_col, block, 2 * STATE), F32), pltpu.VMEM((block, 2 * STATE), BF16),
           pltpu.SemaphoreType.DMA((2, len(pieces) * (n_dp + 1))), pltpu.SemaphoreType.DMA((2, n_dp + n_col)),
           pltpu.SemaphoreType.DMA((2, n_col + n_dp + 2)), pltpu.SemaphoreType.DMA((2, n_col)),
           pltpu.SemaphoreType.DMA((len(later),)), pltpu.VMEM(small, F32)]
        + ([pltpu.VMEM((here, tokens), F32), pltpu.VMEM((here, tokens), BF16), pltpu.VMEM((here, tokens), BF16), pltpu.VMEM((1, rows, 128), F32),
            pltpu.VMEM((here, 128), F32), pltpu.VMEM((1, tokens), F32)] if has_gn else [])
        + ([pltpu.VMEM((widths[0], tokens), BF16), pltpu.VMEM((8, (CONV + 1) * 2 * STATE), F32), pltpu.VMEM((2 * STATE, Q), F32),
            pltpu.VMEM((2 * STATE, Q), BF16), pltpu.VMEM((channels + 2 * STATE, Q), BF16), pltpu.VMEM((2 * STATE, Q), F32),
            pltpu.VMEM((CONV + 1, 2 * STATE, Q), F32), pltpu.VMEM((CONV + 1, 2 * STATE, Q), F32), pltpu.VMEM((2, 2 * STATE, Q), F32),
            pltpu.SemaphoreType.DMA((2, 2))] if fused else []),
        compiler_params=pltpu.CompilerParams(vmem_limit_bytes=60 * 1024 * 1024, collective_id=1, has_side_effects=True),
        cost_estimate=pl.CostEstimate(flops=10**6, bytes_accessed=10**8, transcendentals=0),
        name="close",
    )(*lefts, *([] if fused else [gbd]), *given, *extra, *later)
    count = len(sources)
    return out[:count], out[count], out[count + 1], out[count + 2], out[count + 3] if has_gn else None


def last_kernel(n_row, n_dp, n_col, heads, n_z, bd, x, state, small, *refs):
    refs = list(refs)
    take = lambda count: [refs.pop(0) for _ in range(count)]
    z_parts = take(n_z)
    norm_gain, inner, state_out, step, taps, bias, bc_taps, bc_bias, step_bias, decay, skip, gate = refs
    block = x.shape[0]
    at, channels = 0, inner.shape[2]
    for part in z_parts:
        count = min(part.shape[1], channels - at)
        inner[0, :, at : at + count] = part[:, :count]
        at += count
    inner[1] = x[:, :channels]
    for r in range(n_row):
        for d in range(n_dp):
            state_out[(d * n_row + r) * block : (d * n_row + r + 1) * block, :] = state[
                (r * n_dp + d) * block : (r * n_dp + d + 1) * block, :].astype(F32)
    step[...] = jnp.transpose(bd[:, 2 * STATE :])[:heads]
    by_col = lambda k: jnp.concatenate([small[c, k : k + 1, :channels] for c in range(n_col)], 1)
    for k in range(CONV):
        taps[k : k + 1, :] = by_col(CONV - 1 - k)
    bias[...] = by_col(CONV)
    gate[...] = by_col(CONV + 1)
    over = lambda k, at, count: sum(small[c, k : k + 1, at : at + count] for c in range(n_col))
    norm_gain[...] = over(6, 0, norm_gain.shape[1])
    for k in range(CONV):
        bc_taps[k : k + 1, :] = over(7, (CONV - 1 - k) * 2 * STATE, 2 * STATE)
    bc_bias[...] = over(7, CONV * 2 * STATE, 2 * STATE)
    for k, target in enumerate((step_bias, decay, skip)):
        target[...] = over(8, k * 128, 128)[:, : target.shape[1]]


def last(bd, x, state, small, z_parts, heads, channels):
    n_row, n_dp, n_col = (lax.axis_size(axis) for axis in ("row", "dp", "col"))
    block = x.shape[0]
    width = state.shape[0]
    row = lambda count: shape(F32, 1, count)
    return pl.pallas_call(
        functools.partial(last_kernel, n_row, n_dp, n_col, heads, len(z_parts)),
        out_shape=[row(width), shape(F32, 2, block, channels), shape(F32, width, 2 * STATE), shape(F32, heads, block),
                   shape(F32, CONV, n_col * channels), row(n_col * channels), shape(F32, CONV, 2 * STATE), row(2 * STATE),
                   row(n_col * heads), row(n_col * heads), row(n_col * heads), row(n_col * channels)],
        compiler_params=params(),
        cost_estimate=pl.CostEstimate(flops=10**6, bytes_accessed=10**7, transcendentals=0),
        name="last",
    )(bd, x, state, small, *z_parts)


def open_kernel(n_row, n_col, parts, hidden, inner, state_w, step_w, hx, x4, z_w, bd4, sems):
    row, col = lax.axis_index("row"), lax.axis_index("col")
    cols = [lax.rem(col + k, n_col) for k in range(n_col)]
    ahead, behind = lax.rem(row + 1, n_row), lax.rem(row + n_row - 1, n_row)
    partners = [("row", row ^ 1), ("row", row ^ 2), ("row", ahead), ("row", behind)] + [("col", c) for c in cols[1:]]
    meet(partners)
    width, tokens = hidden.shape
    each = inner.shape[0] // parts
    heads = step_w.shape[0]
    mine = pl.ds(pl.multiple_of(col * width, 16), width)
    counter = [0]
    started = []

    def start(source, target, axis, place):
        copy = far(source, target, sems, counter[0], axis, place)
        counter[0] += 1
        copy.start()
        started.append(copy)
        return copy

    rim = start(hidden.at[:, pl.ds(tokens - Q, Q)], hx.at[mine, pl.ds(0, Q)], "row", ahead)
    wide = [start(hidden, hx.at[mine, pl.ds(Q, tokens)], "col", cols[k]) for k in range(1, n_col)]
    part = lambda p: pl.ds(p * each, each)
    send = lambda p: start(x4.at[row, part(p)], x4.at[row, part(p)], "row", row ^ 2)

    def split(p):
        def body(i, _):
            at = pl.ds(p * each + i * 16, 16)
            x4[row, at, :] = inner[at, 1, :]
            z_w[at, :] = inner[at, 0, :]
            return 0

        lax.fori_loop(0, each // 16, body, 0, unroll=2)

    split(0)
    over = [send(0)]
    bd4[row, : 2 * STATE, :] = jnp.transpose(state_w[...].astype(F32)).astype(BF16)
    rest = bd4.shape[1] - 2 * STATE - heads
    bd4[row, 2 * STATE :, :] = jnp.concatenate([step_w[...], jnp.zeros((rest, step_w.shape[1]), BF16)], 0)
    bd_over = start(bd4.at[row], bd4.at[row], "row", row ^ 2)
    near = [start(bd4.at[row], bd4.at[row], "row", row ^ 1)]
    for p in range(1, parts):
        split(p)
        if p == 1:
            over.append(send(1))
    near.append(start(x4.at[row], x4.at[row], "row", row ^ 1))

    def keep_hidden(i, _):
        hx[pl.ds(pl.multiple_of(col * width + i * 16, 16), 16), pl.ds(Q, tokens)] = hidden[pl.ds(i * 16, 16), :]
        return 0

    lax.fori_loop(0, width // 16, keep_hidden, 0)
    rim.wait_recv()
    wide += [start(hx.at[mine, pl.ds(0, Q)], hx.at[mine, pl.ds(0, Q)], "col", cols[k]) for k in range(1, n_col)]
    bd_over.wait_recv()
    near.append(start(bd4.at[row ^ 2], bd4.at[row ^ 2], "row", row ^ 1))
    waited = []
    for p in range(parts):
        over[p].wait_recv()
        near.append(start(x4.at[row ^ 2, part(p)], x4.at[row ^ 2, part(p)], "row", row ^ 1))
        if p + 2 < parts:
            over[p].wait_send()
            waited.append(id(over[p]))
            over.append(send(p + 2))
    for copy in wide + near:
        copy.wait_recv()
    for copy in started:
        if id(copy) not in waited:
            copy.wait_send()


def open_up(hidden, inner, state_w, step_w):
    n_row, n_col = lax.axis_size("row"), lax.axis_size("col")
    assert n_row == 4
    channels, _, block = inner.shape
    heads = step_w.shape[0]
    parts = 4 if channels % 64 == 0 else 1
    vmem = pl.BlockSpec(memory_space=pltpu.VMEM)
    return pl.pallas_call(
        functools.partial(open_kernel, n_row, n_col, parts),
        in_specs=[vmem] * 4,
        out_specs=[vmem] * 4,
        out_shape=[shape(BF16, hidden.shape[0] * n_col, Q + hidden.shape[1]), shape(BF16, n_row, channels, block), shape(BF16, channels, block),
                   shape(BF16, n_row, 2 * STATE + heads + -heads % 32, block)],
        scratch_shapes=[pltpu.SemaphoreType.DMA((2, 5 + 2 * parts + 2 * (n_col - 1)))],
        compiler_params=pltpu.CompilerParams(vmem_limit_bytes=VMEM_LIMIT, collective_id=2, has_side_effects=True),
        cost_estimate=pl.CostEstimate(flops=0, bytes_accessed=10**8, transcendentals=0),
        name="open",
    )(hidden, inner, state_w, step_w)


def joined(w4_ref):
    return jnp.concatenate([w4_ref[j] for j in range(w4_ref.shape[0])], 1)


def by_distance(n_row, n_dp):
    row, dp = lax.axis_index("row"), lax.axis_index("dp")
    return [lax.rem(dp + k, n_dp) * n_row + (row ^ place) for place in sum_stages(n_row)[0] for k in range(n_dp)]


def put_by_distance(n_row, n_dp, source, target, skip):
    each = target.shape[0] // (n_row * n_dp)
    for k, place in enumerate(by_distance(n_row, n_dp)):
        target[k * each : (k + 1) * each, :] = source[pl.ds(pl.multiple_of(place * each, 32), each), skip:]


def project_kernel(n_row, n_dp, hb, lengths_ref, hx_ref, gain8_ref, x4_ref, bd4_ref, normed_ref, by_ref, rstd_ref, live_ref, xin_ref, bd_ref, dt_ref, gain_ref):
    @pl.when(pl.program_id(0) == 0)
    def _():
        spread(gain8_ref, gain_ref)
        width, count = hx_ref.shape

        def square(i, total):
            v = hx_ref[pl.ds(i * 16, 16), :].astype(F32)
            v = v * v
            return total + v[:8] + v[8:]

        total = lax.fori_loop(0, width // 16, square, jnp.zeros((8, count), F32), unroll=4)
        rstd = lax.rsqrt(jnp.sum(total, 0, keepdims=True) / width + EPS)
        rstd_ref[...] = jnp.broadcast_to(rstd[:, Q:], rstd_ref.shape)
        base, ends = scalars(lengths_ref, count - Q)
        live_ref[...] = (base + iota(live_ref.shape, 1) < ends[-1]).astype(F32)

        def norm(i, _):
            at = pl.ds(i * 16, 16)
            normed_ref[at, :] = (hx_ref[at, :].astype(F32) * rstd * gain_ref[0, at, 0:1]).astype(BF16)
            return 0

        lax.fori_loop(0, width // 16, norm, 0, unroll=4)
        put_by_distance(n_row, n_dp, normed_ref, by_ref, Q)
        bd = nn(joined(bd4_ref), normed_ref[...])
        bd_ref[...] = bd[: 2 * STATE]
        dt_ref[...] = jnp.zeros_like(dt_ref)
        for n in range(dt_ref.shape[0]):
            dt_ref[n, :hb, :] = bd[2 * STATE + n * hb : 2 * STATE + (n + 1) * hb, Q:]

    xin_ref[...] = nn(joined(x4_ref), normed_ref[...])


def second_kernel(n_row, n_dp, steps, hb, given, *refs):
    refs = list(refs)
    take = lambda count: [refs.pop(0) for _ in range(count)]
    far_refs = [take(2), take(2)]
    near_refs = [take(2), take(2)]
    normed, = take(1)
    grads = take(2 if given else 1)
    live, final, keep = take(3)
    z4, z, out4, gg, state_in, grad_by = take(6)
    whole_grad, come, came, kept, sems, sems_state = take(6)
    row, col = lax.axis_index("row"), lax.axis_index("col")
    n = pl.program_id(0)
    each = z4.shape[1]

    def piece(side, which, s):
        rows = pl.ds(s * each, each)
        return far(far_refs[side][which].at[rows], come.at[side, which, rows], sems, (side * 2 + which) * steps + s, "row", row ^ 1)

    def pieces(at):
        return [piece(at // steps, which, at % steps) for which in range(2)]

    def states():
        copies = []
        for k in range(1, n_row):
            there = lax.rem(row + k, n_row)
            copies.append(far(final, came.at[k - 1], sems_state, 2 * k - 2, "row", there))
            copies.append(far(keep, kept.at[k - 1], sems_state, 2 * k - 1, "row", there))
        return copies

    @pl.when(n == 0)
    def _():
        meet([("row", lax.rem(row + k, n_row)) for k in range(1, n_row)])
        for copy in states() + pieces(0) + pieces(1):
            copy.start()

    @pl.when(n == 0)
    def _():
        width = grads[0].shape[0]
        for place, source in zip((col, 1 - col) if given else (0,), grads):
            def body(i, _):
                at = pl.ds(pl.multiple_of(place * width + i * 16, 16), 16)
                whole_grad[at, :] = (source[pl.ds(i * 16, 16), :].astype(F32) * live[0:1, :]).astype(BF16)
                return 0

            lax.fori_loop(0, width // 16, body, 0, unroll=4)
        put_by_distance(n_row, n_dp, whole_grad, grad_by, 0)

    for at in range(2 * steps):
        @pl.when(n == at)
        def _():
            side = at // steps
            if at + 2 < 2 * steps:
                for copy in pieces(at + 2):
                    copy.start()
            for copy in pieces(at):
                copy.wait_recv()
            rows = slice(at % steps * each, (at % steps + 1) * each)
            w4, out = ((z4, z), (out4, gg))[side]
            w4[row] = near_refs[side][0][...]
            w4[row ^ 2] = near_refs[side][1][...]
            w4[row ^ 1] = come[side, 0, rows, :]
            w4[row ^ 3] = come[side, 1, rows, :]
            value = normed[:, Q:] if side == 0 else whole_grad[...]
            out[...] = nn(joined(w4), value)

    @pl.when(n == 2 * steps - 1)
    def _():
        for copy in states():
            copy.wait_recv()
        for head in range(final.shape[0] // HEADDIM):
            at = slice(head * HEADDIM, (head + 1) * HEADDIM)
            total, decay = None, None
            for k in range(1, n_row):
                part = jnp.where(row >= k, came[k - 1, at, :].astype(F32), 0.0)
                total = part if total is None else total + decay * part
                passing = kept[k - 1, head // hb, head % hb : head % hb + 1, :]
                decay = passing if decay is None else decay * passing
            state_in[at, :] = total
        for copy in states():
            copy.wait_send()
        for at in range(2 * steps):
            for copy in pieces(at):
                copy.wait_send()


def placed(value, index, count):
    out = jnp.zeros((count,) + value.shape, F32)
    return lax.dynamic_update_slice(out, value[None], (index,) + (0,) * value.ndim)


def turned(value, axis):
    return lax.all_gather(value, axis, axis=0, tiled=True)


def per_device(hidden_in, grad_out, lengths, norm_gain, inner_proj, state_proj, step_proj, conv_inner, conv_inner_bias,
               conv_state, conv_state_bias, step_bias, decay_log, skip_gain, gate_gain, out_proj):
    cols_here, rows = hidden_in.shape
    ncols = lax.axis_size("col")
    nrow = lax.axis_size("row")
    width = cols_here * ncols
    inner = inner_proj.shape[0]
    heads = step_proj.shape[0]
    col_index = lax.axis_index("col")
    nc = rows // Q
    hb = max(k for k in (1, 2, 3, 4) if heads % k == 0)
    nb = heads // hb
    bh = hb * HEADDIM


    gain_full = norm_gain.astype(F32)
    gain8 = jnp.broadcast_to(gain_full[None], (8, width))
    hx, x4, z_w, bd4 = open_up(hidden_in, inner_proj, state_proj, step_proj)
    out_w, grad_now, hx = lax.optimization_barrier((out_proj, grad_out, hx))
    z_far = swapped(z_w, "row", 2)
    z_far, out_w = lax.optimization_barrier((z_far, out_w))
    out_far = swapped(out_w, "row", 2)
    if ncols == 2:
        grads = [grad_now, swapped(grad_now, "col", 1)]
    else:
        grads = [lax.all_gather(grad_now, "col", axis=0, tiled=True)]

    bm = 2 * bh if nb % 2 == 0 else bh
    part4 = pl.BlockSpec((nrow, bm, width // nrow), lambda n: (0, n, 0))
    ext = rows + Q
    normed_ext, normed_by, rstd8, live8, xin, bdin, dt = pl.pallas_call(
        functools.partial(project_kernel, nrow, lax.axis_size("dp"), hb),
        grid=(inner // bm,),
        in_specs=[SMEM, whole(width, ext), whole(8, width), part4, whole(*bd4.shape)],
        out_specs=[whole(width, ext), whole(width, rows), whole(8, rows), whole(8, rows), pl.BlockSpec((bm, ext), lambda n: (n, 0)), whole(2 * STATE, ext), whole(nb, 8, rows)],
        out_shape=[shape(BF16, width, ext), shape(BF16, width, rows), shape(F32, 8, rows), shape(F32, 8, rows), shape(F32, inner, ext), shape(F32, 2 * STATE, ext), shape(F32, nb, 8, rows)],
        compiler_params=params(),
        scratch_shapes=[pltpu.VMEM((1, width, Q), F32)],
        cost_estimate=pl.CostEstimate(flops=8 * 10**9, bytes_accessed=20 * 10**6, transcendentals=0),
        name="project",
    )(lengths, hx, gain8, x4, bd4)
    rstd_in = rstd8[:1]
    by_head = jnp.pad(jnp.stack([step_bias, decay_log, skip_gain]), ((0, 5), (0, 128 - heads)))

    def taps_of(taps, bias):
        return jnp.pad(jnp.concatenate([taps, bias[None]], axis=0).astype(F32), ((0, 7 - CONV), (0, 0)))

    taps = taps_of(conv_inner, conv_inner_bias)
    bctaps = taps_of(conv_state, conv_state_bias)
    gate = jnp.broadcast_to(gate_gain.astype(F32)[None], (8, inner))

    tok = pl.BlockSpec((bh, rows), lambda n: (n, 0))
    tok_ext = pl.BlockSpec((bh, rows + Q), lambda n: (n, 0))
    eight = pl.BlockSpec((8, bh), lambda n: (0, n))
    bc_ext = pl.BlockSpec((2 * STATE, rows + Q), lambda n: (0, 0))
    state_spec = pl.BlockSpec((bh, STATE), lambda n: (n, 0))
    chunks = pl.BlockSpec((nc, bh, STATE), lambda n: (0, n, 0))
    rows_spec = pl.BlockSpec((1, 6, 8, rows), lambda n: (n, 0, 0, 0))
    head_tok = pl.BlockSpec((1, 8, rows), lambda n: (n, 0, 0))
    head_q = pl.BlockSpec((1, 8, Q), lambda n: (n, 0, 0))
    head8 = pl.BlockSpec((1, 8, 8), lambda n: (n, 0, 0))

    u, ubc, bc, rowpack, scores, y_in, fresh, final, keep, hpar = pl.pallas_call(
        functools.partial(enter_kernel, nc, hb),
        grid=(nb,),
        in_specs=[SMEM, tok_ext, bc_ext, whole(nb, 8, rows), whole(8, 128), eight, whole(8, 2 * STATE),
                  pl.BlockSpec(memory_space=pl.ANY)],
        out_specs=[tok, whole(2 * STATE, rows), whole(2 * STATE, rows), whole(nb, 6, 8, rows), whole(nc, Q, Q), tok, chunks,
                   state_spec, whole(nb, 8, Q), whole(nb, 8, 8)],
        out_shape=[shape(F32, inner, rows), shape(F32, 2 * STATE, rows), shape(F32, 2 * STATE, rows),
                   shape(F32, nb, 6, 8, rows), shape(F32, nc, Q, Q), shape(F32, inner, rows), shape(F32, nc, inner, STATE),
                   shape(BF16, inner, STATE), shape(F32, nb, 8, Q), shape(F32, nb, 8, 8)],
        scratch_shapes=[pltpu.VMEM((bh, STATE), F32), pltpu.VMEM((CONV + 1, bh, Q), F32), pltpu.VMEM((CONV + 1, 2 * STATE, Q), F32)],
        compiler_params=params(),
        cost_estimate=pl.CostEstimate(flops=3 * 10**10, bytes_accessed=40 * 10**6, transcendentals=0),
        name="enter",
    )(lengths, xin, bdin, dt, by_head, taps, bctaps, z_far)

    steps = inner // bm
    block = pl.BlockSpec((bm, width // nrow), lambda n: (jnp.minimum(n, steps - 1), 0))
    block_after = pl.BlockSpec((bm, width // nrow), lambda n: (jnp.maximum(n - steps, 0), 0))
    anywhere = pl.BlockSpec(memory_space=pl.ANY)
    second = pl.pallas_call(
        functools.partial(second_kernel, nrow, lax.axis_size("dp"), steps, hb, ncols == 2),
        grid=(2 * steps,),
        in_specs=[anywhere] * 4 + [block] * 2 + [block_after] * 2 + [whole(width, ext)] + [whole(*value.shape) for value in grads]
        + [whole(8, rows), whole(inner, STATE), whole(nb, 8, Q)],
        out_specs=[pl.BlockSpec((nrow, bm, width // nrow), lambda n: (0, jnp.minimum(n, steps - 1), 0)),
                   pl.BlockSpec((bm, rows), lambda n: (jnp.minimum(n, steps - 1), 0)),
                   pl.BlockSpec((nrow, bm, width // nrow), lambda n: (0, jnp.maximum(n - steps, 0), 0)),
                   pl.BlockSpec((bm, rows), lambda n: (jnp.maximum(n - steps, 0), 0)),
                   whole(inner, STATE), whole(width, rows)],
        out_shape=[shape(BF16, nrow, inner, width // nrow), shape(F32, inner, rows)] * 2 + [shape(F32, inner, STATE), shape(BF16, width, rows)],
        scratch_shapes=[pltpu.VMEM((width, rows), BF16), pltpu.VMEM((2, 2, inner, width // nrow), BF16), pltpu.VMEM((nrow - 1, inner, STATE), BF16),
                        pltpu.VMEM((nrow - 1, nb, 8, Q), F32), pltpu.SemaphoreType.DMA((2, 4 * steps)),
                        pltpu.SemaphoreType.DMA((2, 2 * (nrow - 1)))],
        compiler_params=pltpu.CompilerParams(vmem_limit_bytes=VMEM_LIMIT, collective_id=3, has_side_effects=True),
        cost_estimate=pl.CostEstimate(flops=10**10, bytes_accessed=30 * 10**6, transcendentals=0),
        name="second",
    )(z_w, z_far, out_w, out_far, z_w, z_far, out_w, out_far, normed_ext, *grads, live8, final, keep)
    z4, z, out4, grad_gated, state_in, grad_by = second

    y, states, stats = pl.pallas_call(
        functools.partial(across_kernel, nc, hb),
        grid=(nb,),
        in_specs=[tok, chunks, state_spec, whole(2 * STATE, rows), rows_spec, tok, tok, eight],
        out_specs=[tok, chunks, whole(2, 8, rows)],
        out_shape=[shape(F32, inner, rows), shape(F32, nc, inner, STATE), shape(F32, 2, 8, rows)],
        scratch_shapes=[pltpu.VMEM((bh, STATE), F32), pltpu.VMEM((1, bh, Q), F32)],
        compiler_params=params(),
        cost_estimate=pl.CostEstimate(flops=10**10, bytes_accessed=35 * 10**6, transcendentals=0),
        name="across",
    )(y_in, fresh, state_in, bc, rowpack, z, grad_gated, gate)

    sums = col_sum(jnp.sum(stats, axis=1))
    inner_width = inner * ncols
    rstd_gate = lax.rsqrt(sums[0] / inner_width + EPS)
    pull = rstd_gate * rstd_gate * rstd_gate * (sums[1] / inner_width)
    token_rows = jnp.concatenate([rstd_gate[None], pull[None], jnp.zeros((6, rows), F32)], axis=0)

    gated, grad_z, grad_y, adj, adj_first, ggate = pl.pallas_call(
        functools.partial(gate_kernel, nc, hb),
        grid=(nb,),
        in_specs=[tok, tok, tok, whole(8, rows), eight, whole(2 * STATE, rows), rows_spec],
        out_specs=[tok, tok, tok, chunks, state_spec, eight],
        out_shape=[shape(BF16, inner, rows), shape(BF16, inner, rows), shape(F32, inner, rows),
                   shape(F32, nc, inner, STATE), shape(BF16, inner, STATE), shape(F32, 8, inner)],
        scratch_shapes=[pltpu.VMEM((bh, STATE), F32), pltpu.VMEM((bh, Q), F32), pltpu.VMEM((1, bh, Q), F32)],
        compiler_params=params(),
        cost_estimate=pl.CostEstimate(flops=10**10, bytes_accessed=40 * 10**6, transcendentals=0),
        name="gate",
    )(y, z, grad_gated, token_rows, gate, bc, rowpack)

    adj_in = chained(adj_first, keep, hb, -1)
    def turned_product(w4, value):
        return lax.dot_general(w4, value, (((1,), (0,)), ((), ())), preferred_element_type=F32).reshape(-1, rows)

    def halves_of_features(products):
        return [sum(turned_product(lax.dynamic_slice_in_dim(w4, at * (nrow // 2), nrow // 2, 0), value) for w4, value in products)
                for at in (1 - col_index, col_index)]

    if ncols == 2:
        mixed_other, mixed = halves_of_features([(out4, gated)])
        mixed_come = swapped(mixed_other.astype(BF16), "col", 1)

    n_dp = lax.axis_size("dp")
    early, grads_early, first_z = {}, [], 0
    if nb >= 5 and inner % 768 == 0:
        first_z = inner // 3
        grads_early = [nt(grad_by, gated).astype(BF16), nt(normed_by, grad_z[:first_z]).astype(BF16)]
        each = inner // 6
        places = [(0, k * each, each) for k in range(6)] + [(1, k * each, each) for k in range(2)]
        early = {"pieces": places, "groups": [(2 * k, 2 * k + 1) for k in range(4)], "steps": nb}
    quarter = width // 4
    once = pl.Buffered(1)
    held = pl.BlockSpec(memory_space=pltpu.VMEM)
    back_out = pl.pallas_call(
        functools.partial(back_kernel, nc, hb, heads, early, n_dp),
        grid=(nb,),
        in_specs=[SMEM, tok, tok_ext, tok, tok, chunks, chunks, state_spec, whole(2 * STATE, rows), whole(nc, Q, Q), rows_spec, head8, eight]
        + [pl.BlockSpec(value.shape, lambda n: (0, 0), pipeline_mode=once) for value in grads_early],
        out_specs=[tok, pl.BlockSpec((bh, Q), lambda n: (n, 0)), pl.BlockSpec((bh, Q), lambda n: (n, 0)), eight, head_tok,
                   whole(nc, Q, Q), whole(2 * STATE, rows), whole(8, Q)] + [whole(quarter // n_dp, value.shape[1]) for value in grads_early],
        out_shape=[shape(BF16, inner, rows), shape(F32, inner, Q), shape(BF16, inner, Q), shape(F32, 8, inner), shape(F32, nb, 8, rows),
                   shape(F32, nc, Q, Q), shape(F32, 2 * STATE, rows), shape(F32, 8, Q)]
        + [shape(F32, quarter // n_dp, value.shape[1]) for value in grads_early],
        scratch_shapes=[pltpu.VMEM((bh, STATE), F32), pltpu.VMEM((bh, Q), F32), pltpu.VMEM((CONV + 1, bh, Q), F32),
                        pltpu.VMEM((5, nb, 8, rows), F32), pltpu.VMEM((CONV + 1, bh, Q), F32), pltpu.VMEM((2, bh, Q), F32)]
        + ([pltpu.VMEM((8, 2 * quarter, each), BF16), pltpu.VMEM((8, quarter, each), BF16),
            pltpu.VMEM((8, quarter // n_dp * (n_dp - 1), each), BF16), pltpu.SemaphoreType.DMA((2, 8 * (n_dp + 1)))] if early else []),
        compiler_params=pltpu.CompilerParams(vmem_limit_bytes=VMEM_LIMIT, collective_id=4, has_side_effects=True) if early else params(),
        cost_estimate=pl.CostEstimate(flops=6 * 10**10, bytes_accessed=50 * 10**6, transcendentals=0),
        name="back",
    )(lengths, u, xin, grad_y, y, states, adj, adj_in, bc, scores, rowpack, hpar, taps, *grads_early)
    gx, gx_last, rim_x, gtaps, gdt, gscores, gbct, hsum = back_out[:8]
    if ncols == 2:
        mixed_come, gx = lax.optimization_barrier((mixed_come, gx))

    if ncols == 2:
        mixed = mixed + mixed_come.astype(F32)
    else:
        mixed = lax.psum_scatter(turned_product(out4, gated).astype(BF16), "col", scatter_dimension=0, tiled=True).astype(F32)
    hidden_f = hidden_in.astype(F32)
    block_out = (hidden_f + live8[:1] * mixed).astype(BF16)

    small_width = -(-(2 * STATE + heads) // 128) * 128
    fused = ncols == 2 and bool(early)
    each = inner // 6 if inner % 768 == 0 else inner + -inner % 128
    sources = [(0, 0, None), (0, 0, 0), (0, first_z, 1)]
    pieces = [(0, 0, 2 * STATE), (0, 2 * STATE, small_width - 2 * STATE)]
    z_pieces = [(2, at, each) for at in range(0, inner - first_z, each)]
    x_pieces = [(1, at, each) for at in range(0, inner, each)]
    pieces = z_pieces + pieces + x_pieces if fused else pieces + z_pieces + x_pieces
    gbd = None
    if not fused:
        vmem = pl.BlockSpec(memory_space=pltpu.VMEM)
        gbc, gbc_last, rim_bc, gbctaps = pl.pallas_call(
            functools.partial(state_kernel, nc),
            grid=(1,),
            out_shape=[shape(BF16, 2 * STATE, rows), shape(F32, 2 * STATE, Q), shape(BF16, 2 * STATE, Q),
                       shape(F32, 8, (CONV + 1) * 2 * STATE)],
            in_specs=[SMEM, vmem, vmem, bc_ext, vmem, vmem, vmem],
            out_specs=[vmem] * 4,
            scratch_shapes=[pltpu.VMEM((2 * STATE, Q), F32), pltpu.VMEM((CONV + 1, 2 * STATE, Q), F32),
                            pltpu.VMEM((CONV + 1, 2 * STATE, Q), F32), pltpu.VMEM((2, 2 * STATE, Q), F32)],
            compiler_params=params(),
            cost_estimate=pl.CostEstimate(flops=10**9, bytes_accessed=6 * 10**6, transcendentals=0),
            name="state",
        )(lengths, bc, ubc, bdin, bctaps, gscores, gbct)

        def last_tokens(value, last, rim):
            return lax.dynamic_update_slice(value, (last + rim.astype(F32)).astype(BF16), (0, rows - Q))

        back_x, back_bc = from_before(rim_x, -1), from_before(rim_bc, -1)
        gx = last_tokens(gx, gx_last, back_x)
        gbd = jnp.concatenate([last_tokens(gbc, gbc_last, back_bc), gdt[:, :hb].reshape(heads, rows).astype(BF16),
                               jnp.zeros((bd4.shape[1] - 2 * STATE - heads, rows), BF16)], axis=0)

        gbd_padded = jnp.pad(gbd, ((0, small_width - gbd.shape[0]), (0, 0)))
    lefts, later = [normed_by], [gx, grad_z]
    if ncols == 2:
        later += [x4, z4, bd4, hx, grad_out]
        gn_given, plain = (gain8, rstd8), None
        if fused:
            later += [rim_x, gx_last, bc, ubc, bdin, bctaps, gscores, gbct, gdt]
    else:
        grad_normed = turned_product(z4, grad_z) + turned_product(x4, gx) + turned_product(bd4, gbd)
        whole_rows = hx[:, Q:].astype(F32) * rstd_in
        gain_here = lax.dynamic_slice_in_dim(gain_full, col_index * cols_here, cols_here)[:, None]
        gn_given, plain = None, (jnp.sum(whole_rows * gain_full[:, None] * grad_normed, axis=0)[None], jnp.sum(whole_rows * grad_normed, axis=1)[None])
        gn_here = lax.psum_scatter(grad_normed.astype(BF16), "col", scatter_dimension=0, tiled=True).astype(F32)
    if not early:
        sources.append((1, 0, len(later)))
        lefts.append(grad_by)
        later.append(gated)
        pieces += [(3, at, each) for at in range(0, inner, each)]
    sums, state_out, small_out, stat_out, grad_in = close(
        sources, pieces, lefts, None if fused else gbd_padded, (lengths, gtaps, ggate, hsum) if fused else (gtaps, ggate, gbctaps, hsum),
        gn_given, plain, later, (nc, hb, len(later)) if fused else ())
    if ncols != 2:
        stat_total = jnp.sum(stat_out, axis=0)
        grad_in = (grad_out.astype(F32) + rstd_in * gain_here * gn_here - hidden_f * (rstd_in * rstd_in) * (stat_total / width)).astype(BF16)
    g_out = back_out[8] if early else sums[3][:, :inner]
    (g_norm_gain, g_inner, g_state, g_step, g_taps, g_bias, g_bc_taps, g_bc_bias, g_step_bias, g_decay, g_skip, g_gate) = last(
        sums[0], sums[1], state_out, small_out, [back_out[9], sums[2]] if early else [sums[2]], heads, inner)
    return (
        block_out,
        grad_in,
        g_norm_gain[0],
        jnp.transpose(g_inner, (2, 0, 1)),
        g_state,
        g_step,
        g_taps,
        g_bias[0],
        g_bc_taps,
        g_bc_bias[0],
        g_step_bias[0],
        g_decay[0],
        g_skip[0],
        g_gate[0],
        g_out.T,
    )


def solution(mesh):
    col, tokens, sums = P("col"), P("col", ("dp", "row")), P("col", ("dp", "row"))
    return jax.shard_map(
        per_device,
        mesh=mesh,
        in_specs=(tokens, tokens, P("dp", None), P(), P("col", None, "row"), P("row", None), P("col", "row"),
                  P(None, "col"), col, P(), P(), col, col, col, col, P("col", "row")),
        out_specs=(tokens, tokens, P(), P("col", None, ("dp", "row")), P(), sums, P(), P(), P(), P(), P(), P(), P(), P(), sums),
        check_vma=False,
    )
```

```python
import functools

import jax
import jax.numpy as jnp
from jax import lax
from jax.experimental import pallas as pl
from jax.experimental.pallas import tpu as pltpu
from jax.sharding import PartitionSpec as P

HEADDIM = 64
STATE = 128
CONV = 4
Q = 128
EPS = 1e-05
LOG2E = 1.4426950408889634
F32 = jnp.float32
BF16 = jnp.bfloat16
HIGHEST = lax.Precision.HIGHEST
MESH = pl.DeviceIdType.MESH
VMEM_LIMIT = 56 * 1024 * 1024
CUM, STEP, ENTRY, TAIL, DEC, SIG = range(6)


def nn(a, b, precision=None):
    return lax.dot_general(a, b, (((1,), (0,)), ((), ())), precision=precision, preferred_element_type=F32)


def nt(a, b, precision=None):
    return lax.dot_general(a, b, (((1,), (1,)), ((), ())), precision=precision, preferred_element_type=F32)


def tn(a, b, precision=None):
    return lax.dot_general(a, b, (((0,), (0,)), ((), ())), precision=precision, preferred_element_type=F32)


def halves(v):
    high = v.astype(BF16)
    return high, (v - high.astype(F32)).astype(BF16)


def nn3(a, b):
    (ah, al), (bh, bl) = halves(a), halves(b)
    return nn(jnp.concatenate([ah, ah, al], 1), jnp.concatenate([bh, bl, bh], 0))


def nt3(a, b):
    (ah, al), (bh, bl) = halves(a), halves(b)
    return nt(jnp.concatenate([ah, ah, al], 1), jnp.concatenate([bh, bl, bh], 1))


def sigm(v):
    return 0.5 + 0.5 * jnp.tanh(0.5 * v)


def iota(shape, dim):
    return lax.broadcasted_iota(jnp.int32, shape, dim)


def segment_of(place, ends):
    total = (place >= ends[0]).astype(jnp.int32)
    for end in ends[1:]:
        total = total + (place >= end).astype(jnp.int32)
    return jnp.where(place < 0, -1, total)


def chunk_of(c):
    return pl.ds(pl.multiple_of(c * Q, Q), Q)


def shift_masks(place, ends):
    segment = segment_of(place, ends)
    return [(segment_of(place - d, ends) == segment).astype(F32) for d in range(1, CONV)]


def shifted_right(now, earlier, d, lane):
    return pltpu.roll(jnp.where(lane >= Q - d, earlier, now), d, 1)


def shifted_left(now, later, d, lane):
    return pltpu.roll(jnp.where(lane < d, later, now), Q - d, 1)


def conv_tile(now, earlier, taps, masks, lane):
    total = taps(CONV) + taps(CONV - 1) * now
    for d in range(1, CONV):
        total = total + taps(CONV - 1 - d) * (shifted_right(now, earlier, d, lane) * masks[d - 1])
    return total


def spread(rows_ref, out):
    cols = jnp.transpose(rows_ref[...])
    for k in range(out.shape[0]):
        out[k] = jnp.broadcast_to(cols[:, k : k + 1], out.shape[1:])


def thirds(v):
    high, rest = v.astype(BF16), v
    rest = rest - high.astype(F32)
    middle = rest.astype(BF16)
    return jnp.concatenate([high, middle, (rest - middle.astype(F32)).astype(BF16)], -1)


def times_flags(v, flags):
    return nn(thirds(v), jnp.concatenate([flags.astype(BF16)] * 3, 0))


def stacked(v, count):
    return jnp.concatenate([v[:, c * Q : (c + 1) * Q] for c in range(count)], 0)


def scalars(lengths_ref, rows):
    ends = [lengths_ref[0, 0]]
    for k in range(1, lengths_ref.shape[1]):
        ends.append(ends[-1] + lengths_ref[0, k])
    return lax.axis_index("row") * rows, ends


def enter_kernel(nc, hb, place_ref, xin_ref, bcin_ref, dt_ref, heads_ref, taps8_ref, bctaps8_ref, wait_ref,
                 u_ref, ubc_ref, bc_ref, rows_ref, scores_ref, y_ref, fresh_ref, final_ref, pass_ref, hpar_ref, state, taps_ref, bctaps_ref):
    base, ends = scalars(place_ref, nc * Q)
    wide = iota((HEADDIM, Q), 1)
    block = pl.program_id(0)
    spread(taps8_ref, taps_ref)

    @pl.when(block == 0)
    def _():
        spread(bctaps8_ref, bctaps_ref)
        lane = iota((1, Q), 1)
        row, col = iota((Q, Q), 0), iota((Q, Q), 1)

        def body(c, _):
            masks = shift_masks(base + c * Q + lane, ends)
            for part in range(2 * STATE // HEADDIM):
                at = slice(part * HEADDIM, (part + 1) * HEADDIM)
                u = conv_tile(bcin_ref[at, chunk_of(c + 1)], bcin_ref[at, chunk_of(c)], lambda k: bctaps_ref[k, at, :], masks, wide)
                ubc_ref[at, chunk_of(c)] = u
                bc_ref[at, chunk_of(c)] = u * sigm(u)
            start = base + c * Q
            same = (segment_of(start + row, ends) == segment_of(start + col, ends)) & (row >= col)
            score = nn3(jnp.transpose(bc_ref[STATE:, chunk_of(c)]), bc_ref[:STATE, chunk_of(c)])
            scores_ref[c] = jnp.where(same, score, 0.0)
            return 0

        lax.fori_loop(0, nc, body, 0, unroll=2)

        nb = dt_ref.shape[0]
        by_head = jnp.transpose(heads_ref[...])[:, :8]
        for n in range(nb):
            own = by_head[n * hb : (n + 1) * hb]
            hpar_ref[n] = own if hb == 8 else jnp.concatenate([own, jnp.zeros((8 - hb, 8), F32)], 0)
        raw = jnp.concatenate([dt_ref[n] + hpar_ref[n, :, 0:1] for n in range(nb)], 0)
        rate = jnp.concatenate([-jnp.exp(hpar_ref[n, :, 1:2]) for n in range(nb)], 0)
        small = jnp.exp(-jnp.abs(raw))
        steps = jnp.maximum(raw, 0.0) + jnp.log1p(small)
        sig = jnp.where(raw >= 0, 1.0, small) / (1.0 + small)
        each = nb * 8
        cums = times_flags(stacked(steps * rate * LOG2E, nc), row <= col)
        whole_sum = jnp.zeros((each, 1), F32)
        for c in range(nc):
            at = slice(c * Q, (c + 1) * Q)
            start = base + c * Q
            segment = segment_of(start + lane, ends)
            before = segment_of(start - 1, ends)
            after = segment_of(start + Q - 1, ends)
            cum = cums[c * each : (c + 1) * each]
            last = cum[:, Q - 1 : Q]
            entry = jnp.exp2(cum) * (segment == before).astype(F32)
            tail = jnp.exp2(last - cum) * (segment == after).astype(F32)
            decay = jnp.broadcast_to(jnp.exp2(last), (each, Q)) * (before == after).astype(F32)
            for n in range(nb):
                part = slice(n * 8, (n + 1) * 8)
                rows_ref[n, CUM, :, at] = cum[part]
                rows_ref[n, STEP, :, at] = steps[part, at]
                rows_ref[n, ENTRY, :, at] = entry[part]
                rows_ref[n, TAIL, :, at] = tail[part]
                rows_ref[n, DEC, :, at] = decay[part]
                rows_ref[n, SIG, :, at] = sig[part, at]
            whole_sum = whole_sum + last
        end = segment_of(base + nc * Q - 1, ends)
        keep = jnp.broadcast_to(jnp.exp2(whole_sum), (each, Q)) * (segment_of(base - 1, ends) == end).astype(F32)
        for n in range(nb):
            pass_ref[n] = keep[n * 8 : (n + 1) * 8]

    state[...] = jnp.zeros_like(state)

    def chunk(c, _):
        now = chunk_of(c)
        masks = shift_masks(base + c * Q + iota((1, Q), 1), ends)
        cum8 = rows_ref[block, CUM, :, now]
        cols = jnp.transpose(cum8)
        weighted = []
        for h in range(hb):
            at = slice(h * HEADDIM, (h + 1) * HEADDIM)
            hr = slice(h, h + 1)
            u = conv_tile(xin_ref[at, chunk_of(c + 1)], xin_ref[at, now], lambda k: taps_ref[k, at, :], masks, wide)
            u_ref[at, now] = u
            x = u * sigm(u)
            moved = x * rows_ref[block, STEP, hr, now]
            decay = jnp.exp2(jnp.minimum(cols[:, hr] - cum8[hr, :], 0.0))
            mixing = (decay * scores_ref[c]).astype(BF16)
            y_ref[at, now] = nt(moved.astype(BF16), mixing) + hpar_ref[block, hr, 2:3] * x
            weighted.append((moved * rows_ref[block, TAIL, hr, now]).astype(BF16))
        fresh = nt(jnp.concatenate(weighted, 0), bc_ref[:STATE, now].astype(BF16))
        fresh_ref[c] = fresh
        for h in range(hb):
            at = slice(h * HEADDIM, (h + 1) * HEADDIM)
            state[at, :] = state[at, :] * rows_ref[block, DEC, h : h + 1, now] + fresh[at, :]
        return 0

    lax.fori_loop(0, nc, chunk, 0, unroll=2)
    final_ref[...] = state[...].astype(BF16)


def across_kernel(nc, hb, y_ref, fresh_ref, start_ref, bc_ref, rows_ref, z_ref, gg_ref, gate8_ref,
                  y_out, states_ref, stat_ref, state, gate_ref):
    first = pl.program_id(0) == 0

    @pl.when(first)
    def _():
        stat_ref[...] = jnp.zeros_like(stat_ref)

    state[...] = start_ref[...]
    spread(gate8_ref, gate_ref)

    def chunk(c, _):
        states_ref[c] = state[...]
        outer = nn3(state[...], bc_ref[STATE:, chunk_of(c)])
        square = jnp.zeros((8, Q), F32)
        cross = jnp.zeros((8, Q), F32)
        for h in range(hb):
            at = slice(h * HEADDIM, (h + 1) * HEADDIM)
            y = y_ref[at, chunk_of(c)] + outer[at, :] * rows_ref[0, ENTRY, h : h + 1, chunk_of(c)]
            y_out[at, chunk_of(c)] = y
            z = z_ref[at, chunk_of(c)]
            gz = y * (z * sigm(z))
            other = gz * gate_ref[0, at, :] * gg_ref[at, chunk_of(c)]
            squared = gz * gz
            for k in range(HEADDIM // 8):
                square = square + squared[k * 8 : (k + 1) * 8]
                cross = cross + other[k * 8 : (k + 1) * 8]
            state[at, :] = state[at, :] * rows_ref[0, DEC, h : h + 1, chunk_of(c)] + fresh_ref[c, at, :]
        stat_ref[0, :, chunk_of(c)] += square
        stat_ref[1, :, chunk_of(c)] += cross
        return 0

    lax.fori_loop(0, nc, chunk, 0, unroll=2)


def lane_sums(v):
    return nt(jnp.ones((8, 2 * Q), BF16), jnp.concatenate(halves(v), 1))


def gate_kernel(nc, hb, y_ref, z_ref, gg_ref, tok_ref, gate8_ref, bc_ref, rows_ref,
                gated_ref, gz_ref, gy_ref, adj_ref, first_ref, ggate_ref, adjoint, gsum, gate_ref):
    spread(gate8_ref, gate_ref)
    adjoint[...] = jnp.zeros_like(adjoint)
    gsum[...] = jnp.zeros_like(gsum)

    def chunk(k, _):
        c = nc - 1 - k
        rstd = tok_ref[0:1, chunk_of(c)]
        pull = tok_ref[1:2, chunk_of(c)]
        lifted = []
        for h in range(hb):
            at = slice(h * HEADDIM, (h + 1) * HEADDIM)
            y, z, gg = y_ref[at, chunk_of(c)], z_ref[at, chunk_of(c)], gg_ref[at, chunk_of(c)]
            s = sigm(z)
            silu = z * s
            gz = y * silu
            gate = gate_ref[0, at, :]
            gzr = gz * rstd
            gated_ref[at, chunk_of(c)] = (gzr * gate).astype(BF16)
            gsum[at, :] += gzr * gg
            ggz = rstd * (gate * gg) - gz * pull
            gy = ggz * silu
            gz_ref[at, chunk_of(c)] = (ggz * y * (s * (1.0 + z * (1.0 - s)))).astype(BF16)
            gy_ref[at, chunk_of(c)] = gy
            lifted.append(gy * rows_ref[0, ENTRY, h : h + 1, chunk_of(c)])
        adj = nt3(jnp.concatenate(lifted, 0), bc_ref[STATE:, chunk_of(c)])
        adj_ref[c] = adj
        for h in range(hb):
            at = slice(h * HEADDIM, (h + 1) * HEADDIM)
            adjoint[at, :] = adjoint[at, :] * rows_ref[0, DEC, h : h + 1, chunk_of(c)] + adj[at, :]
        return 0

    lax.fori_loop(0, nc, chunk, 0, unroll=2)
    first_ref[...] = adjoint[...].astype(BF16)
    ggate_ref[...] = lane_sums(gsum[...])


def conv_back(gu, later, taps, masks, lane):
    moved = [gu]
    total = taps(CONV - 1) * gu
    for d in range(1, CONV):
        part = shifted_left(gu * masks[d - 1], later * masks[CONV - 1 + d - 1], d, lane)
        moved.append(part)
        total = total + taps(CONV - 1 - d) * part
    return total, moved


def conv_rim(gu, taps, masks, lane, rim_in):
    total = jnp.zeros_like(gu)
    sums = []
    for d in range(1, CONV):
        part = pltpu.roll(jnp.where(lane < d, gu * masks[d - 1], 0.0), Q - d, 1)
        total = total + taps(CONV - 1 - d) * part
        sums.append(rim_in * part)
    return total, sums


def back_masks(base, c, ends):
    lane = iota((1, Q), 1)
    return shift_masks(base + c * Q + lane, ends) + shift_masks(base + (c + 1) * Q + lane, ends)


def total_rows(v):
    return jnp.sum(v, 0, keepdims=True)


def early_sums(early, n_dp, grads, outs, come1, come2, come3, sems):
    half = grads[0].shape[0] // 2
    views = []
    for k, (a, at, width) in enumerate(early["pieces"]):
        columns = pl.ds(at, width)
        views.append((grads[a].at[pl.ds(0, half), columns], grads[a].at[pl.ds(half, half), columns], come1.at[k], come2.at[k], come3.at[k],
                      outs[a].at[:, columns]))
    return RowSums(n_dp, views, sems)


def sent_sums(early, n_dp, grads, outs, *refs):
    sums = early_sums(early, n_dp, grads, outs, *refs)
    groups = early["groups"]
    for t in range(early["steps"]):
        @pl.when(pl.program_id(0) == t)
        def _():
            if t == 0:
                meet(sums.partners())
            for stage, lag in ((sums.along, 2), (sums.across, 1), (sums.pair, 0), (sums.finish, 3)):
                if 0 <= t - lag < len(groups):
                    for p in groups[t - lag]:
                        stage(p)


def end_sums(early, n_dp, grads, outs, *refs):
    sums = early_sums(early, n_dp, grads, outs, *refs)
    groups, steps = early["groups"], early["steps"]

    @pl.when(pl.program_id(0) == steps - 1)
    def _():
        for t in range(steps, len(groups) + 3):
            for stage, lag in ((sums.along, 2), (sums.across, 1), (sums.finish, 3)):
                if 0 <= t - lag < len(groups):
                    for p in groups[t - lag]:
                        stage(p)
        for p in range(len(early["pieces"])):
            sums.first(p).wait_send()
            sums.sent(p)


def back_kernel(nc, hb, heads, early, n_dp, place_ref, u_ref, xin_ref, gy_ref, y_ref, states_ref, adj_ref, start_ref, bc_ref, scores_ref,
                rows_ref, hpar_ref, taps8_ref, *refs):
    refs = list(refs)
    take = lambda count: [refs.pop(0) for _ in range(count)]
    arrays = 2 if early else 0
    grads = take(arrays)
    gx_ref, gxlast_ref, rim_ref, gtaps_ref, gdt_ref, gscores, gbct, hsum_ref = take(8)
    sums_out = take(arrays)
    adjoint, gnext, tapsum, hrow, taps_ref, ends_at = take(6)
    if early:
        sent_sums(early, n_dp, grads, sums_out, *refs)
    spread(taps8_ref, taps_ref)
    base, ends = scalars(place_ref, nc * Q)
    wide = iota((HEADDIM, Q), 1)
    block = pl.program_id(0)

    @pl.when(block == 0)
    def _():
        hsum_ref[...] = jnp.zeros_like(hsum_ref)
        gscores[...] = jnp.zeros_like(gscores)
        gbct[...] = jnp.zeros_like(gbct)
        hrow[...] = jnp.zeros_like(hrow)

    adjoint[...] = start_ref[...]
    gnext[...] = jnp.zeros_like(gnext)
    tapsum[...] = jnp.zeros_like(tapsum)

    def chunk(k, _):
        c = nc - 1 - k
        now = chunk_of(c)
        masks = back_masks(base, c, ends)
        from_later = nn(adjoint[...].astype(BF16), bc_ref[:STATE, now].astype(BF16))
        cum8 = rows_ref[0, CUM, :, now]
        cols = jnp.transpose(cum8)
        lifted, weighted = [], []
        for h in range(hb):
            at = slice(h * HEADDIM, (h + 1) * HEADDIM)
            hr = slice(h, h + 1)
            u = u_ref[at, now]
            gy = gy_ref[at, now]
            s = sigm(u)
            x = u * s
            step = rows_ref[0, STEP, hr, now]
            tail = rows_ref[0, TAIL, hr, now]
            moved = x * step
            moved_low = moved.astype(BF16)
            gy_low = gy.astype(BF16)
            decay = jnp.exp2(jnp.minimum(cols[:, hr] - cum8[hr, :], 0.0))
            gmix = tn(gy_low, moved_low)
            gscores[c] += gmix * decay
            gmoved = nn(gy_low, (decay * scores_ref[c]).astype(BF16))
            later = from_later[at, :] * tail
            lifted.append((gy * rows_ref[0, ENTRY, hr, now]).astype(BF16))
            weighted.append((moved * tail).astype(BF16))
            skip = hpar_ref[0, hr, 2:3]
            taken = gy_low.astype(F32) * (y_ref[at, now] - skip * x) - moved_low.astype(F32) * gmoved
            hrow[0, block, hr, now] = total_rows(taken)
            hrow[1, block, hr, now] = total_rows(moved * later)
            hrow[2, block, hr, now] = total_rows(adjoint[at, :] * states_ref[c, at, :]) * rows_ref[0, DEC, hr, now]
            gmoved = gmoved + later
            hrow[3, block, hr, now] = total_rows(x * gmoved)
            hrow[4, block, hr, now] = total_rows(x * gy)
            gx = gmoved * step + skip * gy
            gu = gx * (s * (1.0 + u * (1.0 - s)))
            gin, shifts = conv_back(gu, gnext[at, :], lambda k: taps_ref[k, at, :], masks, wide)
            gnext[at, :] = gu
            gx_ref[at, now] = gin.astype(BF16)

            ends_at[jnp.minimum(k, 1), at, :] = gin
            xin = xin_ref[at, chunk_of(c + 1)]
            for d in range(CONV):
                tapsum[d, at, :] += xin * shifts[d]
            tapsum[CONV, at, :] += gu
        gbct[STATE:, now] += tn(states_ref[c].astype(BF16), jnp.concatenate(lifted, 0))
        gbct[:STATE, now] += tn(adjoint[...].astype(BF16), jnp.concatenate(weighted, 0))
        for h in range(hb):
            at = slice(h * HEADDIM, (h + 1) * HEADDIM)
            adjoint[at, :] = adjoint[at, :] * rows_ref[0, DEC, h : h + 1, now] + adj_ref[c, at, :]
        return 0

    lax.fori_loop(0, nc, chunk, 0, unroll=2)

    gxlast_ref[...] = ends_at[0]
    masks = back_masks(base, 0, ends)
    for h in range(hb):
        at = slice(h * HEADDIM, (h + 1) * HEADDIM)
        rim, sums = conv_rim(gnext[at, :], lambda k: taps_ref[k, at, :], masks, wide, xin_ref[at, :Q])
        rim_ref[at, :] = rim.astype(BF16)
        for d in range(1, CONV):
            tapsum[d, at, :] += sums[d - 1]
    gtaps_ref[...] = jnp.concatenate([lane_sums(tapsum[d])[0:1] for d in range(CONV + 1)] + [jnp.zeros((7 - CONV, hb * HEADDIM), F32)], 0)

    row, col = iota((Q, Q), 0), iota((Q, Q), 1)
    glogs = (times_flags(stacked(hrow[0, block], nc), row >= col) + times_flags(stacked(hrow[1, block], nc), row < col)
             + times_flags(stacked(hrow[2, block], nc), row >= 0))
    rate = -jnp.exp(hpar_ref[0, :, 1:2])
    total = [jnp.zeros((8, Q), F32) for _ in range(3)]
    for c in range(nc):
        at = slice(c * Q, (c + 1) * Q)
        glog = glogs[c * 8 : (c + 1) * 8] * rate
        gdt = (hrow[3, block, :, at] + glog) * rows_ref[0, SIG, :, at]
        gdt_ref[0, :, at] = gdt
        total[0] = total[0] + gdt
        total[1] = total[1] + glog * rows_ref[0, STEP, :, at]
        total[2] = total[2] + hrow[4, block, :, at]
    sums = times_flags(jnp.concatenate(total, 0), row >= 0)
    first = lax.axis_index("col") * heads + block * hb
    lane = iota((1, Q), 1)
    for k in range(3):
        for h in range(hb):
            hsum_ref[k : k + 1, :] += jnp.where(lane == first + h, sums[k * 8 + h : k * 8 + h + 1, :], 0.0)

    if early:
        end_sums(early, n_dp, grads, sums_out, *refs)


def state_kernel(nc, place_ref, bc_ref, ubc_ref, bcin_ref, bctaps8_ref, gscores_in, gbct_in,
                 gbc_ref, gbclast_ref, bcrim_ref, gbctaps_ref, gnext, tapsum, bctaps_ref, ends_at):
    spread(bctaps8_ref, bctaps_ref)
    base, ends = scalars(place_ref, nc * Q)
    row, col = iota((Q, Q), 0), iota((Q, Q), 1)
    wide = iota((HEADDIM, Q), 1)
    gnext[...] = jnp.zeros_like(gnext)
    tapsum[...] = jnp.zeros_like(tapsum)
    tiles = [slice(k * HEADDIM, (k + 1) * HEADDIM) for k in range(2 * STATE // HEADDIM)]

    def body(k, _):
        c = nc - 1 - k
        now = chunk_of(c)
        start = base + c * Q
        same = (segment_of(start + row, ends) == segment_of(start + col, ends)) & (row >= col)
        gscore = jnp.where(same, gscores_in[c], 0.0)
        masks = back_masks(base, c, ends)
        inter = gbct_in[:, now]
        g_c = inter[STATE:] + nt3(bc_ref[:STATE, now], gscore)
        g_b = inter[:STATE] + nn3(bc_ref[STATE:, now], gscore)
        g_bc = jnp.concatenate([g_b, g_c], 0)
        for at in tiles:
            u = ubc_ref[at, now]
            s = sigm(u)
            gu = g_bc[at] * (s * (1.0 + u * (1.0 - s)))
            gin, shifts = conv_back(gu, gnext[at, :], lambda k: bctaps_ref[k, at, :], masks, wide)
            gnext[at, :] = gu
            gbc_ref[at, now] = gin.astype(BF16)

            ends_at[jnp.minimum(k, 1), at, :] = gin
            xin = bcin_ref[at, chunk_of(c + 1)]
            for d in range(CONV):
                tapsum[d, at, :] += xin * shifts[d]
            tapsum[CONV, at, :] += gu
        return 0

    lax.fori_loop(0, nc, body, 0)
    gbclast_ref[...] = ends_at[0]
    masks = back_masks(base, 0, ends)
    for at in tiles:
        rim, more = conv_rim(gnext[at, :], lambda k: bctaps_ref[k, at, :], masks, wide, bcin_ref[at, :Q])
        bcrim_ref[at, :] = rim.astype(BF16)
        for d in range(1, CONV):
            tapsum[d, at, :] += more[d - 1]
    for d in range(CONV + 1):
        gbctaps_ref[:, d * 2 * STATE : (d + 1) * 2 * STATE] = lane_sums(tapsum[d])


def whole(*shape):
    return pl.BlockSpec(shape, lambda n: (0,) * len(shape))


def params():
    return pltpu.CompilerParams(vmem_limit_bytes=VMEM_LIMIT)


SMEM = pl.BlockSpec(memory_space=pltpu.SMEM)


def shape(dtype, *dims):
    return jax.ShapeDtypeStruct(dims, dtype)


def after(value, *others):
    return lax.optimization_barrier((value,) + others)[0]


def moved(value, axis, steps):
    n = lax.axis_size(axis)
    return lax.ppermute(value, axis, [(k, (k + steps) % n) for k in range(n)])


def swapped(value, axis, bit):
    n = lax.axis_size(axis)
    return lax.ppermute(value, axis, [(k, k ^ bit) for k in range(n)])


def col_sum(value):
    if lax.axis_size("col") == 2:
        return value + swapped(value, "col", 1)
    return lax.psum(value, "col")


def from_before(value, steps):
    n = lax.axis_size("row")
    pairs = [(k, k + steps) for k in range(max(0, -steps), min(n, n - steps))]
    return lax.ppermute(value, "row", pairs)


def chained(state, keep, hb, direction):
    nb, inner = keep.shape[0], state.shape[0]
    flat = keep.reshape(nb * 8, Q)
    high, low = halves(flat)
    packed = jnp.concatenate([state, high, low], axis=0)
    total, decay = None, None
    for k in range(1, lax.axis_size("row")):
        part = from_before(packed, direction * k)
        passing = part[inner : inner + nb * 8].astype(F32) + part[inner + nb * 8 :].astype(F32)
        passing = jnp.repeat(passing.reshape(nb, 8, Q)[:, :hb].reshape(nb * hb, Q), HEADDIM, axis=0)
        part = part[:inner].astype(F32)
        total = part if total is None else total + decay * part
        decay = passing if decay is None else decay * passing
    return total


def sum_stages(n_row):
    order, bits = [0], []
    bit = n_row // 2
    while bit:
        order = [k + bit for k in order] + order
        bits.insert(0, bit)
        bit //= 2
    return order, bits


def far(source, target, sems, k, axis, place):
    return pltpu.make_async_remote_copy(
        src_ref=source, dst_ref=target, send_sem=sems.at[0, k], recv_sem=sems.at[1, k],
        device_id={axis: place}, device_id_type=MESH)


def meet(partners):
    barrier = pltpu.get_barrier_semaphore()
    for axis, place in partners:
        pl.semaphore_signal(barrier, inc=1, device_id={axis: place}, device_id_type=MESH)
    pl.semaphore_wait(barrier, len(partners))


class RowSums:
    def __init__(self, n_dp, pieces, sems):
        self.row, dp = lax.axis_index("row"), lax.axis_index("dp")
        self.n_dp, self.pieces, self.sems = n_dp, pieces, sems
        self.dps = [lax.rem(dp + k, n_dp) for k in range(n_dp)]
        self.quarter = pieces[0][3].shape[0]
        self.block = self.quarter // n_dp
        self.per = n_dp + 1

    def partners(self):
        return [("row", self.row ^ 1), ("row", self.row ^ 2)] + [("dp", d) for d in self.dps[1:]]

    def first(self, p):
        send, _, come1, _, _, _ = self.pieces[p]
        return far(send, come1, self.sems, p * self.per, "row", self.row ^ 1)

    def second(self, p):
        _, _, come1, come2, _, _ = self.pieces[p]
        return far(come1.at[pl.ds(0, self.quarter)], come2, self.sems, p * self.per + 1, "row", self.row ^ 2)

    def third(self, p):
        _, _, _, come2, come3, _ = self.pieces[p]
        block = self.block
        return [far(come2.at[pl.ds(k * block, block)], come3.at[pl.ds((k - 1) * block, block)], self.sems, p * self.per + 1 + k, "dp", self.dps[k])
                for k in range(self.n_dp - 1, 0, -1)]

    def pair(self, p):
        self.first(p).start()

    def across(self, p):
        _, kept, come1, _, _, _ = self.pieces[p]
        self.first(p).wait_recv()
        add_rows(come1, 0, kept, 0, self.quarter)
        self.second(p).start()
        add_rows(come1, self.quarter, kept, self.quarter, self.quarter)

    def along(self, p):
        _, _, come1, come2, _, _ = self.pieces[p]
        self.second(p).wait_recv()
        add_rows(come2, 0, come1, self.quarter, self.quarter)
        for copy in self.third(p):
            copy.start()

    def finish(self, p):
        _, _, _, come2, come3, out = self.pieces[p]
        for copy in self.third(p):
            copy.wait_recv()

        def body(i, _):
            at = i * 32
            total = come2[pl.ds(at, 32), :].astype(F32)
            for k in range(1, self.n_dp):
                total = total + come3[pl.ds((k - 1) * self.block + at, 32), :].astype(F32)
            out[pl.ds(at, 32), :] = total
            return 0

        lax.fori_loop(0, self.block // 32, body, 0, unroll=True)

    def sent(self, p):
        self.second(p).wait_send()
        for copy in self.third(p):
            copy.wait_send()


def add_rows(out, out_at, other, other_at, count):
    def body(i, _):
        at = i * 32
        out[pl.ds(out_at + at, 32), :] = out[pl.ds(out_at + at, 32), :] + other[pl.ds(other_at + at, 32), :]
        return 0

    lax.fori_loop(0, count // 32, body, 0, unroll=4)


def close_kernel(n_row, n_dp, n_col, sources, pieces, has_gn, fused, *refs):
    refs = list(refs)
    take = lambda count: [refs.pop(0) for _ in range(count)]
    lefts = take(1 + max(left for left, _, _ in sources))
    if fused:
        nc, hb, n_late = fused
        lengths_ref, = take(1)
        rows_given = take(3)
    else:
        gbd, = take(1)
        rows_given = take(4)
    if has_gn:
        gain8, rstd8 = take(2)
    else:
        stat, gain_row = take(2)
    later_given = take(n_late if fused else 2 + len(sources) - 3 + (5 if has_gn else 0))
    outs = take(len(sources))
    state_out, small_out, stat_out = take(3)
    if has_gn:
        grad_in, = take(1)
    come1, come2, come3 = take(len(sources)), take(len(sources)), take(len(sources))
    grad_slots, = take(1)
    later_held = take(len(later_given))
    small_a, small_b, small_c, state_a, state_b = take(5)
    sems_grad, sems_small, sems_state, sems_other, sems_local, small = take(6)
    if has_gn:
        gn_sum, gn, gn_come, gain, gsum, stat = take(6)
    if fused:
        gbd, gbctaps, gbclast, rim_bc, rims, gnext, tapsum, bctaps, ends_at, sems_rim = take(10)
        rows_given = rows_given[:2] + [gbctaps] + rows_given[2:]

    loads = [pltpu.make_async_copy(source, held, sems_local.at[k]) for k, (source, held) in enumerate(zip(later_given, later_held))]
    for load in loads:
        load.start()
    loaded = set()

    def held(k):
        if k not in loaded:
            loads[k].wait()
            loaded.add(k)
        return later_held[k]

    row, dp, col = lax.axis_index("row"), lax.axis_index("dp"), lax.axis_index("col")
    dps = [lax.rem(dp + k, n_dp) for k in range(n_dp)]
    cols = [lax.rem(col + k, n_col) for k in range(n_col)]
    rows = lefts[0].shape[0]
    half, quarter = rows // 2, rows // 4
    block = quarter // n_dp
    count = len(pieces)
    slots = grad_slots.shape[0]
    views = []
    for p, (a, at, width) in enumerate(pieces):
        columns, mine = pl.ds(at, width), grad_slots.at[p % slots, :, pl.ds(0, width)]
        views.append((mine.at[pl.ds(0, half)], mine.at[pl.ds(half, half)], come1[a].at[:, columns], come2[a].at[:, columns],
                      come3[a].at[:, columns], outs[a].at[:, columns]))
    sums = RowSums(n_dp, views, sems_grad)
    ahead, behind = lax.rem(row + 1, n_row), lax.rem(row + n_row - 1, n_row)
    meet(sums.partners() + [("col", c) for c in cols[1:]] + ([("row", ahead), ("row", behind)] if fused else []))
    started = []

    def start(copy):
        copy.start()
        started.append(copy)
        return copy

    def make(p):
        a, at, width = pieces[p]
        left, first_row, right = sources[a]
        if p >= slots:
            sums.first(p - slots).wait_send()
        right = gbd if right is None else held(right)
        value = right[first_row + at : min(first_row + at + width, right.shape[0]), :]
        if value.shape[0] < width:
            value = jnp.concatenate([value, jnp.zeros((width - value.shape[0], value.shape[1]), BF16)], 0)
        for part in range(2):
            rows_here = slice(part * half, (part + 1) * half)
            grad_slots[p % slots, rows_here, :width] = nt(lefts[left][rows_here, :], value).astype(BF16)
            if part == 0:
                sums.pair(p)

    group = lambda r: pl.ds(pl.multiple_of(r * (n_dp * block), 16), n_dp * block)
    here = pl.ds(pl.multiple_of((row * n_dp + dp) * block, 16), block)
    n0 = n_col - 1
    n1 = n0 + n_dp - 1
    later = {"others": []}

    def send_rim():
        later["rim"] = start(far(held(7), rims.at[pl.ds(0, held(7).shape[0])], sems_rim, 0, "row", behind))

    def add_rim(target, last, at, count):
        tokens = target.shape[1]
        come = jnp.where(row < n_row - 1, rims[at : at + count, :].astype(F32), 0.0)
        target[:count, tokens - Q :] = (last[...] + come).astype(BF16)

    def take_rim():
        later["rim"].wait_recv()
        add_rim(held(0), held(8), 0, held(8).shape[0])

    def state_back():
        bc, ubc, bcin, bctaps8, gscores, gbct, gdt = (held(k) for k in range(9, 16))
        state_kernel(nc, lengths_ref, bc, ubc, bcin, bctaps8, gscores, gbct, gbd, gbclast, rim_bc, gbctaps, gnext, tapsum, bctaps, ends_at)
        channels = held(8).shape[0]
        later["rim_bc"] = start(far(rim_bc, rims.at[pl.ds(channels, 2 * STATE)], sems_rim, 1, "row", behind))
        steps = [gdt[n, :hb, :] for n in range(gdt.shape[0])]
        rest = gbd.shape[0] - 2 * STATE - hb * gdt.shape[0]
        gbd[2 * STATE :, :] = jnp.concatenate(steps + [jnp.zeros((rest, gdt.shape[2]), F32)], 0).astype(BF16)

    def take_rim_bc():
        later["rim_bc"].wait_recv()
        add_rim(gbd, gbclast, held(8).shape[0], 2 * STATE)

    def product(place, which):
        value, w4 = held(which), held(2 + which)
        weights = lambda w4: jnp.concatenate([w4[place * (n_row // 2) + k] for k in range(n_row // 2)], 1)
        part = tn(weights(w4), value[...])
        if which:
            gn_sum[...] = part
        else:
            bd4 = held(4)
            gn_sum[...] += part + tn(weights(bd4), gbd[: bd4.shape[1], :])

    def prepare(k, place):
        hx = held(5)
        width = gn_sum.shape[0]
        rstd = rstd8[0:1, :]

        def body(i, total):
            at = pl.ds(i * 16, 16)
            there = pl.ds(pl.multiple_of(place * width + i * 16, 16), 16)
            pushed = gn_sum[at, :]
            if k == 0:
                gn[at, :] = pushed.astype(BF16)
            product = hx[there, Q:].astype(F32) * pushed
            scaled = product * rstd
            summed = scaled[:, :128]
            for tile in range(1, scaled.shape[1] // 128):
                summed = summed + scaled[:, tile * 128 : (tile + 1) * 128]
            gsum[at, :] = summed
            product = product * gain[0, there, 0:1]
            return total + product[:8] + product[8:]

        total = lax.fori_loop(0, width // 16, body, jnp.zeros((8, rstd.shape[1]), F32), unroll=2)
        total = rstd * total_rows(total)
        stat[...] = total if k == 0 else stat[...] + total
        small[6:7, pl.ds(pl.multiple_of(place * width, 128), width)] = lane_sums(gsum[...])[0:1]

    def begin_rows():
        channels = rows_given[0].shape[1]
        small[0 : CONV + 1, :channels] = rows_given[0][0 : CONV + 1, :]
        small[CONV + 1 : CONV + 2, :channels] = rows_given[1][0:1, :]
        small[7:8, : rows_given[2].shape[1]] = rows_given[2][0:1, :]
        for k in range(3):
            small[8:9, k * 128 : (k + 1) * 128] = rows_given[3][k : k + 1, :]

    def begin():
        small[...] = jnp.zeros_like(small)
        if has_gn:
            spread(gain8, gain)
        else:
            small[6:7, : gain_row.shape[1]] = gain_row[...]
        if not fused:
            begin_rows()

    def send_norm():
        if fused:
            begin()
        prepare(0, 1 - col)
        later["others"].append(start(far(gn, gn_come, sems_other, 0, "col", cols[1])))

    def send_small():
        if fused:
            begin_rows()
        if has_gn:
            prepare(1, col)
        later["small1"] = start(far(small, small_a.at[0], sems_small, 0, "row", row ^ 1))
        later["others"] += [start(far(stat, stat_out.at[col], sems_other, k, "col", cols[k])) for k in range(1, n_col)]
        stat_out[col] = stat[...]

    def small_pair():
        later["small1"].wait_recv()
        small_a[1] = small[...] + small_a[0]
        later["small2"] = start(far(small_a.at[1], small_b.at[0], sems_small, 1, "row", row ^ 2))

    def small_dp():
        later["small2"].wait_recv()
        small_b[1] = small_a[1] + small_b[0]
        later["small3"] = [start(far(small_b.at[1], small_c.at[k], sems_small, 1 + k, "dp", dps[k])) for k in range(1, n_dp)]

    def small_col():
        for copy in later["small3"]:
            copy.wait_recv()
        total = small_b[1]
        for k in range(1, n_dp):
            total = total + small_c[k]
        small_out[col] = total
        later["small4"] = [start(far(small_out.at[col], small_out.at[col], sems_small, n_dp + k, "col", cols[k])) for k in range(1, n_col)]

    def state_col():
        state_a[0] = outs[0][:, : state_a.shape[2]]
        later["state1"] = [start(far(state_a.at[0], state_a.at[k], sems_state, k - 1, "col", cols[k])) for k in range(1, n_col)]

    def state_dp():
        for copy in later["state1"]:
            copy.wait_recv()
        total = state_a[0]
        for k in range(1, n_col):
            total = total + state_a[k]
        state_b[...] = total.astype(state_b.dtype)
        state_out[here, :] = state_b[...]
        later["state2"] = [start(far(state_b, state_out.at[here], sems_state, n0 + k - 1, "dp", dps[k])) for k in range(1, n_dp)]

    def state_row():
        for copy in later["state2"]:
            copy.wait_recv()
        later["state3"] = start(far(state_out.at[group(row)], state_out.at[group(row)], sems_state, n1, "row", row ^ 2))

    def state_pair():
        later["state3"].wait_recv()
        later["state4"] = [start(far(state_out.at[group(r)], state_out.at[group(r)], sems_state, n1 + 1 + k, "row", row ^ 1))
                           for k, r in enumerate((row, row ^ 2))]

    def norm_back():
        for copy in later["others"]:
            copy.wait_recv()
        if not has_gn:
            return
        hx, grad_out = held(5), held(6)
        rstd = rstd8[0:1, :]
        total = stat_out[0]
        for k in range(1, n_col):
            total = total + stat_out[k]
        own = gn_sum.shape[0]
        width = n_col * own
        pull = (rstd * rstd) * (total / width)

        def body(i, _):
            at = pl.ds(i * 16, 16)
            there = pl.ds(pl.multiple_of(col * own + i * 16, 16), 16)
            pushed = gn_sum[at, :] + gn_come[at, :].astype(F32)
            grad_in[at, :] = (grad_out[at, :].astype(F32) + (rstd * gain[0, there, 0:1]) * pushed
                              - hx[there, Q:].astype(F32) * pull).astype(BF16)
            return 0

        lax.fori_loop(0, own // 16, body, 0, unroll=2)

    ahead_of = {}
    if fused:
        ahead_of = {4: [take_rim_bc], 6: [take_rim]}
        extra = {0: [send_rim], 1: [state_back], 3: [lambda: product(1 - col, 1)], 7: [lambda: product(1 - col, 0), send_norm],
                 8: [lambda: product(col, 1)], 9: [state_col], 10: [lambda: product(col, 0), send_small], 11: [state_dp, small_pair],
                 12: [state_row, small_dp], 13: [state_pair, small_col], 15: [norm_back]}
    elif has_gn:
        extra = {1: [lambda: product(1 - col, 1)], 2: [lambda: product(1 - col, 0), send_norm], 4: [lambda: product(col, 1)],
                 6: [lambda: product(col, 0), send_small], 7: [state_col], 8: [small_pair], 9: [state_dp], 10: [small_dp], 11: [state_row],
                 12: [small_col], 13: [state_pair, norm_back]}
    else:
        extra = {1: [send_small], 3: [small_pair], 4: [small_dp], 5: [small_col], 7: [state_col], 8: [state_dp], 9: [state_row],
                 10: [state_pair], 11: [norm_back]}
    for step in extra.get(0, ()):
        step()
    make(0)
    if not fused:
        begin()
    for t in range(1, max(count + 6, 16)):
        if 0 <= t - 1 < count:
            sums.across(t - 1)
        for step in ahead_of.get(t, ()):
            step()
        if t < count:
            make(t)
        if 0 <= t - 3 < count:
            sums.along(t - 3)
        if 0 <= t - 5 < count:
            sums.finish(t - 5)
        for step in extra.get(t, ()):
            step()
    for copy in later["small4"] + later["state4"]:
        copy.wait_recv()
    for k in range(len(loads)):
        held(k)
    for copy in started:
        copy.wait_send()
    for p in range(count):
        if p + slots >= count:
            sums.first(p).wait_send()
        sums.sent(p)


def close(sources, pieces, lefts, gbd, given, gn, plain, later, fused=()):
    n_row, n_dp, n_col = (lax.axis_size(axis) for axis in ("row", "dp", "col"))
    assert n_row == 4
    rows, tokens = lefts[0].shape
    widths = [max(at + width for a, at, width in pieces if a == k) for k in range(len(sources))]
    half, quarter, block = rows // 2, rows // 4, rows // 4 // n_dp
    vmem, anywhere = pl.BlockSpec(memory_space=pltpu.VMEM), pl.BlockSpec(memory_space=pl.ANY)
    has_gn = gn is not None
    here = rows // n_col
    given = list(given)
    small = (16, max(rows, given[1 if fused else 0].shape[1]))
    channels = given[1].shape[1]
    extra = list(gn) if has_gn else list(plain)
    out = pl.pallas_call(
        functools.partial(close_kernel, n_row, n_dp, n_col, sources, pieces, has_gn, fused),
        in_specs=[vmem] * len(lefts) + ([SMEM] + [vmem] * 3 if fused else [vmem] * 5) + [vmem] * len(extra) + [anywhere] * len(later),
        out_specs=[vmem] * (len(sources) + 3 + has_gn),
        out_shape=[shape(F32, block, width) for width in widths]
        + [shape(BF16, rows, 2 * STATE), shape(F32, n_col, *small), shape(F32, n_col, 1, tokens)] + [shape(BF16, here, tokens)] * has_gn,
        scratch_shapes=[pltpu.VMEM((half, width), BF16) for width in widths] + [pltpu.VMEM((quarter, width), BF16) for width in widths]
        + [pltpu.VMEM(((n_dp - 1) * block, width), BF16) for width in widths]
        + [pltpu.VMEM((min(2 if fused else 4, len(pieces)), rows, max(width for _, _, width in pieces)), BF16)]
        + [pltpu.VMEM(value.shape, value.dtype) for value in later]
        + [pltpu.VMEM((2,) + small, F32), pltpu.VMEM((2,) + small, F32), pltpu.VMEM((n_dp,) + small, F32),
           pltpu.VMEM((n_col, block, 2 * STATE), F32), pltpu.VMEM((block, 2 * STATE), BF16),
           pltpu.SemaphoreType.DMA((2, len(pieces) * (n_dp + 1))), pltpu.SemaphoreType.DMA((2, n_dp + n_col)),
           pltpu.SemaphoreType.DMA((2, n_col + n_dp + 2)), pltpu.SemaphoreType.DMA((2, n_col)),
           pltpu.SemaphoreType.DMA((len(later),)), pltpu.VMEM(small, F32)]
        + ([pltpu.VMEM((here, tokens), F32), pltpu.VMEM((here, tokens), BF16), pltpu.VMEM((here, tokens), BF16), pltpu.VMEM((1, rows, 128), F32),
            pltpu.VMEM((here, 128), F32), pltpu.VMEM((1, tokens), F32)] if has_gn else [])
        + ([pltpu.VMEM((widths[0], tokens), BF16), pltpu.VMEM((8, (CONV + 1) * 2 * STATE), F32), pltpu.VMEM((2 * STATE, Q), F32),
            pltpu.VMEM((2 * STATE, Q), BF16), pltpu.VMEM((channels + 2 * STATE, Q), BF16), pltpu.VMEM((2 * STATE, Q), F32),
            pltpu.VMEM((CONV + 1, 2 * STATE, Q), F32), pltpu.VMEM((CONV + 1, 2 * STATE, Q), F32), pltpu.VMEM((2, 2 * STATE, Q), F32),
            pltpu.SemaphoreType.DMA((2, 2))] if fused else []),
        compiler_params=pltpu.CompilerParams(vmem_limit_bytes=60 * 1024 * 1024, collective_id=1, has_side_effects=True),
        cost_estimate=pl.CostEstimate(flops=10**6, bytes_accessed=10**8, transcendentals=0),
        name="close",
    )(*lefts, *([] if fused else [gbd]), *given, *extra, *later)
    count = len(sources)
    return out[:count], out[count], out[count + 1], out[count + 2], out[count + 3] if has_gn else None


def last_kernel(n_row, n_dp, n_col, heads, n_z, bd, x, state, small, *refs):
    refs = list(refs)
    take = lambda count: [refs.pop(0) for _ in range(count)]
    z_parts = take(n_z)
    norm_gain, inner, state_out, step, taps, bias, bc_taps, bc_bias, step_bias, decay, skip, gate = refs
    block = x.shape[0]
    at, channels = 0, inner.shape[2]
    for part in z_parts:
        count = min(part.shape[1], channels - at)
        inner[0, :, at : at + count] = part[:, :count]
        at += count
    inner[1] = x[:, :channels]
    for r in range(n_row):
        for d in range(n_dp):
            state_out[(d * n_row + r) * block : (d * n_row + r + 1) * block, :] = state[
                (r * n_dp + d) * block : (r * n_dp + d + 1) * block, :].astype(F32)
    step[...] = jnp.transpose(bd[:, 2 * STATE :])[:heads]
    by_col = lambda k: jnp.concatenate([small[c, k : k + 1, :channels] for c in range(n_col)], 1)
    for k in range(CONV):
        taps[k : k + 1, :] = by_col(CONV - 1 - k)
    bias[...] = by_col(CONV)
    gate[...] = by_col(CONV + 1)
    over = lambda k, at, count: sum(small[c, k : k + 1, at : at + count] for c in range(n_col))
    norm_gain[...] = over(6, 0, norm_gain.shape[1])
    for k in range(CONV):
        bc_taps[k : k + 1, :] = over(7, (CONV - 1 - k) * 2 * STATE, 2 * STATE)
    bc_bias[...] = over(7, CONV * 2 * STATE, 2 * STATE)
    for k, target in enumerate((step_bias, decay, skip)):
        target[...] = over(8, k * 128, 128)[:, : target.shape[1]]


def last(bd, x, state, small, z_parts, heads, channels):
    n_row, n_dp, n_col = (lax.axis_size(axis) for axis in ("row", "dp", "col"))
    block = x.shape[0]
    width = state.shape[0]
    row = lambda count: shape(F32, 1, count)
    return pl.pallas_call(
        functools.partial(last_kernel, n_row, n_dp, n_col, heads, len(z_parts)),
        out_shape=[row(width), shape(F32, 2, block, channels), shape(F32, width, 2 * STATE), shape(F32, heads, block),
                   shape(F32, CONV, n_col * channels), row(n_col * channels), shape(F32, CONV, 2 * STATE), row(2 * STATE),
                   row(n_col * heads), row(n_col * heads), row(n_col * heads), row(n_col * channels)],
        compiler_params=params(),
        cost_estimate=pl.CostEstimate(flops=10**6, bytes_accessed=10**7, transcendentals=0),
        name="last",
    )(bd, x, state, small, *z_parts)


def open_kernel(n_row, n_col, parts, hidden, inner, state_w, step_w, hx, x4, z_w, bd4, sems):
    row, col = lax.axis_index("row"), lax.axis_index("col")
    cols = [lax.rem(col + k, n_col) for k in range(n_col)]
    ahead, behind = lax.rem(row + 1, n_row), lax.rem(row + n_row - 1, n_row)
    partners = [("row", row ^ 1), ("row", row ^ 2), ("row", ahead), ("row", behind)] + [("col", c) for c in cols[1:]]
    meet(partners)
    width, tokens = hidden.shape
    each = inner.shape[0] // parts
    heads = step_w.shape[0]
    mine = pl.ds(pl.multiple_of(col * width, 16), width)
    counter = [0]
    started = []

    def start(source, target, axis, place):
        copy = far(source, target, sems, counter[0], axis, place)
        counter[0] += 1
        copy.start()
        started.append(copy)
        return copy

    rim = start(hidden.at[:, pl.ds(tokens - Q, Q)], hx.at[mine, pl.ds(0, Q)], "row", ahead)
    wide = [start(hidden, hx.at[mine, pl.ds(Q, tokens)], "col", cols[k]) for k in range(1, n_col)]
    part = lambda p: pl.ds(p * each, each)
    send = lambda p: start(x4.at[row, part(p)], x4.at[row, part(p)], "row", row ^ 2)

    def split(p):
        def body(i, _):
            at = pl.ds(p * each + i * 16, 16)
            x4[row, at, :] = inner[at, 1, :]
            z_w[at, :] = inner[at, 0, :]
            return 0

        lax.fori_loop(0, each // 16, body, 0, unroll=2)

    split(0)
    over = [send(0)]
    bd4[row, : 2 * STATE, :] = jnp.transpose(state_w[...].astype(F32)).astype(BF16)
    rest = bd4.shape[1] - 2 * STATE - heads
    bd4[row, 2 * STATE :, :] = jnp.concatenate([step_w[...], jnp.zeros((rest, step_w.shape[1]), BF16)], 0)
    bd_over = start(bd4.at[row], bd4.at[row], "row", row ^ 2)
    near = [start(bd4.at[row], bd4.at[row], "row", row ^ 1)]
    for p in range(1, parts):
        split(p)
        if p == 1:
            over.append(send(1))
    near.append(start(x4.at[row], x4.at[row], "row", row ^ 1))

    def keep_hidden(i, _):
        hx[pl.ds(pl.multiple_of(col * width + i * 16, 16), 16), pl.ds(Q, tokens)] = hidden[pl.ds(i * 16, 16), :]
        return 0

    lax.fori_loop(0, width // 16, keep_hidden, 0)
    rim.wait_recv()
    wide += [start(hx.at[mine, pl.ds(0, Q)], hx.at[mine, pl.ds(0, Q)], "col", cols[k]) for k in range(1, n_col)]
    bd_over.wait_recv()
    near.append(start(bd4.at[row ^ 2], bd4.at[row ^ 2], "row", row ^ 1))
    waited = []
    for p in range(parts):
        over[p].wait_recv()
        near.append(start(x4.at[row ^ 2, part(p)], x4.at[row ^ 2, part(p)], "row", row ^ 1))
        if p + 2 < parts:
            over[p].wait_send()
            waited.append(id(over[p]))
            over.append(send(p + 2))
    for copy in wide + near:
        copy.wait_recv()
    for copy in started:
        if id(copy) not in waited:
            copy.wait_send()


def open_up(hidden, inner, state_w, step_w):
    n_row, n_col = lax.axis_size("row"), lax.axis_size("col")
    assert n_row == 4
    channels, _, block = inner.shape
    heads = step_w.shape[0]
    parts = 4 if channels % 64 == 0 else 1
    vmem = pl.BlockSpec(memory_space=pltpu.VMEM)
    return pl.pallas_call(
        functools.partial(open_kernel, n_row, n_col, parts),
        in_specs=[vmem] * 4,
        out_specs=[vmem] * 4,
        out_shape=[shape(BF16, hidden.shape[0] * n_col, Q + hidden.shape[1]), shape(BF16, n_row, channels, block), shape(BF16, channels, block),
                   shape(BF16, n_row, 2 * STATE + heads + -heads % 32, block)],
        scratch_shapes=[pltpu.SemaphoreType.DMA((2, 5 + 2 * parts + 2 * (n_col - 1)))],
        compiler_params=pltpu.CompilerParams(vmem_limit_bytes=VMEM_LIMIT, collective_id=2, has_side_effects=True),
        cost_estimate=pl.CostEstimate(flops=0, bytes_accessed=10**8, transcendentals=0),
        name="open",
    )(hidden, inner, state_w, step_w)


def joined(w4_ref):
    return jnp.concatenate([w4_ref[j] for j in range(w4_ref.shape[0])], 1)


def by_distance(n_row, n_dp):
    row, dp = lax.axis_index("row"), lax.axis_index("dp")
    return [lax.rem(dp + k, n_dp) * n_row + (row ^ place) for place in sum_stages(n_row)[0] for k in range(n_dp)]


def put_by_distance(n_row, n_dp, source, target, skip):
    each = target.shape[0] // (n_row * n_dp)
    for k, place in enumerate(by_distance(n_row, n_dp)):
        target[k * each : (k + 1) * each, :] = source[pl.ds(pl.multiple_of(place * each, 32), each), skip:]


def project_kernel(n_row, n_dp, hb, lengths_ref, hx_ref, gain8_ref, x4_ref, bd4_ref, normed_ref, by_ref, rstd_ref, live_ref, xin_ref, bd_ref, dt_ref, gain_ref):
    @pl.when(pl.program_id(0) == 0)
    def _():
        spread(gain8_ref, gain_ref)
        width, count = hx_ref.shape

        def square(i, total):
            v = hx_ref[pl.ds(i * 16, 16), :].astype(F32)
            v = v * v
            return total + v[:8] + v[8:]

        total = lax.fori_loop(0, width // 16, square, jnp.zeros((8, count), F32), unroll=4)
        rstd = lax.rsqrt(jnp.sum(total, 0, keepdims=True) / width + EPS)
        rstd_ref[...] = jnp.broadcast_to(rstd[:, Q:], rstd_ref.shape)
        base, ends = scalars(lengths_ref, count - Q)
        live_ref[...] = (base + iota(live_ref.shape, 1) < ends[-1]).astype(F32)

        def norm(i, _):
            at = pl.ds(i * 16, 16)
            normed_ref[at, :] = (hx_ref[at, :].astype(F32) * rstd * gain_ref[0, at, 0:1]).astype(BF16)
            return 0

        lax.fori_loop(0, width // 16, norm, 0, unroll=4)
        put_by_distance(n_row, n_dp, normed_ref, by_ref, Q)
        bd = nn(joined(bd4_ref), normed_ref[...])
        bd_ref[...] = bd[: 2 * STATE]
        dt_ref[...] = jnp.zeros_like(dt_ref)
        for n in range(dt_ref.shape[0]):
            dt_ref[n, :hb, :] = bd[2 * STATE + n * hb : 2 * STATE + (n + 1) * hb, Q:]

    xin_ref[...] = nn(joined(x4_ref), normed_ref[...])


def second_kernel(n_row, n_dp, steps, hb, given, *refs):
    refs = list(refs)
    take = lambda count: [refs.pop(0) for _ in range(count)]
    far_refs = [take(2), take(2)]
    near_refs = [take(2), take(2)]
    normed, = take(1)
    grads = take(2 if given else 1)
    live, final, keep = take(3)
    z4, z, out4, gg, state_in, grad_by = take(6)
    whole_grad, come, came, kept, sems, sems_state = take(6)
    row, col = lax.axis_index("row"), lax.axis_index("col")
    n = pl.program_id(0)
    each = z4.shape[1]

    def piece(side, which, s):
        rows = pl.ds(s * each, each)
        return far(far_refs[side][which].at[rows], come.at[side, which, rows], sems, (side * 2 + which) * steps + s, "row", row ^ 1)

    def pieces(at):
        return [piece(at // steps, which, at % steps) for which in range(2)]

    def states():
        copies = []
        for k in range(1, n_row):
            there = lax.rem(row + k, n_row)
            copies.append(far(final, came.at[k - 1], sems_state, 2 * k - 2, "row", there))
            copies.append(far(keep, kept.at[k - 1], sems_state, 2 * k - 1, "row", there))
        return copies

    @pl.when(n == 0)
    def _():
        meet([("row", lax.rem(row + k, n_row)) for k in range(1, n_row)])
        for copy in states() + pieces(0) + pieces(1):
            copy.start()

    @pl.when(n == 0)
    def _():
        width = grads[0].shape[0]
        for place, source in zip((col, 1 - col) if given else (0,), grads):
            def body(i, _):
                at = pl.ds(pl.multiple_of(place * width + i * 16, 16), 16)
                whole_grad[at, :] = (source[pl.ds(i * 16, 16), :].astype(F32) * live[0:1, :]).astype(BF16)
                return 0

            lax.fori_loop(0, width // 16, body, 0, unroll=4)
        put_by_distance(n_row, n_dp, whole_grad, grad_by, 0)

    for at in range(2 * steps):
        @pl.when(n == at)
        def _():
            side = at // steps
            if at + 2 < 2 * steps:
                for copy in pieces(at + 2):
                    copy.start()
            for copy in pieces(at):
                copy.wait_recv()
            rows = slice(at % steps * each, (at % steps + 1) * each)
            w4, out = ((z4, z), (out4, gg))[side]
            w4[row] = near_refs[side][0][...]
            w4[row ^ 2] = near_refs[side][1][...]
            w4[row ^ 1] = come[side, 0, rows, :]
            w4[row ^ 3] = come[side, 1, rows, :]
            value = normed[:, Q:] if side == 0 else whole_grad[...]
            out[...] = nn(joined(w4), value)

    @pl.when(n == 2 * steps - 1)
    def _():
        for copy in states():
            copy.wait_recv()
        for head in range(final.shape[0] // HEADDIM):
            at = slice(head * HEADDIM, (head + 1) * HEADDIM)
            total, decay = None, None
            for k in range(1, n_row):
                part = jnp.where(row >= k, came[k - 1, at, :].astype(F32), 0.0)
                total = part if total is None else total + decay * part
                passing = kept[k - 1, head // hb, head % hb : head % hb + 1, :]
                decay = passing if decay is None else decay * passing
            state_in[at, :] = total
        for copy in states():
            copy.wait_send()
        for at in range(2 * steps):
            for copy in pieces(at):
                copy.wait_send()


def placed(value, index, count):
    out = jnp.zeros((count,) + value.shape, F32)
    return lax.dynamic_update_slice(out, value[None], (index,) + (0,) * value.ndim)


def turned(value, axis):
    return lax.all_gather(value, axis, axis=0, tiled=True)


def per_device(hidden_in, grad_out, lengths, norm_gain, inner_proj, state_proj, step_proj, conv_inner, conv_inner_bias,
               conv_state, conv_state_bias, step_bias, decay_log, skip_gain, gate_gain, out_proj):
    cols_here, rows = hidden_in.shape
    ncols = lax.axis_size("col")
    nrow = lax.axis_size("row")
    width = cols_here * ncols
    inner = inner_proj.shape[0]
    heads = step_proj.shape[0]
    col_index = lax.axis_index("col")
    nc = rows // Q
    hb = max(k for k in (1, 2, 3, 4) if heads % k == 0)
    nb = heads // hb
    bh = hb * HEADDIM


    gain_full = norm_gain.astype(F32)
    gain8 = jnp.broadcast_to(gain_full[None], (8, width))
    hx, x4, z_w, bd4 = open_up(hidden_in, inner_proj, state_proj, step_proj)
    out_w, grad_now, hx = lax.optimization_barrier((out_proj, grad_out, hx))
    z_far = swapped(z_w, "row", 2)
    z_far, out_w = lax.optimization_barrier((z_far, out_w))
    out_far = swapped(out_w, "row", 2)
    if ncols == 2:
        grads = [grad_now, swapped(grad_now, "col", 1)]
    else:
        grads = [lax.all_gather(grad_now, "col", axis=0, tiled=True)]

    bm = 2 * bh if nb % 2 == 0 else bh
    part4 = pl.BlockSpec((nrow, bm, width // nrow), lambda n: (0, n, 0))
    ext = rows + Q
    normed_ext, normed_by, rstd8, live8, xin, bdin, dt = pl.pallas_call(
        functools.partial(project_kernel, nrow, lax.axis_size("dp"), hb),
        grid=(inner // bm,),
        in_specs=[SMEM, whole(width, ext), whole(8, width), part4, whole(*bd4.shape)],
        out_specs=[whole(width, ext), whole(width, rows), whole(8, rows), whole(8, rows), pl.BlockSpec((bm, ext), lambda n: (n, 0)), whole(2 * STATE, ext), whole(nb, 8, rows)],
        out_shape=[shape(BF16, width, ext), shape(BF16, width, rows), shape(F32, 8, rows), shape(F32, 8, rows), shape(F32, inner, ext), shape(F32, 2 * STATE, ext), shape(F32, nb, 8, rows)],
        compiler_params=params(),
        scratch_shapes=[pltpu.VMEM((1, width, Q), F32)],
        cost_estimate=pl.CostEstimate(flops=8 * 10**9, bytes_accessed=20 * 10**6, transcendentals=0),
        name="project",
    )(lengths, hx, gain8, x4, bd4)
    rstd_in = rstd8[:1]
    by_head = jnp.pad(jnp.stack([step_bias, decay_log, skip_gain]), ((0, 5), (0, 128 - heads)))

    def taps_of(taps, bias):
        return jnp.pad(jnp.concatenate([taps, bias[None]], axis=0).astype(F32), ((0, 7 - CONV), (0, 0)))

    taps = taps_of(conv_inner, conv_inner_bias)
    bctaps = taps_of(conv_state, conv_state_bias)
    gate = jnp.broadcast_to(gate_gain.astype(F32)[None], (8, inner))

    tok = pl.BlockSpec((bh, rows), lambda n: (n, 0))
    tok_ext = pl.BlockSpec((bh, rows + Q), lambda n: (n, 0))
    eight = pl.BlockSpec((8, bh), lambda n: (0, n))
    bc_ext = pl.BlockSpec((2 * STATE, rows + Q), lambda n: (0, 0))
    state_spec = pl.BlockSpec((bh, STATE), lambda n: (n, 0))
    chunks = pl.BlockSpec((nc, bh, STATE), lambda n: (0, n, 0))
    rows_spec = pl.BlockSpec((1, 6, 8, rows), lambda n: (n, 0, 0, 0))
    head_tok = pl.BlockSpec((1, 8, rows), lambda n: (n, 0, 0))
    head_q = pl.BlockSpec((1, 8, Q), lambda n: (n, 0, 0))
    head8 = pl.BlockSpec((1, 8, 8), lambda n: (n, 0, 0))

    u, ubc, bc, rowpack, scores, y_in, fresh, final, keep, hpar = pl.pallas_call(
        functools.partial(enter_kernel, nc, hb),
        grid=(nb,),
        in_specs=[SMEM, tok_ext, bc_ext, whole(nb, 8, rows), whole(8, 128), eight, whole(8, 2 * STATE),
                  pl.BlockSpec(memory_space=pl.ANY)],
        out_specs=[tok, whole(2 * STATE, rows), whole(2 * STATE, rows), whole(nb, 6, 8, rows), whole(nc, Q, Q), tok, chunks,
                   state_spec, whole(nb, 8, Q), whole(nb, 8, 8)],
        out_shape=[shape(F32, inner, rows), shape(F32, 2 * STATE, rows), shape(F32, 2 * STATE, rows),
                   shape(F32, nb, 6, 8, rows), shape(F32, nc, Q, Q), shape(F32, inner, rows), shape(F32, nc, inner, STATE),
                   shape(BF16, inner, STATE), shape(F32, nb, 8, Q), shape(F32, nb, 8, 8)],
        scratch_shapes=[pltpu.VMEM((bh, STATE), F32), pltpu.VMEM((CONV + 1, bh, Q), F32), pltpu.VMEM((CONV + 1, 2 * STATE, Q), F32)],
        compiler_params=params(),
        cost_estimate=pl.CostEstimate(flops=3 * 10**10, bytes_accessed=40 * 10**6, transcendentals=0),
        name="enter",
    )(lengths, xin, bdin, dt, by_head, taps, bctaps, z_far)

    steps = inner // bm
    block = pl.BlockSpec((bm, width // nrow), lambda n: (jnp.minimum(n, steps - 1), 0))
    block_after = pl.BlockSpec((bm, width // nrow), lambda n: (jnp.maximum(n - steps, 0), 0))
    anywhere = pl.BlockSpec(memory_space=pl.ANY)
    second = pl.pallas_call(
        functools.partial(second_kernel, nrow, lax.axis_size("dp"), steps, hb, ncols == 2),
        grid=(2 * steps,),
        in_specs=[anywhere] * 4 + [block] * 2 + [block_after] * 2 + [whole(width, ext)] + [whole(*value.shape) for value in grads]
        + [whole(8, rows), whole(inner, STATE), whole(nb, 8, Q)],
        out_specs=[pl.BlockSpec((nrow, bm, width // nrow), lambda n: (0, jnp.minimum(n, steps - 1), 0)),
                   pl.BlockSpec((bm, rows), lambda n: (jnp.minimum(n, steps - 1), 0)),
                   pl.BlockSpec((nrow, bm, width // nrow), lambda n: (0, jnp.maximum(n - steps, 0), 0)),
                   pl.BlockSpec((bm, rows), lambda n: (jnp.maximum(n - steps, 0), 0)),
                   whole(inner, STATE), whole(width, rows)],
        out_shape=[shape(BF16, nrow, inner, width // nrow), shape(F32, inner, rows)] * 2 + [shape(F32, inner, STATE), shape(BF16, width, rows)],
        scratch_shapes=[pltpu.VMEM((width, rows), BF16), pltpu.VMEM((2, 2, inner, width // nrow), BF16), pltpu.VMEM((nrow - 1, inner, STATE), BF16),
                        pltpu.VMEM((nrow - 1, nb, 8, Q), F32), pltpu.SemaphoreType.DMA((2, 4 * steps)),
                        pltpu.SemaphoreType.DMA((2, 2 * (nrow - 1)))],
        compiler_params=pltpu.CompilerParams(vmem_limit_bytes=VMEM_LIMIT, collective_id=3, has_side_effects=True),
        cost_estimate=pl.CostEstimate(flops=10**10, bytes_accessed=30 * 10**6, transcendentals=0),
        name="second",
    )(z_w, z_far, out_w, out_far, z_w, z_far, out_w, out_far, normed_ext, *grads, live8, final, keep)
    z4, z, out4, grad_gated, state_in, grad_by = second

    y, states, stats = pl.pallas_call(
        functools.partial(across_kernel, nc, hb),
        grid=(nb,),
        in_specs=[tok, chunks, state_spec, whole(2 * STATE, rows), rows_spec, tok, tok, eight],
        out_specs=[tok, chunks, whole(2, 8, rows)],
        out_shape=[shape(F32, inner, rows), shape(F32, nc, inner, STATE), shape(F32, 2, 8, rows)],
        scratch_shapes=[pltpu.VMEM((bh, STATE), F32), pltpu.VMEM((1, bh, Q), F32)],
        compiler_params=params(),
        cost_estimate=pl.CostEstimate(flops=10**10, bytes_accessed=35 * 10**6, transcendentals=0),
        name="across",
    )(y_in, fresh, state_in, bc, rowpack, z, grad_gated, gate)

    sums = col_sum(jnp.sum(stats, axis=1))
    inner_width = inner * ncols
    rstd_gate = lax.rsqrt(sums[0] / inner_width + EPS)
    pull = rstd_gate * rstd_gate * rstd_gate * (sums[1] / inner_width)
    token_rows = jnp.concatenate([rstd_gate[None], pull[None], jnp.zeros((6, rows), F32)], axis=0)

    gated, grad_z, grad_y, adj, adj_first, ggate = pl.pallas_call(
        functools.partial(gate_kernel, nc, hb),
        grid=(nb,),
        in_specs=[tok, tok, tok, whole(8, rows), eight, whole(2 * STATE, rows), rows_spec],
        out_specs=[tok, tok, tok, chunks, state_spec, eight],
        out_shape=[shape(BF16, inner, rows), shape(BF16, inner, rows), shape(F32, inner, rows),
                   shape(F32, nc, inner, STATE), shape(BF16, inner, STATE), shape(F32, 8, inner)],
        scratch_shapes=[pltpu.VMEM((bh, STATE), F32), pltpu.VMEM((bh, Q), F32), pltpu.VMEM((1, bh, Q), F32)],
        compiler_params=params(),
        cost_estimate=pl.CostEstimate(flops=10**10, bytes_accessed=40 * 10**6, transcendentals=0),
        name="gate",
    )(y, z, grad_gated, token_rows, gate, bc, rowpack)

    adj_in = chained(adj_first, keep, hb, -1)
    def turned_product(w4, value):
        return lax.dot_general(w4, value, (((1,), (0,)), ((), ())), preferred_element_type=F32).reshape(-1, rows)

    def halves_of_features(products):
        return [sum(turned_product(lax.dynamic_slice_in_dim(w4, at * (nrow // 2), nrow // 2, 0), value) for w4, value in products)
                for at in (1 - col_index, col_index)]

    if ncols == 2:
        mixed_other, mixed = halves_of_features([(out4, gated)])
        mixed_come = swapped(mixed_other.astype(BF16), "col", 1)

    n_dp = lax.axis_size("dp")
    early, grads_early, first_z = {}, [], 0
    if nb >= 5 and inner % 768 == 0:
        first_z = inner // 3
        grads_early = [nt(grad_by, gated).astype(BF16), nt(normed_by, grad_z[:first_z]).astype(BF16)]
        each = inner // 6
        places = [(0, k * each, each) for k in range(6)] + [(1, k * each, each) for k in range(2)]
        early = {"pieces": places, "groups": [(2 * k, 2 * k + 1) for k in range(4)], "steps": nb}
    quarter = width // 4
    once = pl.Buffered(1)
    held = pl.BlockSpec(memory_space=pltpu.VMEM)
    back_out = pl.pallas_call(
        functools.partial(back_kernel, nc, hb, heads, early, n_dp),
        grid=(nb,),
        in_specs=[SMEM, tok, tok_ext, tok, tok, chunks, chunks, state_spec, whole(2 * STATE, rows), whole(nc, Q, Q), rows_spec, head8, eight]
        + [pl.BlockSpec(value.shape, lambda n: (0, 0), pipeline_mode=once) for value in grads_early],
        out_specs=[tok, pl.BlockSpec((bh, Q), lambda n: (n, 0)), pl.BlockSpec((bh, Q), lambda n: (n, 0)), eight, head_tok,
                   whole(nc, Q, Q), whole(2 * STATE, rows), whole(8, Q)] + [whole(quarter // n_dp, value.shape[1]) for value in grads_early],
        out_shape=[shape(BF16, inner, rows), shape(F32, inner, Q), shape(BF16, inner, Q), shape(F32, 8, inner), shape(F32, nb, 8, rows),
                   shape(F32, nc, Q, Q), shape(F32, 2 * STATE, rows), shape(F32, 8, Q)]
        + [shape(F32, quarter // n_dp, value.shape[1]) for value in grads_early],
        scratch_shapes=[pltpu.VMEM((bh, STATE), F32), pltpu.VMEM((bh, Q), F32), pltpu.VMEM((CONV + 1, bh, Q), F32),
                        pltpu.VMEM((5, nb, 8, rows), F32), pltpu.VMEM((CONV + 1, bh, Q), F32), pltpu.VMEM((2, bh, Q), F32)]
        + ([pltpu.VMEM((8, 2 * quarter, each), BF16), pltpu.VMEM((8, quarter, each), BF16),
            pltpu.VMEM((8, quarter // n_dp * (n_dp - 1), each), BF16), pltpu.SemaphoreType.DMA((2, 8 * (n_dp + 1)))] if early else []),
        compiler_params=pltpu.CompilerParams(vmem_limit_bytes=VMEM_LIMIT, collective_id=4, has_side_effects=True) if early else params(),
        cost_estimate=pl.CostEstimate(flops=6 * 10**10, bytes_accessed=50 * 10**6, transcendentals=0),
        name="back",
    )(lengths, u, xin, grad_y, y, states, adj, adj_in, bc, scores, rowpack, hpar, taps, *grads_early)
    gx, gx_last, rim_x, gtaps, gdt, gscores, gbct, hsum = back_out[:8]
    if ncols == 2:
        mixed_come, gx = lax.optimization_barrier((mixed_come, gx))

    if ncols == 2:
        mixed = mixed + mixed_come.astype(F32)
    else:
        mixed = lax.psum_scatter(turned_product(out4, gated).astype(BF16), "col", scatter_dimension=0, tiled=True).astype(F32)
    hidden_f = hidden_in.astype(F32)
    block_out = (hidden_f + live8[:1] * mixed).astype(BF16)

    small_width = -(-(2 * STATE + heads) // 128) * 128
    fused = ncols == 2 and bool(early)
    each = inner // 6 if inner % 768 == 0 else inner + -inner % 128
    sources = [(0, 0, None), (0, 0, 0), (0, first_z, 1)]
    pieces = [(0, 0, 2 * STATE), (0, 2 * STATE, small_width - 2 * STATE)]
    z_pieces = [(2, at, each) for at in range(0, inner - first_z, each)]
    x_pieces = [(1, at, each) for at in range(0, inner, each)]
    if inner % 768 == 0:
        x_pieces[-1:] = [(1, inner - each, each // 2), (1, inner - each // 2, each // 2)]
    pieces = z_pieces + pieces + x_pieces if fused else pieces + z_pieces + x_pieces
    gbd = None
    if not fused:
        vmem = pl.BlockSpec(memory_space=pltpu.VMEM)
        gbc, gbc_last, rim_bc, gbctaps = pl.pallas_call(
            functools.partial(state_kernel, nc),
            grid=(1,),
            out_shape=[shape(BF16, 2 * STATE, rows), shape(F32, 2 * STATE, Q), shape(BF16, 2 * STATE, Q),
                       shape(F32, 8, (CONV + 1) * 2 * STATE)],
            in_specs=[SMEM, vmem, vmem, bc_ext, vmem, vmem, vmem],
            out_specs=[vmem] * 4,
            scratch_shapes=[pltpu.VMEM((2 * STATE, Q), F32), pltpu.VMEM((CONV + 1, 2 * STATE, Q), F32),
                            pltpu.VMEM((CONV + 1, 2 * STATE, Q), F32), pltpu.VMEM((2, 2 * STATE, Q), F32)],
            compiler_params=params(),
            cost_estimate=pl.CostEstimate(flops=10**9, bytes_accessed=6 * 10**6, transcendentals=0),
            name="state",
        )(lengths, bc, ubc, bdin, bctaps, gscores, gbct)

        def last_tokens(value, last, rim):
            return lax.dynamic_update_slice(value, (last + rim.astype(F32)).astype(BF16), (0, rows - Q))

        back_x, back_bc = from_before(rim_x, -1), from_before(rim_bc, -1)
        gx = last_tokens(gx, gx_last, back_x)
        gbd = jnp.concatenate([last_tokens(gbc, gbc_last, back_bc), gdt[:, :hb].reshape(heads, rows).astype(BF16),
                               jnp.zeros((bd4.shape[1] - 2 * STATE - heads, rows), BF16)], axis=0)

        gbd_padded = jnp.pad(gbd, ((0, small_width - gbd.shape[0]), (0, 0)))
    lefts, later = [normed_by], [gx, grad_z]
    if ncols == 2:
        later += [x4, z4, bd4, hx, grad_out]
        gn_given, plain = (gain8, rstd8), None
        if fused:
            later += [rim_x, gx_last, bc, ubc, bdin, bctaps, gscores, gbct, gdt]
    else:
        grad_normed = turned_product(z4, grad_z) + turned_product(x4, gx) + turned_product(bd4, gbd)
        whole_rows = hx[:, Q:].astype(F32) * rstd_in
        gain_here = lax.dynamic_slice_in_dim(gain_full, col_index * cols_here, cols_here)[:, None]
        gn_given, plain = None, (jnp.sum(whole_rows * gain_full[:, None] * grad_normed, axis=0)[None], jnp.sum(whole_rows * grad_normed, axis=1)[None])
        gn_here = lax.psum_scatter(grad_normed.astype(BF16), "col", scatter_dimension=0, tiled=True).astype(F32)
    if not early:
        sources.append((1, 0, len(later)))
        lefts.append(grad_by)
        later.append(gated)
        pieces += [(3, at, each) for at in range(0, inner, each)]
    sums, state_out, small_out, stat_out, grad_in = close(
        sources, pieces, lefts, None if fused else gbd_padded, (lengths, gtaps, ggate, hsum) if fused else (gtaps, ggate, gbctaps, hsum),
        gn_given, plain, later, (nc, hb, len(later)) if fused else ())
    if ncols != 2:
        stat_total = jnp.sum(stat_out, axis=0)
        grad_in = (grad_out.astype(F32) + rstd_in * gain_here * gn_here - hidden_f * (rstd_in * rstd_in) * (stat_total / width)).astype(BF16)
    g_out = back_out[8] if early else sums[3][:, :inner]
    (g_norm_gain, g_inner, g_state, g_step, g_taps, g_bias, g_bc_taps, g_bc_bias, g_step_bias, g_decay, g_skip, g_gate) = last(
        sums[0], sums[1], state_out, small_out, [back_out[9], sums[2]] if early else [sums[2]], heads, inner)
    return (
        block_out,
        grad_in,
        g_norm_gain[0],
        jnp.transpose(g_inner, (2, 0, 1)),
        g_state,
        g_step,
        g_taps,
        g_bias[0],
        g_bc_taps,
        g_bc_bias[0],
        g_step_bias[0],
        g_decay[0],
        g_skip[0],
        g_gate[0],
        g_out.T,
    )


def solution(mesh):
    col, tokens, sums = P("col"), P("col", ("dp", "row")), P("col", ("dp", "row"))
    return jax.shard_map(
        per_device,
        mesh=mesh,
        in_specs=(tokens, tokens, P("dp", None), P(), P("col", None, "row"), P("row", None), P("col", "row"),
                  P(None, "col"), col, P(), P(), col, col, col, col, P("col", "row")),
        out_specs=(tokens, tokens, P(), P("col", None, ("dp", "row")), P(), sums, P(), P(), P(), P(), P(), P(), P(), P(), sums),
        check_vma=False,
    )
```

```python
import functools

import jax
import jax.numpy as jnp
from jax import lax
from jax.experimental import pallas as pl
from jax.experimental.pallas import tpu as pltpu
from jax.sharding import PartitionSpec as P

HEADDIM = 64
STATE = 128
CONV = 4
Q = 128
EPS = 1e-05
LOG2E = 1.4426950408889634
F32 = jnp.float32
BF16 = jnp.bfloat16
HIGHEST = lax.Precision.HIGHEST
MESH = pl.DeviceIdType.MESH
VMEM_LIMIT = 56 * 1024 * 1024
CUM, STEP, ENTRY, TAIL, DEC, SIG = range(6)


def nn(a, b, precision=None):
    return lax.dot_general(a, b, (((1,), (0,)), ((), ())), precision=precision, preferred_element_type=F32)


def nt(a, b, precision=None):
    return lax.dot_general(a, b, (((1,), (1,)), ((), ())), precision=precision, preferred_element_type=F32)


def tn(a, b, precision=None):
    return lax.dot_general(a, b, (((0,), (0,)), ((), ())), precision=precision, preferred_element_type=F32)


def halves(v):
    high = v.astype(BF16)
    return high, (v - high.astype(F32)).astype(BF16)


def nn3(a, b):
    (ah, al), (bh, bl) = halves(a), halves(b)
    return nn(jnp.concatenate([ah, ah, al], 1), jnp.concatenate([bh, bl, bh], 0))


def nt3(a, b):
    (ah, al), (bh, bl) = halves(a), halves(b)
    return nt(jnp.concatenate([ah, ah, al], 1), jnp.concatenate([bh, bl, bh], 1))


def sigm(v):
    return 0.5 + 0.5 * jnp.tanh(0.5 * v)


def iota(shape, dim):
    return lax.broadcasted_iota(jnp.int32, shape, dim)


def segment_of(place, ends):
    total = (place >= ends[0]).astype(jnp.int32)
    for end in ends[1:]:
        total = total + (place >= end).astype(jnp.int32)
    return jnp.where(place < 0, -1, total)


def chunk_of(c):
    return pl.ds(pl.multiple_of(c * Q, Q), Q)


def shift_masks(place, ends):
    segment = segment_of(place, ends)
    return [(segment_of(place - d, ends) == segment).astype(F32) for d in range(1, CONV)]


def shifted_right(now, earlier, d, lane):
    return pltpu.roll(jnp.where(lane >= Q - d, earlier, now), d, 1)


def shifted_left(now, later, d, lane):
    return pltpu.roll(jnp.where(lane < d, later, now), Q - d, 1)


def conv_tile(now, earlier, taps, masks, lane):
    total = taps(CONV) + taps(CONV - 1) * now
    for d in range(1, CONV):
        total = total + taps(CONV - 1 - d) * (shifted_right(now, earlier, d, lane) * masks[d - 1])
    return total


def spread(rows_ref, out):
    cols = jnp.transpose(rows_ref[...])
    for k in range(out.shape[0]):
        out[k] = jnp.broadcast_to(cols[:, k : k + 1], out.shape[1:])


def thirds(v):
    high, rest = v.astype(BF16), v
    rest = rest - high.astype(F32)
    middle = rest.astype(BF16)
    return jnp.concatenate([high, middle, (rest - middle.astype(F32)).astype(BF16)], -1)


def times_flags(v, flags):
    return nn(thirds(v), jnp.concatenate([flags.astype(BF16)] * 3, 0))


def stacked(v, count):
    return jnp.concatenate([v[:, c * Q : (c + 1) * Q] for c in range(count)], 0)


def scalars(lengths_ref, rows):
    ends = [lengths_ref[0, 0]]
    for k in range(1, lengths_ref.shape[1]):
        ends.append(ends[-1] + lengths_ref[0, k])
    return lax.axis_index("row") * rows, ends


def enter_kernel(nc, hb, place_ref, xin_ref, bcin_ref, dt_ref, heads_ref, taps8_ref, bctaps8_ref, wait_ref,
                 u_ref, ubc_ref, bc_ref, rows_ref, scores_ref, y_ref, fresh_ref, final_ref, pass_ref, hpar_ref, state, taps_ref, bctaps_ref):
    base, ends = scalars(place_ref, nc * Q)
    wide = iota((HEADDIM, Q), 1)
    block = pl.program_id(0)
    spread(taps8_ref, taps_ref)

    @pl.when(block == 0)
    def _():
        spread(bctaps8_ref, bctaps_ref)
        lane = iota((1, Q), 1)
        row, col = iota((Q, Q), 0), iota((Q, Q), 1)

        def body(c, _):
            masks = shift_masks(base + c * Q + lane, ends)
            for part in range(2 * STATE // HEADDIM):
                at = slice(part * HEADDIM, (part + 1) * HEADDIM)
                u = conv_tile(bcin_ref[at, chunk_of(c + 1)], bcin_ref[at, chunk_of(c)], lambda k: bctaps_ref[k, at, :], masks, wide)
                ubc_ref[at, chunk_of(c)] = u
                bc_ref[at, chunk_of(c)] = u * sigm(u)
            start = base + c * Q
            same = (segment_of(start + row, ends) == segment_of(start + col, ends)) & (row >= col)
            score = nn3(jnp.transpose(bc_ref[STATE:, chunk_of(c)]), bc_ref[:STATE, chunk_of(c)])
            scores_ref[c] = jnp.where(same, score, 0.0)
            return 0

        lax.fori_loop(0, nc, body, 0, unroll=2)

        nb = dt_ref.shape[0]
        by_head = jnp.transpose(heads_ref[...])[:, :8]
        for n in range(nb):
            own = by_head[n * hb : (n + 1) * hb]
            hpar_ref[n] = own if hb == 8 else jnp.concatenate([own, jnp.zeros((8 - hb, 8), F32)], 0)
        raw = jnp.concatenate([dt_ref[n] + hpar_ref[n, :, 0:1] for n in range(nb)], 0)
        rate = jnp.concatenate([-jnp.exp(hpar_ref[n, :, 1:2]) for n in range(nb)], 0)
        small = jnp.exp(-jnp.abs(raw))
        steps = jnp.maximum(raw, 0.0) + jnp.log1p(small)
        sig = jnp.where(raw >= 0, 1.0, small) / (1.0 + small)
        each = nb * 8
        cums = times_flags(stacked(steps * rate * LOG2E, nc), row <= col)
        whole_sum = jnp.zeros((each, 1), F32)
        for c in range(nc):
            at = slice(c * Q, (c + 1) * Q)
            start = base + c * Q
            segment = segment_of(start + lane, ends)
            before = segment_of(start - 1, ends)
            after = segment_of(start + Q - 1, ends)
            cum = cums[c * each : (c + 1) * each]
            last = cum[:, Q - 1 : Q]
            entry = jnp.exp2(cum) * (segment == before).astype(F32)
            tail = jnp.exp2(last - cum) * (segment == after).astype(F32)
            decay = jnp.broadcast_to(jnp.exp2(last), (each, Q)) * (before == after).astype(F32)
            for n in range(nb):
                part = slice(n * 8, (n + 1) * 8)
                rows_ref[n, CUM, :, at] = cum[part]
                rows_ref[n, STEP, :, at] = steps[part, at]
                rows_ref[n, ENTRY, :, at] = entry[part]
                rows_ref[n, TAIL, :, at] = tail[part]
                rows_ref[n, DEC, :, at] = decay[part]
                rows_ref[n, SIG, :, at] = sig[part, at]
            whole_sum = whole_sum + last
        end = segment_of(base + nc * Q - 1, ends)
        keep = jnp.broadcast_to(jnp.exp2(whole_sum), (each, Q)) * (segment_of(base - 1, ends) == end).astype(F32)
        for n in range(nb):
            pass_ref[n] = keep[n * 8 : (n + 1) * 8]

    state[...] = jnp.zeros_like(state)

    def chunk(c, _):
        now = chunk_of(c)
        masks = shift_masks(base + c * Q + iota((1, Q), 1), ends)
        cum8 = rows_ref[block, CUM, :, now]
        cols = jnp.transpose(cum8)
        weighted = []
        for h in range(hb):
            at = slice(h * HEADDIM, (h + 1) * HEADDIM)
            hr = slice(h, h + 1)
            u = conv_tile(xin_ref[at, chunk_of(c + 1)], xin_ref[at, now], lambda k: taps_ref[k, at, :], masks, wide)
            u_ref[at, now] = u
            x = u * sigm(u)
            moved = x * rows_ref[block, STEP, hr, now]
            decay = jnp.exp2(jnp.minimum(cols[:, hr] - cum8[hr, :], 0.0))
            mixing = (decay * scores_ref[c]).astype(BF16)
            y_ref[at, now] = nt(moved.astype(BF16), mixing) + hpar_ref[block, hr, 2:3] * x
            weighted.append((moved * rows_ref[block, TAIL, hr, now]).astype(BF16))
        fresh = nt(jnp.concatenate(weighted, 0), bc_ref[:STATE, now].astype(BF16))
        fresh_ref[c] = fresh
        for h in range(hb):
            at = slice(h * HEADDIM, (h + 1) * HEADDIM)
            state[at, :] = state[at, :] * rows_ref[block, DEC, h : h + 1, now] + fresh[at, :]
        return 0

    lax.fori_loop(0, nc, chunk, 0, unroll=2)
    final_ref[...] = state[...].astype(BF16)


def across_kernel(nc, hb, y_ref, fresh_ref, start_ref, bc_ref, rows_ref, z_ref, gg_ref, gate8_ref,
                  y_out, states_ref, stat_ref, state, gate_ref):
    first = pl.program_id(0) == 0

    @pl.when(first)
    def _():
        stat_ref[...] = jnp.zeros_like(stat_ref)

    state[...] = start_ref[...]
    spread(gate8_ref, gate_ref)

    def chunk(c, _):
        states_ref[c] = state[...]
        outer = nn3(state[...], bc_ref[STATE:, chunk_of(c)])
        square = jnp.zeros((8, Q), F32)
        cross = jnp.zeros((8, Q), F32)
        for h in range(hb):
            at = slice(h * HEADDIM, (h + 1) * HEADDIM)
            y = y_ref[at, chunk_of(c)] + outer[at, :] * rows_ref[0, ENTRY, h : h + 1, chunk_of(c)]
            y_out[at, chunk_of(c)] = y
            z = z_ref[at, chunk_of(c)]
            gz = y * (z * sigm(z))
            other = gz * gate_ref[0, at, :] * gg_ref[at, chunk_of(c)]
            squared = gz * gz
            for k in range(HEADDIM // 8):
                square = square + squared[k * 8 : (k + 1) * 8]
                cross = cross + other[k * 8 : (k + 1) * 8]
            state[at, :] = state[at, :] * rows_ref[0, DEC, h : h + 1, chunk_of(c)] + fresh_ref[c, at, :]
        stat_ref[0, :, chunk_of(c)] += square
        stat_ref[1, :, chunk_of(c)] += cross
        return 0

    lax.fori_loop(0, nc, chunk, 0, unroll=4)


def lane_sums(v):
    return nt(jnp.ones((8, 2 * Q), BF16), jnp.concatenate(halves(v), 1))


def gate_kernel(nc, hb, y_ref, z_ref, gg_ref, tok_ref, gate8_ref, bc_ref, rows_ref,
                gated_ref, gz_ref, gy_ref, adj_ref, first_ref, ggate_ref, adjoint, gsum, gate_ref):
    spread(gate8_ref, gate_ref)
    adjoint[...] = jnp.zeros_like(adjoint)
    gsum[...] = jnp.zeros_like(gsum)

    def chunk(k, _):
        c = nc - 1 - k
        rstd = tok_ref[0:1, chunk_of(c)]
        pull = tok_ref[1:2, chunk_of(c)]
        lifted = []
        for h in range(hb):
            at = slice(h * HEADDIM, (h + 1) * HEADDIM)
            y, z, gg = y_ref[at, chunk_of(c)], z_ref[at, chunk_of(c)], gg_ref[at, chunk_of(c)]
            s = sigm(z)
            silu = z * s
            gz = y * silu
            gate = gate_ref[0, at, :]
            gzr = gz * rstd
            gated_ref[at, chunk_of(c)] = (gzr * gate).astype(BF16)
            gsum[at, :] += gzr * gg
            ggz = rstd * (gate * gg) - gz * pull
            gy = ggz * silu
            gz_ref[at, chunk_of(c)] = (ggz * y * (s * (1.0 + z * (1.0 - s)))).astype(BF16)
            gy_ref[at, chunk_of(c)] = gy
            lifted.append(gy * rows_ref[0, ENTRY, h : h + 1, chunk_of(c)])
        adj = nt3(jnp.concatenate(lifted, 0), bc_ref[STATE:, chunk_of(c)])
        adj_ref[c] = adj
        for h in range(hb):
            at = slice(h * HEADDIM, (h + 1) * HEADDIM)
            adjoint[at, :] = adjoint[at, :] * rows_ref[0, DEC, h : h + 1, chunk_of(c)] + adj[at, :]
        return 0

    lax.fori_loop(0, nc, chunk, 0, unroll=4)
    first_ref[...] = adjoint[...].astype(BF16)
    ggate_ref[...] = lane_sums(gsum[...])


def conv_back(gu, later, taps, masks, lane):
    moved = [gu]
    total = taps(CONV - 1) * gu
    for d in range(1, CONV):
        part = shifted_left(gu * masks[d - 1], later * masks[CONV - 1 + d - 1], d, lane)
        moved.append(part)
        total = total + taps(CONV - 1 - d) * part
    return total, moved


def conv_rim(gu, taps, masks, lane, rim_in):
    total = jnp.zeros_like(gu)
    sums = []
    for d in range(1, CONV):
        part = pltpu.roll(jnp.where(lane < d, gu * masks[d - 1], 0.0), Q - d, 1)
        total = total + taps(CONV - 1 - d) * part
        sums.append(rim_in * part)
    return total, sums


def back_masks(base, c, ends):
    lane = iota((1, Q), 1)
    return shift_masks(base + c * Q + lane, ends) + shift_masks(base + (c + 1) * Q + lane, ends)


def total_rows(v):
    return jnp.sum(v, 0, keepdims=True)


def early_sums(early, n_dp, grads, outs, come1, come2, come3, sems):
    half = grads[0].shape[0] // 2
    views = []
    for k, (a, at, width) in enumerate(early["pieces"]):
        columns = pl.ds(at, width)
        views.append((grads[a].at[pl.ds(0, half), columns], grads[a].at[pl.ds(half, half), columns], come1.at[k], come2.at[k], come3.at[k],
                      outs[a].at[:, columns]))
    return RowSums(n_dp, views, sems)


def sent_sums(early, n_dp, grads, outs, *refs):
    sums = early_sums(early, n_dp, grads, outs, *refs)
    groups = early["groups"]
    for t in range(early["steps"]):
        @pl.when(pl.program_id(0) == t)
        def _():
            if t == 0:
                meet(sums.partners())
            for stage, lag in ((sums.along, 2), (sums.across, 1), (sums.pair, 0), (sums.finish, 3)):
                if 0 <= t - lag < len(groups):
                    for p in groups[t - lag]:
                        stage(p)


def end_sums(early, n_dp, grads, outs, *refs):
    sums = early_sums(early, n_dp, grads, outs, *refs)
    groups, steps = early["groups"], early["steps"]

    @pl.when(pl.program_id(0) == steps - 1)
    def _():
        for t in range(steps, len(groups) + 3):
            for stage, lag in ((sums.along, 2), (sums.across, 1), (sums.finish, 3)):
                if 0 <= t - lag < len(groups):
                    for p in groups[t - lag]:
                        stage(p)
        for p in range(len(early["pieces"])):
            sums.first(p).wait_send()
            sums.sent(p)


def back_kernel(nc, hb, heads, early, n_dp, place_ref, u_ref, xin_ref, gy_ref, y_ref, states_ref, adj_ref, start_ref, bc_ref, scores_ref,
                rows_ref, hpar_ref, taps8_ref, *refs):
    refs = list(refs)
    take = lambda count: [refs.pop(0) for _ in range(count)]
    arrays = 2 if early else 0
    grads = take(arrays)
    gx_ref, gxlast_ref, rim_ref, gtaps_ref, gdt_ref, gscores, gbct, hsum_ref = take(8)
    sums_out = take(arrays)
    adjoint, gnext, tapsum, hrow, taps_ref, ends_at = take(6)
    if early:
        sent_sums(early, n_dp, grads, sums_out, *refs)
    spread(taps8_ref, taps_ref)
    base, ends = scalars(place_ref, nc * Q)
    wide = iota((HEADDIM, Q), 1)
    block = pl.program_id(0)

    @pl.when(block == 0)
    def _():
        hsum_ref[...] = jnp.zeros_like(hsum_ref)
        gscores[...] = jnp.zeros_like(gscores)
        gbct[...] = jnp.zeros_like(gbct)
        hrow[...] = jnp.zeros_like(hrow)

    adjoint[...] = start_ref[...]
    gnext[...] = jnp.zeros_like(gnext)
    tapsum[...] = jnp.zeros_like(tapsum)

    def chunk(k, _):
        c = nc - 1 - k
        now = chunk_of(c)
        masks = back_masks(base, c, ends)
        from_later = nn(adjoint[...].astype(BF16), bc_ref[:STATE, now].astype(BF16))
        cum8 = rows_ref[0, CUM, :, now]
        cols = jnp.transpose(cum8)
        lifted, weighted = [], []
        for h in range(hb):
            at = slice(h * HEADDIM, (h + 1) * HEADDIM)
            hr = slice(h, h + 1)
            u = u_ref[at, now]
            gy = gy_ref[at, now]
            s = sigm(u)
            x = u * s
            step = rows_ref[0, STEP, hr, now]
            tail = rows_ref[0, TAIL, hr, now]
            moved = x * step
            moved_low = moved.astype(BF16)
            gy_low = gy.astype(BF16)
            decay = jnp.exp2(jnp.minimum(cols[:, hr] - cum8[hr, :], 0.0))
            gmix = tn(gy_low, moved_low)
            gscores[c] += gmix * decay
            gmoved = nn(gy_low, (decay * scores_ref[c]).astype(BF16))
            later = from_later[at, :] * tail
            lifted.append((gy * rows_ref[0, ENTRY, hr, now]).astype(BF16))
            weighted.append((moved * tail).astype(BF16))
            skip = hpar_ref[0, hr, 2:3]
            taken = gy_low.astype(F32) * (y_ref[at, now] - skip * x) - moved_low.astype(F32) * gmoved
            hrow[0, block, hr, now] = total_rows(taken)
            hrow[1, block, hr, now] = total_rows(moved * later)
            hrow[2, block, hr, now] = total_rows(adjoint[at, :] * states_ref[c, at, :]) * rows_ref[0, DEC, hr, now]
            gmoved = gmoved + later
            hrow[3, block, hr, now] = total_rows(x * gmoved)
            hrow[4, block, hr, now] = total_rows(x * gy)
            gx = gmoved * step + skip * gy
            gu = gx * (s * (1.0 + u * (1.0 - s)))
            gin, shifts = conv_back(gu, gnext[at, :], lambda k: taps_ref[k, at, :], masks, wide)
            gnext[at, :] = gu
            gx_ref[at, now] = gin.astype(BF16)

            ends_at[jnp.minimum(k, 1), at, :] = gin
            xin = xin_ref[at, chunk_of(c + 1)]
            for d in range(CONV):
                tapsum[d, at, :] += xin * shifts[d]
            tapsum[CONV, at, :] += gu
        gbct[STATE:, now] += tn(states_ref[c].astype(BF16), jnp.concatenate(lifted, 0))
        gbct[:STATE, now] += tn(adjoint[...].astype(BF16), jnp.concatenate(weighted, 0))
        for h in range(hb):
            at = slice(h * HEADDIM, (h + 1) * HEADDIM)
            adjoint[at, :] = adjoint[at, :] * rows_ref[0, DEC, h : h + 1, now] + adj_ref[c, at, :]
        return 0

    lax.fori_loop(0, nc, chunk, 0, unroll=2)

    gxlast_ref[...] = ends_at[0]
    masks = back_masks(base, 0, ends)
    for h in range(hb):
        at = slice(h * HEADDIM, (h + 1) * HEADDIM)
        rim, sums = conv_rim(gnext[at, :], lambda k: taps_ref[k, at, :], masks, wide, xin_ref[at, :Q])
        rim_ref[at, :] = rim.astype(BF16)
        for d in range(1, CONV):
            tapsum[d, at, :] += sums[d - 1]
    gtaps_ref[...] = jnp.concatenate([lane_sums(tapsum[d])[0:1] for d in range(CONV + 1)] + [jnp.zeros((7 - CONV, hb * HEADDIM), F32)], 0)

    row, col = iota((Q, Q), 0), iota((Q, Q), 1)
    glogs = (times_flags(stacked(hrow[0, block], nc), row >= col) + times_flags(stacked(hrow[1, block], nc), row < col)
             + times_flags(stacked(hrow[2, block], nc), row >= 0))
    rate = -jnp.exp(hpar_ref[0, :, 1:2])
    total = [jnp.zeros((8, Q), F32) for _ in range(3)]
    for c in range(nc):
        at = slice(c * Q, (c + 1) * Q)
        glog = glogs[c * 8 : (c + 1) * 8] * rate
        gdt = (hrow[3, block, :, at] + glog) * rows_ref[0, SIG, :, at]
        gdt_ref[0, :, at] = gdt
        total[0] = total[0] + gdt
        total[1] = total[1] + glog * rows_ref[0, STEP, :, at]
        total[2] = total[2] + hrow[4, block, :, at]
    sums = times_flags(jnp.concatenate(total, 0), row >= 0)
    first = lax.axis_index("col") * heads + block * hb
    lane = iota((1, Q), 1)
    for k in range(3):
        for h in range(hb):
            hsum_ref[k : k + 1, :] += jnp.where(lane == first + h, sums[k * 8 + h : k * 8 + h + 1, :], 0.0)

    if early:
        end_sums(early, n_dp, grads, sums_out, *refs)


def state_kernel(nc, place_ref, bc_ref, ubc_ref, bcin_ref, bctaps8_ref, gscores_in, gbct_in,
                 gbc_ref, gbclast_ref, bcrim_ref, gbctaps_ref, gnext, tapsum, bctaps_ref, ends_at):
    spread(bctaps8_ref, bctaps_ref)
    base, ends = scalars(place_ref, nc * Q)
    row, col = iota((Q, Q), 0), iota((Q, Q), 1)
    wide = iota((HEADDIM, Q), 1)
    gnext[...] = jnp.zeros_like(gnext)
    tapsum[...] = jnp.zeros_like(tapsum)
    tiles = [slice(k * HEADDIM, (k + 1) * HEADDIM) for k in range(2 * STATE // HEADDIM)]

    def body(k, _):
        c = nc - 1 - k
        now = chunk_of(c)
        start = base + c * Q
        same = (segment_of(start + row, ends) == segment_of(start + col, ends)) & (row >= col)
        gscore = jnp.where(same, gscores_in[c], 0.0)
        masks = back_masks(base, c, ends)
        inter = gbct_in[:, now]
        g_c = inter[STATE:] + nt3(bc_ref[:STATE, now], gscore)
        g_b = inter[:STATE] + nn3(bc_ref[STATE:, now], gscore)
        g_bc = jnp.concatenate([g_b, g_c], 0)
        for at in tiles:
            u = ubc_ref[at, now]
            s = sigm(u)
            gu = g_bc[at] * (s * (1.0 + u * (1.0 - s)))
            gin, shifts = conv_back(gu, gnext[at, :], lambda k: bctaps_ref[k, at, :], masks, wide)
            gnext[at, :] = gu
            gbc_ref[at, now] = gin.astype(BF16)

            ends_at[jnp.minimum(k, 1), at, :] = gin
            xin = bcin_ref[at, chunk_of(c + 1)]
            for d in range(CONV):
                tapsum[d, at, :] += xin * shifts[d]
            tapsum[CONV, at, :] += gu
        return 0

    lax.fori_loop(0, nc, body, 0)
    gbclast_ref[...] = ends_at[0]
    masks = back_masks(base, 0, ends)
    for at in tiles:
        rim, more = conv_rim(gnext[at, :], lambda k: bctaps_ref[k, at, :], masks, wide, bcin_ref[at, :Q])
        bcrim_ref[at, :] = rim.astype(BF16)
        for d in range(1, CONV):
            tapsum[d, at, :] += more[d - 1]
    for d in range(CONV + 1):
        gbctaps_ref[:, d * 2 * STATE : (d + 1) * 2 * STATE] = lane_sums(tapsum[d])


def whole(*shape):
    return pl.BlockSpec(shape, lambda n: (0,) * len(shape))


def params():
    return pltpu.CompilerParams(vmem_limit_bytes=VMEM_LIMIT)


SMEM = pl.BlockSpec(memory_space=pltpu.SMEM)


def shape(dtype, *dims):
    return jax.ShapeDtypeStruct(dims, dtype)


def after(value, *others):
    return lax.optimization_barrier((value,) + others)[0]


def moved(value, axis, steps):
    n = lax.axis_size(axis)
    return lax.ppermute(value, axis, [(k, (k + steps) % n) for k in range(n)])


def swapped(value, axis, bit):
    n = lax.axis_size(axis)
    return lax.ppermute(value, axis, [(k, k ^ bit) for k in range(n)])


def col_sum(value):
    if lax.axis_size("col") == 2:
        return value + swapped(value, "col", 1)
    return lax.psum(value, "col")


def from_before(value, steps):
    n = lax.axis_size("row")
    pairs = [(k, k + steps) for k in range(max(0, -steps), min(n, n - steps))]
    return lax.ppermute(value, "row", pairs)


def chained(state, keep, hb, direction):
    nb, inner = keep.shape[0], state.shape[0]
    flat = keep.reshape(nb * 8, Q)
    high, low = halves(flat)
    packed = jnp.concatenate([state, high, low], axis=0)
    total, decay = None, None
    for k in range(1, lax.axis_size("row")):
        part = from_before(packed, direction * k)
        passing = part[inner : inner + nb * 8].astype(F32) + part[inner + nb * 8 :].astype(F32)
        passing = jnp.repeat(passing.reshape(nb, 8, Q)[:, :hb].reshape(nb * hb, Q), HEADDIM, axis=0)
        part = part[:inner].astype(F32)
        total = part if total is None else total + decay * part
        decay = passing if decay is None else decay * passing
    return total


def sum_stages(n_row):
    order, bits = [0], []
    bit = n_row // 2
    while bit:
        order = [k + bit for k in order] + order
        bits.insert(0, bit)
        bit //= 2
    return order, bits


def far(source, target, sems, k, axis, place):
    return pltpu.make_async_remote_copy(
        src_ref=source, dst_ref=target, send_sem=sems.at[0, k], recv_sem=sems.at[1, k],
        device_id={axis: place}, device_id_type=MESH)


def meet(partners):
    barrier = pltpu.get_barrier_semaphore()
    for axis, place in partners:
        pl.semaphore_signal(barrier, inc=1, device_id={axis: place}, device_id_type=MESH)
    pl.semaphore_wait(barrier, len(partners))


class RowSums:
    def __init__(self, n_dp, pieces, sems):
        self.row, dp = lax.axis_index("row"), lax.axis_index("dp")
        self.n_dp, self.pieces, self.sems = n_dp, pieces, sems
        self.dps = [lax.rem(dp + k, n_dp) for k in range(n_dp)]
        self.quarter = pieces[0][3].shape[0]
        self.block = self.quarter // n_dp
        self.per = n_dp + 1

    def partners(self):
        return [("row", self.row ^ 1), ("row", self.row ^ 2)] + [("dp", d) for d in self.dps[1:]]

    def first(self, p):
        send, _, come1, _, _, _ = self.pieces[p]
        return far(send, come1, self.sems, p * self.per, "row", self.row ^ 1)

    def second(self, p):
        _, _, come1, come2, _, _ = self.pieces[p]
        return far(come1.at[pl.ds(0, self.quarter)], come2, self.sems, p * self.per + 1, "row", self.row ^ 2)

    def third(self, p):
        _, _, _, come2, come3, _ = self.pieces[p]
        block = self.block
        return [far(come2.at[pl.ds(k * block, block)], come3.at[pl.ds((k - 1) * block, block)], self.sems, p * self.per + 1 + k, "dp", self.dps[k])
                for k in range(self.n_dp - 1, 0, -1)]

    def pair(self, p):
        self.first(p).start()

    def across(self, p):
        _, kept, come1, _, _, _ = self.pieces[p]
        self.first(p).wait_recv()
        add_rows(come1, 0, kept, 0, self.quarter)
        self.second(p).start()
        add_rows(come1, self.quarter, kept, self.quarter, self.quarter)

    def along(self, p):
        _, _, come1, come2, _, _ = self.pieces[p]
        self.second(p).wait_recv()
        add_rows(come2, 0, come1, self.quarter, self.quarter)
        for copy in self.third(p):
            copy.start()

    def finish(self, p):
        _, _, _, come2, come3, out = self.pieces[p]
        for copy in self.third(p):
            copy.wait_recv()

        def body(i, _):
            at = i * 32
            total = come2[pl.ds(at, 32), :].astype(F32)
            for k in range(1, self.n_dp):
                total = total + come3[pl.ds((k - 1) * self.block + at, 32), :].astype(F32)
            out[pl.ds(at, 32), :] = total
            return 0

        lax.fori_loop(0, self.block // 32, body, 0, unroll=True)

    def sent(self, p):
        self.second(p).wait_send()
        for copy in self.third(p):
            copy.wait_send()


def add_rows(out, out_at, other, other_at, count):
    def body(i, _):
        at = i * 32
        out[pl.ds(out_at + at, 32), :] = out[pl.ds(out_at + at, 32), :] + other[pl.ds(other_at + at, 32), :]
        return 0

    lax.fori_loop(0, count // 32, body, 0, unroll=4)


def close_kernel(n_row, n_dp, n_col, sources, pieces, has_gn, fused, *refs):
    refs = list(refs)
    take = lambda count: [refs.pop(0) for _ in range(count)]
    lefts = take(1 + max(left for left, _, _ in sources))
    if fused:
        nc, hb, n_late = fused
        lengths_ref, = take(1)
        rows_given = take(3)
    else:
        gbd, = take(1)
        rows_given = take(4)
    if has_gn:
        gain8, rstd8 = take(2)
    else:
        stat, gain_row = take(2)
    later_given = take(n_late if fused else 2 + len(sources) - 3 + (5 if has_gn else 0))
    outs = take(len(sources))
    state_out, small_out, stat_out = take(3)
    if has_gn:
        grad_in, = take(1)
    come1, come2, come3 = take(len(sources)), take(len(sources)), take(len(sources))
    grad_slots, = take(1)
    later_held = take(len(later_given))
    small_a, small_b, small_c, state_a, state_b = take(5)
    sems_grad, sems_small, sems_state, sems_other, sems_local, small = take(6)
    if has_gn:
        gn_sum, gn, gn_come, gain, gsum, stat = take(6)
    if fused:
        gbd, gbctaps, gbclast, rim_bc, rims, gnext, tapsum, bctaps, ends_at, sems_rim = take(10)
        rows_given = rows_given[:2] + [gbctaps] + rows_given[2:]

    loads = [pltpu.make_async_copy(source, held, sems_local.at[k]) for k, (source, held) in enumerate(zip(later_given, later_held))]
    loading, loaded = set(), set()

    def fetch(*keys):
        for k in keys:
            if k not in loading:
                loads[k].start()
                loading.add(k)

    def held(k):
        fetch(k)
        if k not in loaded:
            loads[k].wait()
            loaded.add(k)
        return later_held[k]

    fetch(*((1, 7) if fused else range(len(loads))))

    row, dp, col = lax.axis_index("row"), lax.axis_index("dp"), lax.axis_index("col")
    dps = [lax.rem(dp + k, n_dp) for k in range(n_dp)]
    cols = [lax.rem(col + k, n_col) for k in range(n_col)]
    rows = lefts[0].shape[0]
    half, quarter = rows // 2, rows // 4
    block = quarter // n_dp
    count = len(pieces)
    slots = grad_slots.shape[0]
    views = []
    for p, (a, at, width) in enumerate(pieces):
        columns, mine = pl.ds(at, width), grad_slots.at[p % slots, :, pl.ds(0, width)]
        views.append((mine.at[pl.ds(0, half)], mine.at[pl.ds(half, half)], come1[a].at[:, columns], come2[a].at[:, columns],
                      come3[a].at[:, columns], outs[a].at[:, columns]))
    sums = RowSums(n_dp, views, sems_grad)
    ahead, behind = lax.rem(row + 1, n_row), lax.rem(row + n_row - 1, n_row)
    meet(sums.partners() + [("col", c) for c in cols[1:]] + ([("row", ahead), ("row", behind)] if fused else []))
    started = []

    def start(copy):
        copy.start()
        started.append(copy)
        return copy

    def make(p):
        a, at, width = pieces[p]
        left, first_row, right = sources[a]
        if p >= slots:
            sums.first(p - slots).wait_send()
        right = gbd if right is None else held(right)
        value = right[first_row + at : min(first_row + at + width, right.shape[0]), :]
        if value.shape[0] < width:
            value = jnp.concatenate([value, jnp.zeros((width - value.shape[0], value.shape[1]), BF16)], 0)
        for part in range(2):
            rows_here = slice(part * half, (part + 1) * half)
            grad_slots[p % slots, rows_here, :width] = nt(lefts[left][rows_here, :], value).astype(BF16)
            if part == 0:
                sums.pair(p)

    group = lambda r: pl.ds(pl.multiple_of(r * (n_dp * block), 16), n_dp * block)
    here = pl.ds(pl.multiple_of((row * n_dp + dp) * block, 16), block)
    n0 = n_col - 1
    n1 = n0 + n_dp - 1
    later = {"others": []}

    def send_rim():
        later["rim"] = start(far(held(7), rims.at[pl.ds(0, held(7).shape[0])], sems_rim, 0, "row", behind))

    def add_rim(target, last, at, count):
        tokens = target.shape[1]
        come = jnp.where(row < n_row - 1, rims[at : at + count, :].astype(F32), 0.0)
        target[:count, tokens - Q :] = (last[...] + come).astype(BF16)

    def take_rim():
        later["rim"].wait_recv()
        add_rim(held(0), held(8), 0, held(8).shape[0])

    def state_back():
        bc, ubc, bcin, bctaps8, gscores, gbct, gdt = (held(k) for k in range(9, 16))
        state_kernel(nc, lengths_ref, bc, ubc, bcin, bctaps8, gscores, gbct, gbd, gbclast, rim_bc, gbctaps, gnext, tapsum, bctaps, ends_at)
        channels = held(8).shape[0]
        later["rim_bc"] = start(far(rim_bc, rims.at[pl.ds(channels, 2 * STATE)], sems_rim, 1, "row", behind))
        steps = [gdt[n, :hb, :] for n in range(gdt.shape[0])]
        rest = gbd.shape[0] - 2 * STATE - hb * gdt.shape[0]
        gbd[2 * STATE :, :] = jnp.concatenate(steps + [jnp.zeros((rest, gdt.shape[2]), F32)], 0).astype(BF16)

    def take_rim_bc():
        later["rim_bc"].wait_recv()
        add_rim(gbd, gbclast, held(8).shape[0], 2 * STATE)

    def product(place, which):
        value, w4 = held(which), held(2 + which)
        weights = lambda w4: jnp.concatenate([w4[place * (n_row // 2) + k] for k in range(n_row // 2)], 1)
        part = tn(weights(w4), value[...])
        if which:
            gn_sum[...] = part
        else:
            bd4 = held(4)
            gn_sum[...] += part + tn(weights(bd4), gbd[: bd4.shape[1], :])

    def prepare(k, place):
        hx = held(5)
        width = gn_sum.shape[0]
        rstd = rstd8[0:1, :]

        def body(i, total):
            at = pl.ds(i * 16, 16)
            there = pl.ds(pl.multiple_of(place * width + i * 16, 16), 16)
            pushed = gn_sum[at, :]
            if k == 0:
                gn[at, :] = pushed.astype(BF16)
            product = hx[there, Q:].astype(F32) * pushed
            scaled = product * rstd
            summed = scaled[:, :128]
            for tile in range(1, scaled.shape[1] // 128):
                summed = summed + scaled[:, tile * 128 : (tile + 1) * 128]
            gsum[at, :] = summed
            product = product * gain[0, there, 0:1]
            return total + product[:8] + product[8:]

        total = lax.fori_loop(0, width // 16, body, jnp.zeros((8, rstd.shape[1]), F32), unroll=2)
        total = rstd * total_rows(total)
        stat[...] = total if k == 0 else stat[...] + total
        small[6:7, pl.ds(pl.multiple_of(place * width, 128), width)] = lane_sums(gsum[...])[0:1]

    def begin_rows():
        channels = rows_given[0].shape[1]
        small[0 : CONV + 1, :channels] = rows_given[0][0 : CONV + 1, :]
        small[CONV + 1 : CONV + 2, :channels] = rows_given[1][0:1, :]
        small[7:8, : rows_given[2].shape[1]] = rows_given[2][0:1, :]
        for k in range(3):
            small[8:9, k * 128 : (k + 1) * 128] = rows_given[3][k : k + 1, :]

    def begin():
        small[...] = jnp.zeros_like(small)
        if has_gn:
            spread(gain8, gain)
        else:
            small[6:7, : gain_row.shape[1]] = gain_row[...]
        if not fused:
            begin_rows()

    def send_norm():
        if fused:
            begin()
        prepare(0, 1 - col)
        later["others"].append(start(far(gn, gn_come, sems_other, 0, "col", cols[1])))

    def send_small():
        if fused:
            begin_rows()
        if has_gn:
            prepare(1, col)
        later["small1"] = start(far(small, small_a.at[0], sems_small, 0, "row", row ^ 1))
        later["others"] += [start(far(stat, stat_out.at[col], sems_other, k, "col", cols[k])) for k in range(1, n_col)]
        stat_out[col] = stat[...]

    def small_pair():
        later["small1"].wait_recv()
        small_a[1] = small[...] + small_a[0]
        later["small2"] = start(far(small_a.at[1], small_b.at[0], sems_small, 1, "row", row ^ 2))

    def small_dp():
        later["small2"].wait_recv()
        small_b[1] = small_a[1] + small_b[0]
        later["small3"] = [start(far(small_b.at[1], small_c.at[k], sems_small, 1 + k, "dp", dps[k])) for k in range(1, n_dp)]

    def small_col():
        for copy in later["small3"]:
            copy.wait_recv()
        total = small_b[1]
        for k in range(1, n_dp):
            total = total + small_c[k]
        small_out[col] = total
        later["small4"] = [start(far(small_out.at[col], small_out.at[col], sems_small, n_dp + k, "col", cols[k])) for k in range(1, n_col)]

    def state_col():
        state_a[0] = outs[0][:, : state_a.shape[2]]
        later["state1"] = [start(far(state_a.at[0], state_a.at[k], sems_state, k - 1, "col", cols[k])) for k in range(1, n_col)]

    def state_dp():
        for copy in later["state1"]:
            copy.wait_recv()
        total = state_a[0]
        for k in range(1, n_col):
            total = total + state_a[k]
        state_b[...] = total.astype(state_b.dtype)
        state_out[here, :] = state_b[...]
        later["state2"] = [start(far(state_b, state_out.at[here], sems_state, n0 + k - 1, "dp", dps[k])) for k in range(1, n_dp)]

    def state_row():
        for copy in later["state2"]:
            copy.wait_recv()
        later["state3"] = start(far(state_out.at[group(row)], state_out.at[group(row)], sems_state, n1, "row", row ^ 2))

    def state_pair():
        later["state3"].wait_recv()
        later["state4"] = [start(far(state_out.at[group(r)], state_out.at[group(r)], sems_state, n1 + 1 + k, "row", row ^ 1))
                           for k, r in enumerate((row, row ^ 2))]

    def norm_back():
        for copy in later["others"]:
            copy.wait_recv()
        if not has_gn:
            return
        hx, grad_out = held(5), held(6)
        rstd = rstd8[0:1, :]
        total = stat_out[0]
        for k in range(1, n_col):
            total = total + stat_out[k]
        own = gn_sum.shape[0]
        width = n_col * own
        pull = (rstd * rstd) * (total / width)

        def body(i, _):
            at = pl.ds(i * 16, 16)
            there = pl.ds(pl.multiple_of(col * own + i * 16, 16), 16)
            pushed = gn_sum[at, :] + gn_come[at, :].astype(F32)
            grad_in[at, :] = (grad_out[at, :].astype(F32) + (rstd * gain[0, there, 0:1]) * pushed
                              - hx[there, Q:].astype(F32) * pull).astype(BF16)
            return 0

        lax.fori_loop(0, own // 16, body, 0, unroll=2)

    ahead_of = {}
    if fused:
        ahead_of = {4: [take_rim_bc], 6: [take_rim]}
        extra = {0: [send_rim], 2: [state_back], 4: [lambda: product(1 - col, 1)], 7: [lambda: product(1 - col, 0), send_norm],
                 8: [lambda: product(col, 1)], 9: [state_col], 10: [lambda: product(col, 0), send_small], 11: [state_dp, small_pair],
                 12: [state_row, small_dp], 13: [state_pair, small_col], 15: [norm_back]}
    elif has_gn:
        extra = {1: [lambda: product(1 - col, 1)], 2: [lambda: product(1 - col, 0), send_norm], 4: [lambda: product(col, 1)],
                 6: [lambda: product(col, 0), send_small], 7: [state_col], 8: [small_pair], 9: [state_dp], 10: [small_dp], 11: [state_row],
                 12: [small_col], 13: [state_pair, norm_back]}
    else:
        extra = {1: [send_small], 3: [small_pair], 4: [small_dp], 5: [small_col], 7: [state_col], 8: [state_dp], 9: [state_row],
                 10: [state_pair], 11: [norm_back]}
    for step in extra.get(0, ()):
        step()
    make(0)
    if fused:
        fetch(*range(9, 16), 3, 0, 8, 2, 4, 5, 6)
    else:
        begin()
    for t in range(1, max(count + 6, 16)):
        for step in ahead_of.get(t, ()):
            step()
        if t < count:
            make(t)
        if 0 <= t - 1 < count:
            sums.across(t - 1)
        if 0 <= t - 3 < count:
            sums.along(t - 3)
        if 0 <= t - 5 < count:
            sums.finish(t - 5)
        for step in extra.get(t, ()):
            step()
    for copy in later["small4"] + later["state4"]:
        copy.wait_recv()
    for k in range(len(loads)):
        held(k)
    for copy in started:
        copy.wait_send()
    for p in range(count):
        if p + slots >= count:
            sums.first(p).wait_send()
        sums.sent(p)


def close(sources, pieces, lefts, gbd, given, gn, plain, later, fused=()):
    n_row, n_dp, n_col = (lax.axis_size(axis) for axis in ("row", "dp", "col"))
    assert n_row == 4
    rows, tokens = lefts[0].shape
    widths = [max(at + width for a, at, width in pieces if a == k) for k in range(len(sources))]
    half, quarter, block = rows // 2, rows // 4, rows // 4 // n_dp
    vmem, anywhere = pl.BlockSpec(memory_space=pltpu.VMEM), pl.BlockSpec(memory_space=pl.ANY)
    has_gn = gn is not None
    here = rows // n_col
    given = list(given)
    small = (16, max(rows, given[1 if fused else 0].shape[1]))
    channels = given[1].shape[1]
    extra = list(gn) if has_gn else list(plain)
    out = pl.pallas_call(
        functools.partial(close_kernel, n_row, n_dp, n_col, sources, pieces, has_gn, fused),
        in_specs=[vmem] * len(lefts) + ([SMEM] + [vmem] * 3 if fused else [vmem] * 5) + [vmem] * len(extra) + [anywhere] * len(later),
        out_specs=[vmem] * (len(sources) + 3 + has_gn),
        out_shape=[shape(F32, block, width) for width in widths]
        + [shape(BF16, rows, 2 * STATE), shape(F32, n_col, *small), shape(F32, n_col, 1, tokens)] + [shape(BF16, here, tokens)] * has_gn,
        scratch_shapes=[pltpu.VMEM((half, width), BF16) for width in widths] + [pltpu.VMEM((quarter, width), BF16) for width in widths]
        + [pltpu.VMEM(((n_dp - 1) * block, width), BF16) for width in widths]
        + [pltpu.VMEM((min(2 if fused else 4, len(pieces)), rows, max(width for _, _, width in pieces)), BF16)]
        + [pltpu.VMEM(value.shape, value.dtype) for value in later]
        + [pltpu.VMEM((2,) + small, F32), pltpu.VMEM((2,) + small, F32), pltpu.VMEM((n_dp,) + small, F32),
           pltpu.VMEM((n_col, block, 2 * STATE), F32), pltpu.VMEM((block, 2 * STATE), BF16),
           pltpu.SemaphoreType.DMA((2, len(pieces) * (n_dp + 1))), pltpu.SemaphoreType.DMA((2, n_dp + n_col)),
           pltpu.SemaphoreType.DMA((2, n_col + n_dp + 2)), pltpu.SemaphoreType.DMA((2, n_col)),
           pltpu.SemaphoreType.DMA((len(later),)), pltpu.VMEM(small, F32)]
        + ([pltpu.VMEM((here, tokens), F32), pltpu.VMEM((here, tokens), BF16), pltpu.VMEM((here, tokens), BF16), pltpu.VMEM((1, rows, 128), F32),
            pltpu.VMEM((here, 128), F32), pltpu.VMEM((1, tokens), F32)] if has_gn else [])
        + ([pltpu.VMEM((widths[0], tokens), BF16), pltpu.VMEM((8, (CONV + 1) * 2 * STATE), F32), pltpu.VMEM((2 * STATE, Q), F32),
            pltpu.VMEM((2 * STATE, Q), BF16), pltpu.VMEM((channels + 2 * STATE, Q), BF16), pltpu.VMEM((2 * STATE, Q), F32),
            pltpu.VMEM((CONV + 1, 2 * STATE, Q), F32), pltpu.VMEM((CONV + 1, 2 * STATE, Q), F32), pltpu.VMEM((2, 2 * STATE, Q), F32),
            pltpu.SemaphoreType.DMA((2, 2))] if fused else []),
        compiler_params=pltpu.CompilerParams(vmem_limit_bytes=60 * 1024 * 1024, collective_id=1, has_side_effects=True),
        cost_estimate=pl.CostEstimate(flops=10**6, bytes_accessed=10**8, transcendentals=0),
        name="close",
    )(*lefts, *([] if fused else [gbd]), *given, *extra, *later)
    count = len(sources)
    return out[:count], out[count], out[count + 1], out[count + 2], out[count + 3] if has_gn else None


def last_kernel(n_row, n_dp, n_col, heads, n_z, bd, x, state, small, *refs):
    refs = list(refs)
    take = lambda count: [refs.pop(0) for _ in range(count)]
    z_parts = take(n_z)
    norm_gain, inner, state_out, step, taps, bias, bc_taps, bc_bias, step_bias, decay, skip, gate = refs
    block = x.shape[0]
    at, channels = 0, inner.shape[2]
    for part in z_parts:
        count = min(part.shape[1], channels - at)
        inner[0, :, at : at + count] = part[:, :count]
        at += count
    inner[1] = x[:, :channels]
    for r in range(n_row):
        for d in range(n_dp):
            state_out[(d * n_row + r) * block : (d * n_row + r + 1) * block, :] = state[
                (r * n_dp + d) * block : (r * n_dp + d + 1) * block, :].astype(F32)
    step[...] = jnp.transpose(bd[:, 2 * STATE :])[:heads]
    by_col = lambda k: jnp.concatenate([small[c, k : k + 1, :channels] for c in range(n_col)], 1)
    for k in range(CONV):
        taps[k : k + 1, :] = by_col(CONV - 1 - k)
    bias[...] = by_col(CONV)
    gate[...] = by_col(CONV + 1)
    over = lambda k, at, count: sum(small[c, k : k + 1, at : at + count] for c in range(n_col))
    norm_gain[...] = over(6, 0, norm_gain.shape[1])
    for k in range(CONV):
        bc_taps[k : k + 1, :] = over(7, (CONV - 1 - k) * 2 * STATE, 2 * STATE)
    bc_bias[...] = over(7, CONV * 2 * STATE, 2 * STATE)
    for k, target in enumerate((step_bias, decay, skip)):
        target[...] = over(8, k * 128, 128)[:, : target.shape[1]]


def last(bd, x, state, small, z_parts, heads, channels):
    n_row, n_dp, n_col = (lax.axis_size(axis) for axis in ("row", "dp", "col"))
    block = x.shape[0]
    width = state.shape[0]
    row = lambda count: shape(F32, 1, count)
    return pl.pallas_call(
        functools.partial(last_kernel, n_row, n_dp, n_col, heads, len(z_parts)),
        out_shape=[row(width), shape(F32, 2, block, channels), shape(F32, width, 2 * STATE), shape(F32, heads, block),
                   shape(F32, CONV, n_col * channels), row(n_col * channels), shape(F32, CONV, 2 * STATE), row(2 * STATE),
                   row(n_col * heads), row(n_col * heads), row(n_col * heads), row(n_col * channels)],
        compiler_params=params(),
        cost_estimate=pl.CostEstimate(flops=10**6, bytes_accessed=10**7, transcendentals=0),
        name="last",
    )(bd, x, state, small, *z_parts)


def open_kernel(n_row, n_col, parts, hidden, inner, state_w, step_w, hx, x4, z_w, bd4, sems):
    row, col = lax.axis_index("row"), lax.axis_index("col")
    cols = [lax.rem(col + k, n_col) for k in range(n_col)]
    ahead, behind = lax.rem(row + 1, n_row), lax.rem(row + n_row - 1, n_row)
    partners = [("row", row ^ 1), ("row", row ^ 2), ("row", ahead), ("row", behind)] + [("col", c) for c in cols[1:]]
    meet(partners)
    width, tokens = hidden.shape
    each = inner.shape[0] // parts
    heads = step_w.shape[0]
    mine = pl.ds(pl.multiple_of(col * width, 16), width)
    counter = [0]
    started = []

    def start(source, target, axis, place):
        copy = far(source, target, sems, counter[0], axis, place)
        counter[0] += 1
        copy.start()
        started.append(copy)
        return copy

    rim = start(hidden.at[:, pl.ds(tokens - Q, Q)], hx.at[mine, pl.ds(0, Q)], "row", ahead)
    wide = [start(hidden, hx.at[mine, pl.ds(Q, tokens)], "col", cols[k]) for k in range(1, n_col)]
    part = lambda p: pl.ds(p * each, each)
    send = lambda p: start(x4.at[row, part(p)], x4.at[row, part(p)], "row", row ^ 2)

    def split(p):
        def body(i, _):
            at = pl.ds(p * each + i * 16, 16)
            x4[row, at, :] = inner[at, 1, :]
            z_w[at, :] = inner[at, 0, :]
            return 0

        lax.fori_loop(0, each // 16, body, 0, unroll=2)

    split(0)
    over = [send(0)]
    bd4[row, : 2 * STATE, :] = jnp.transpose(state_w[...].astype(F32)).astype(BF16)
    rest = bd4.shape[1] - 2 * STATE - heads
    bd4[row, 2 * STATE :, :] = jnp.concatenate([step_w[...], jnp.zeros((rest, step_w.shape[1]), BF16)], 0)
    bd_over = start(bd4.at[row], bd4.at[row], "row", row ^ 2)
    near = [start(bd4.at[row], bd4.at[row], "row", row ^ 1)]
    for p in range(1, parts):
        split(p)
        if p == 1:
            over.append(send(1))
    near.append(start(x4.at[row], x4.at[row], "row", row ^ 1))

    def keep_hidden(i, _):
        hx[pl.ds(pl.multiple_of(col * width + i * 16, 16), 16), pl.ds(Q, tokens)] = hidden[pl.ds(i * 16, 16), :]
        return 0

    lax.fori_loop(0, width // 16, keep_hidden, 0)
    rim.wait_recv()
    wide += [start(hx.at[mine, pl.ds(0, Q)], hx.at[mine, pl.ds(0, Q)], "col", cols[k]) for k in range(1, n_col)]
    bd_over.wait_recv()
    near.append(start(bd4.at[row ^ 2], bd4.at[row ^ 2], "row", row ^ 1))
    waited = []
    for p in range(parts):
        over[p].wait_recv()
        near.append(start(x4.at[row ^ 2, part(p)], x4.at[row ^ 2, part(p)], "row", row ^ 1))
        if p + 2 < parts:
            over[p].wait_send()
            waited.append(id(over[p]))
            over.append(send(p + 2))
    for copy in wide + near:
        copy.wait_recv()
    for copy in started:
        if id(copy) not in waited:
            copy.wait_send()


def open_up(hidden, inner, state_w, step_w):
    n_row, n_col = lax.axis_size("row"), lax.axis_size("col")
    assert n_row == 4
    channels, _, block = inner.shape
    heads = step_w.shape[0]
    parts = 4 if channels % 64 == 0 else 1
    vmem = pl.BlockSpec(memory_space=pltpu.VMEM)
    return pl.pallas_call(
        functools.partial(open_kernel, n_row, n_col, parts),
        in_specs=[vmem] * 4,
        out_specs=[vmem] * 4,
        out_shape=[shape(BF16, hidden.shape[0] * n_col, Q + hidden.shape[1]), shape(BF16, n_row, channels, block), shape(BF16, channels, block),
                   shape(BF16, n_row, 2 * STATE + heads + -heads % 32, block)],
        scratch_shapes=[pltpu.SemaphoreType.DMA((2, 5 + 2 * parts + 2 * (n_col - 1)))],
        compiler_params=pltpu.CompilerParams(vmem_limit_bytes=VMEM_LIMIT, collective_id=2, has_side_effects=True),
        cost_estimate=pl.CostEstimate(flops=0, bytes_accessed=10**8, transcendentals=0),
        name="open",
    )(hidden, inner, state_w, step_w)


def joined(w4_ref):
    return jnp.concatenate([w4_ref[j] for j in range(w4_ref.shape[0])], 1)


def by_distance(n_row, n_dp):
    row, dp = lax.axis_index("row"), lax.axis_index("dp")
    return [lax.rem(dp + k, n_dp) * n_row + (row ^ place) for place in sum_stages(n_row)[0] for k in range(n_dp)]


def put_by_distance(n_row, n_dp, source, target, skip):
    each = target.shape[0] // (n_row * n_dp)
    for k, place in enumerate(by_distance(n_row, n_dp)):
        target[k * each : (k + 1) * each, :] = source[pl.ds(pl.multiple_of(place * each, 32), each), skip:]


def project_kernel(n_row, n_dp, hb, lengths_ref, hx_ref, gain8_ref, x4_ref, bd4_ref, normed_ref, by_ref, rstd_ref, live_ref, xin_ref, bd_ref, dt_ref, gain_ref):
    @pl.when(pl.program_id(0) == 0)
    def _():
        spread(gain8_ref, gain_ref)
        width, count = hx_ref.shape

        def square(i, total):
            v = hx_ref[pl.ds(i * 16, 16), :].astype(F32)
            v = v * v
            return total + v[:8] + v[8:]

        total = lax.fori_loop(0, width // 16, square, jnp.zeros((8, count), F32), unroll=4)
        rstd = lax.rsqrt(jnp.sum(total, 0, keepdims=True) / width + EPS)
        rstd_ref[...] = jnp.broadcast_to(rstd[:, Q:], rstd_ref.shape)
        base, ends = scalars(lengths_ref, count - Q)
        live_ref[...] = (base + iota(live_ref.shape, 1) < ends[-1]).astype(F32)

        def norm(i, _):
            at = pl.ds(i * 16, 16)
            normed_ref[at, :] = (hx_ref[at, :].astype(F32) * rstd * gain_ref[0, at, 0:1]).astype(BF16)
            return 0

        lax.fori_loop(0, width // 16, norm, 0, unroll=4)
        put_by_distance(n_row, n_dp, normed_ref, by_ref, Q)
        bd = nn(joined(bd4_ref), normed_ref[...])
        bd_ref[...] = bd[: 2 * STATE]
        dt_ref[...] = jnp.zeros_like(dt_ref)
        for n in range(dt_ref.shape[0]):
            dt_ref[n, :hb, :] = bd[2 * STATE + n * hb : 2 * STATE + (n + 1) * hb, Q:]

    xin_ref[...] = nn(joined(x4_ref), normed_ref[...])


def second_kernel(n_row, n_dp, steps, hb, given, *refs):
    refs = list(refs)
    take = lambda count: [refs.pop(0) for _ in range(count)]
    far_refs = [take(2), take(2)]
    near_refs = [take(2), take(2)]
    normed, = take(1)
    grads = take(2 if given else 1)
    live, final, keep = take(3)
    z4, z, out4, gg, state_in, grad_by = take(6)
    whole_grad, come, came, kept, sems, sems_state = take(6)
    row, col = lax.axis_index("row"), lax.axis_index("col")
    n = pl.program_id(0)
    each = z4.shape[1]

    def piece(side, which, s):
        rows = pl.ds(s * each, each)
        return far(far_refs[side][which].at[rows], come.at[side, which, rows], sems, (side * 2 + which) * steps + s, "row", row ^ 1)

    def pieces(at):
        return [piece(at // steps, which, at % steps) for which in range(2)]

    def states():
        copies = []
        for k in range(1, n_row):
            there = lax.rem(row + k, n_row)
            copies.append(far(final, came.at[k - 1], sems_state, 2 * k - 2, "row", there))
            copies.append(far(keep, kept.at[k - 1], sems_state, 2 * k - 1, "row", there))
        return copies

    @pl.when(n == 0)
    def _():
        meet([("row", lax.rem(row + k, n_row)) for k in range(1, n_row)])
        for copy in states() + pieces(0) + pieces(1):
            copy.start()

    @pl.when(n == 0)
    def _():
        width = grads[0].shape[0]
        for place, source in zip((col, 1 - col) if given else (0,), grads):
            def body(i, _):
                at = pl.ds(pl.multiple_of(place * width + i * 16, 16), 16)
                whole_grad[at, :] = (source[pl.ds(i * 16, 16), :].astype(F32) * live[0:1, :]).astype(BF16)
                return 0

            lax.fori_loop(0, width // 16, body, 0, unroll=4)
        put_by_distance(n_row, n_dp, whole_grad, grad_by, 0)

    for at in range(2 * steps):
        @pl.when(n == at)
        def _():
            side = at // steps
            if at + 2 < 2 * steps:
                for copy in pieces(at + 2):
                    copy.start()
            for copy in pieces(at):
                copy.wait_recv()
            rows = slice(at % steps * each, (at % steps + 1) * each)
            w4, out = ((z4, z), (out4, gg))[side]
            w4[row] = near_refs[side][0][...]
            w4[row ^ 2] = near_refs[side][1][...]
            w4[row ^ 1] = come[side, 0, rows, :]
            w4[row ^ 3] = come[side, 1, rows, :]
            value = normed[:, Q:] if side == 0 else whole_grad[...]
            out[...] = nn(joined(w4), value)

    @pl.when(n == 2 * steps - 1)
    def _():
        for copy in states():
            copy.wait_recv()
        for head in range(final.shape[0] // HEADDIM):
            at = slice(head * HEADDIM, (head + 1) * HEADDIM)
            total, decay = None, None
            for k in range(1, n_row):
                part = jnp.where(row >= k, came[k - 1, at, :].astype(F32), 0.0)
                total = part if total is None else total + decay * part
                passing = kept[k - 1, head // hb, head % hb : head % hb + 1, :]
                decay = passing if decay is None else decay * passing
            state_in[at, :] = total
        for copy in states():
            copy.wait_send()
        for at in range(2 * steps):
            for copy in pieces(at):
                copy.wait_send()


def placed(value, index, count):
    out = jnp.zeros((count,) + value.shape, F32)
    return lax.dynamic_update_slice(out, value[None], (index,) + (0,) * value.ndim)


def turned(value, axis):
    return lax.all_gather(value, axis, axis=0, tiled=True)


def per_device(hidden_in, grad_out, lengths, norm_gain, inner_proj, state_proj, step_proj, conv_inner, conv_inner_bias,
               conv_state, conv_state_bias, step_bias, decay_log, skip_gain, gate_gain, out_proj):
    cols_here, rows = hidden_in.shape
    ncols = lax.axis_size("col")
    nrow = lax.axis_size("row")
    width = cols_here * ncols
    inner = inner_proj.shape[0]
    heads = step_proj.shape[0]
    col_index = lax.axis_index("col")
    nc = rows // Q
    hb = max(k for k in (1, 2, 3, 4) if heads % k == 0)
    nb = heads // hb
    bh = hb * HEADDIM


    gain_full = norm_gain.astype(F32)
    gain8 = jnp.broadcast_to(gain_full[None], (8, width))
    hx, x4, z_w, bd4 = open_up(hidden_in, inner_proj, state_proj, step_proj)
    out_w, grad_now, hx = lax.optimization_barrier((out_proj, grad_out, hx))
    z_far = swapped(z_w, "row", 2)
    z_far, out_w = lax.optimization_barrier((z_far, out_w))
    out_far = swapped(out_w, "row", 2)
    if ncols == 2:
        grads = [grad_now, swapped(grad_now, "col", 1)]
    else:
        grads = [lax.all_gather(grad_now, "col", axis=0, tiled=True)]

    bm = 2 * bh if nb % 2 == 0 else bh
    part4 = pl.BlockSpec((nrow, bm, width // nrow), lambda n: (0, n, 0))
    ext = rows + Q
    normed_ext, normed_by, rstd8, live8, xin, bdin, dt = pl.pallas_call(
        functools.partial(project_kernel, nrow, lax.axis_size("dp"), hb),
        grid=(inner // bm,),
        in_specs=[SMEM, whole(width, ext), whole(8, width), part4, whole(*bd4.shape)],
        out_specs=[whole(width, ext), whole(width, rows), whole(8, rows), whole(8, rows), pl.BlockSpec((bm, ext), lambda n: (n, 0)), whole(2 * STATE, ext), whole(nb, 8, rows)],
        out_shape=[shape(BF16, width, ext), shape(BF16, width, rows), shape(F32, 8, rows), shape(F32, 8, rows), shape(F32, inner, ext), shape(F32, 2 * STATE, ext), shape(F32, nb, 8, rows)],
        compiler_params=params(),
        scratch_shapes=[pltpu.VMEM((1, width, Q), F32)],
        cost_estimate=pl.CostEstimate(flops=8 * 10**9, bytes_accessed=20 * 10**6, transcendentals=0),
        name="project",
    )(lengths, hx, gain8, x4, bd4)
    rstd_in = rstd8[:1]
    by_head = jnp.pad(jnp.stack([step_bias, decay_log, skip_gain]), ((0, 5), (0, 128 - heads)))

    def taps_of(taps, bias):
        return jnp.pad(jnp.concatenate([taps, bias[None]], axis=0).astype(F32), ((0, 7 - CONV), (0, 0)))

    taps = taps_of(conv_inner, conv_inner_bias)
    bctaps = taps_of(conv_state, conv_state_bias)
    gate = jnp.broadcast_to(gate_gain.astype(F32)[None], (8, inner))

    tok = pl.BlockSpec((bh, rows), lambda n: (n, 0))
    tok_ext = pl.BlockSpec((bh, rows + Q), lambda n: (n, 0))
    eight = pl.BlockSpec((8, bh), lambda n: (0, n))
    bc_ext = pl.BlockSpec((2 * STATE, rows + Q), lambda n: (0, 0))
    state_spec = pl.BlockSpec((bh, STATE), lambda n: (n, 0))
    chunks = pl.BlockSpec((nc, bh, STATE), lambda n: (0, n, 0))
    rows_spec = pl.BlockSpec((1, 6, 8, rows), lambda n: (n, 0, 0, 0))
    head_tok = pl.BlockSpec((1, 8, rows), lambda n: (n, 0, 0))
    head_q = pl.BlockSpec((1, 8, Q), lambda n: (n, 0, 0))
    head8 = pl.BlockSpec((1, 8, 8), lambda n: (n, 0, 0))

    u, ubc, bc, rowpack, scores, y_in, fresh, final, keep, hpar = pl.pallas_call(
        functools.partial(enter_kernel, nc, hb),
        grid=(nb,),
        in_specs=[SMEM, tok_ext, bc_ext, whole(nb, 8, rows), whole(8, 128), eight, whole(8, 2 * STATE),
                  pl.BlockSpec(memory_space=pl.ANY)],
        out_specs=[tok, whole(2 * STATE, rows), whole(2 * STATE, rows), whole(nb, 6, 8, rows), whole(nc, Q, Q), tok, chunks,
                   state_spec, whole(nb, 8, Q), whole(nb, 8, 8)],
        out_shape=[shape(F32, inner, rows), shape(F32, 2 * STATE, rows), shape(F32, 2 * STATE, rows),
                   shape(F32, nb, 6, 8, rows), shape(F32, nc, Q, Q), shape(F32, inner, rows), shape(F32, nc, inner, STATE),
                   shape(BF16, inner, STATE), shape(F32, nb, 8, Q), shape(F32, nb, 8, 8)],
        scratch_shapes=[pltpu.VMEM((bh, STATE), F32), pltpu.VMEM((CONV + 1, bh, Q), F32), pltpu.VMEM((CONV + 1, 2 * STATE, Q), F32)],
        compiler_params=params(),
        cost_estimate=pl.CostEstimate(flops=3 * 10**10, bytes_accessed=40 * 10**6, transcendentals=0),
        name="enter",
    )(lengths, xin, bdin, dt, by_head, taps, bctaps, z_far)

    steps = inner // bm
    block = pl.BlockSpec((bm, width // nrow), lambda n: (jnp.minimum(n, steps - 1), 0))
    block_after = pl.BlockSpec((bm, width // nrow), lambda n: (jnp.maximum(n - steps, 0), 0))
    anywhere = pl.BlockSpec(memory_space=pl.ANY)
    second = pl.pallas_call(
        functools.partial(second_kernel, nrow, lax.axis_size("dp"), steps, hb, ncols == 2),
        grid=(2 * steps,),
        in_specs=[anywhere] * 4 + [block] * 2 + [block_after] * 2 + [whole(width, ext)] + [whole(*value.shape) for value in grads]
        + [whole(8, rows), whole(inner, STATE), whole(nb, 8, Q)],
        out_specs=[pl.BlockSpec((nrow, bm, width // nrow), lambda n: (0, jnp.minimum(n, steps - 1), 0)),
                   pl.BlockSpec((bm, rows), lambda n: (jnp.minimum(n, steps - 1), 0)),
                   pl.BlockSpec((nrow, bm, width // nrow), lambda n: (0, jnp.maximum(n - steps, 0), 0)),
                   pl.BlockSpec((bm, rows), lambda n: (jnp.maximum(n - steps, 0), 0)),
                   whole(inner, STATE), whole(width, rows)],
        out_shape=[shape(BF16, nrow, inner, width // nrow), shape(F32, inner, rows)] * 2 + [shape(F32, inner, STATE), shape(BF16, width, rows)],
        scratch_shapes=[pltpu.VMEM((width, rows), BF16), pltpu.VMEM((2, 2, inner, width // nrow), BF16), pltpu.VMEM((nrow - 1, inner, STATE), BF16),
                        pltpu.VMEM((nrow - 1, nb, 8, Q), F32), pltpu.SemaphoreType.DMA((2, 4 * steps)),
                        pltpu.SemaphoreType.DMA((2, 2 * (nrow - 1)))],
        compiler_params=pltpu.CompilerParams(vmem_limit_bytes=VMEM_LIMIT, collective_id=3, has_side_effects=True),
        cost_estimate=pl.CostEstimate(flops=10**10, bytes_accessed=30 * 10**6, transcendentals=0),
        name="second",
    )(z_w, z_far, out_w, out_far, z_w, z_far, out_w, out_far, normed_ext, *grads, live8, final, keep)
    z4, z, out4, grad_gated, state_in, grad_by = second

    y, states, stats = pl.pallas_call(
        functools.partial(across_kernel, nc, hb),
        grid=(nb,),
        in_specs=[tok, chunks, state_spec, whole(2 * STATE, rows), rows_spec, tok, tok, eight],
        out_specs=[tok, chunks, whole(2, 8, rows)],
        out_shape=[shape(F32, inner, rows), shape(F32, nc, inner, STATE), shape(F32, 2, 8, rows)],
        scratch_shapes=[pltpu.VMEM((bh, STATE), F32), pltpu.VMEM((1, bh, Q), F32)],
        compiler_params=params(),
        cost_estimate=pl.CostEstimate(flops=10**10, bytes_accessed=35 * 10**6, transcendentals=0),
        name="across",
    )(y_in, fresh, state_in, bc, rowpack, z, grad_gated, gate)

    sums = col_sum(jnp.sum(stats, axis=1))
    inner_width = inner * ncols
    rstd_gate = lax.rsqrt(sums[0] / inner_width + EPS)
    pull = rstd_gate * rstd_gate * rstd_gate * (sums[1] / inner_width)
    token_rows = jnp.concatenate([rstd_gate[None], pull[None], jnp.zeros((6, rows), F32)], axis=0)

    gated, grad_z, grad_y, adj, adj_first, ggate = pl.pallas_call(
        functools.partial(gate_kernel, nc, hb),
        grid=(nb,),
        in_specs=[tok, tok, tok, whole(8, rows), eight, whole(2 * STATE, rows), rows_spec],
        out_specs=[tok, tok, tok, chunks, state_spec, eight],
        out_shape=[shape(BF16, inner, rows), shape(BF16, inner, rows), shape(F32, inner, rows),
                   shape(F32, nc, inner, STATE), shape(BF16, inner, STATE), shape(F32, 8, inner)],
        scratch_shapes=[pltpu.VMEM((bh, STATE), F32), pltpu.VMEM((bh, Q), F32), pltpu.VMEM((1, bh, Q), F32)],
        compiler_params=params(),
        cost_estimate=pl.CostEstimate(flops=10**10, bytes_accessed=40 * 10**6, transcendentals=0),
        name="gate",
    )(y, z, grad_gated, token_rows, gate, bc, rowpack)

    adj_in = chained(adj_first, keep, hb, -1)
    def turned_product(w4, value):
        return lax.dot_general(w4, value, (((1,), (0,)), ((), ())), preferred_element_type=F32).reshape(-1, rows)

    def halves_of_features(products):
        return [sum(turned_product(lax.dynamic_slice_in_dim(w4, at * (nrow // 2), nrow // 2, 0), value) for w4, value in products)
                for at in (1 - col_index, col_index)]

    if ncols == 2:
        mixed_other, mixed = halves_of_features([(out4, gated)])
        mixed_come = swapped(mixed_other.astype(BF16), "col", 1)

    n_dp = lax.axis_size("dp")
    early, grads_early, first_z = {}, [], 0
    if nb >= 5 and inner % 768 == 0:
        first_z = inner // 3
        grads_early = [nt(grad_by, gated).astype(BF16), nt(normed_by, grad_z[:first_z]).astype(BF16)]
        each = inner // 6
        places = [(0, k * each, each) for k in range(6)] + [(1, k * each, each) for k in range(2)]
        early = {"pieces": places, "groups": [(2 * k, 2 * k + 1) for k in range(4)], "steps": nb}
    quarter = width // 4
    once = pl.Buffered(1)
    held = pl.BlockSpec(memory_space=pltpu.VMEM)
    back_out = pl.pallas_call(
        functools.partial(back_kernel, nc, hb, heads, early, n_dp),
        grid=(nb,),
        in_specs=[SMEM, tok, tok_ext, tok, tok, chunks, chunks, state_spec, whole(2 * STATE, rows), whole(nc, Q, Q), rows_spec, head8, eight]
        + [pl.BlockSpec(value.shape, lambda n: (0, 0), pipeline_mode=once) for value in grads_early],
        out_specs=[tok, pl.BlockSpec((bh, Q), lambda n: (n, 0)), pl.BlockSpec((bh, Q), lambda n: (n, 0)), eight, head_tok,
                   whole(nc, Q, Q), whole(2 * STATE, rows), whole(8, Q)] + [whole(quarter // n_dp, value.shape[1]) for value in grads_early],
        out_shape=[shape(BF16, inner, rows), shape(F32, inner, Q), shape(BF16, inner, Q), shape(F32, 8, inner), shape(F32, nb, 8, rows),
                   shape(F32, nc, Q, Q), shape(F32, 2 * STATE, rows), shape(F32, 8, Q)]
        + [shape(F32, quarter // n_dp, value.shape[1]) for value in grads_early],
        scratch_shapes=[pltpu.VMEM((bh, STATE), F32), pltpu.VMEM((bh, Q), F32), pltpu.VMEM((CONV + 1, bh, Q), F32),
                        pltpu.VMEM((5, nb, 8, rows), F32), pltpu.VMEM((CONV + 1, bh, Q), F32), pltpu.VMEM((2, bh, Q), F32)]
        + ([pltpu.VMEM((8, 2 * quarter, each), BF16), pltpu.VMEM((8, quarter, each), BF16),
            pltpu.VMEM((8, quarter // n_dp * (n_dp - 1), each), BF16), pltpu.SemaphoreType.DMA((2, 8 * (n_dp + 1)))] if early else []),
        compiler_params=pltpu.CompilerParams(vmem_limit_bytes=VMEM_LIMIT, collective_id=4, has_side_effects=True) if early else params(),
        cost_estimate=pl.CostEstimate(flops=6 * 10**10, bytes_accessed=50 * 10**6, transcendentals=0),
        name="back",
    )(lengths, u, xin, grad_y, y, states, adj, adj_in, bc, scores, rowpack, hpar, taps, *grads_early)
    gx, gx_last, rim_x, gtaps, gdt, gscores, gbct, hsum = back_out[:8]
    if ncols == 2:
        mixed_come, gx = lax.optimization_barrier((mixed_come, gx))

    if ncols == 2:
        mixed = mixed + mixed_come.astype(F32)
    else:
        mixed = lax.psum_scatter(turned_product(out4, gated).astype(BF16), "col", scatter_dimension=0, tiled=True).astype(F32)
    hidden_f = hidden_in.astype(F32)
    block_out = (hidden_f + live8[:1] * mixed).astype(BF16)

    small_width = -(-(2 * STATE + heads) // 128) * 128
    fused = ncols == 2 and bool(early)
    each = inner // 6 if inner % 768 == 0 else inner + -inner % 128
    sources = [(0, 0, None), (0, 0, 0), (0, first_z, 1)]
    pieces = [(0, 0, 2 * STATE), (0, 2 * STATE, small_width - 2 * STATE)]
    z_pieces = [(2, at, each) for at in range(0, inner - first_z, each)]
    x_pieces = [(1, at, each) for at in range(0, inner, each)]
    if inner % 768 == 0:
        x_pieces[-1:] = [(1, inner - each, each // 2), (1, inner - each // 2, each // 2)]
    pieces = z_pieces + pieces + x_pieces if fused else pieces + z_pieces + x_pieces
    gbd = None
    if not fused:
        vmem = pl.BlockSpec(memory_space=pltpu.VMEM)
        gbc, gbc_last, rim_bc, gbctaps = pl.pallas_call(
            functools.partial(state_kernel, nc),
            grid=(1,),
            out_shape=[shape(BF16, 2 * STATE, rows), shape(F32, 2 * STATE, Q), shape(BF16, 2 * STATE, Q),
                       shape(F32, 8, (CONV + 1) * 2 * STATE)],
            in_specs=[SMEM, vmem, vmem, bc_ext, vmem, vmem, vmem],
            out_specs=[vmem] * 4,
            scratch_shapes=[pltpu.VMEM((2 * STATE, Q), F32), pltpu.VMEM((CONV + 1, 2 * STATE, Q), F32),
                            pltpu.VMEM((CONV + 1, 2 * STATE, Q), F32), pltpu.VMEM((2, 2 * STATE, Q), F32)],
            compiler_params=params(),
            cost_estimate=pl.CostEstimate(flops=10**9, bytes_accessed=6 * 10**6, transcendentals=0),
            name="state",
        )(lengths, bc, ubc, bdin, bctaps, gscores, gbct)

        def last_tokens(value, last, rim):
            return lax.dynamic_update_slice(value, (last + rim.astype(F32)).astype(BF16), (0, rows - Q))

        back_x, back_bc = from_before(rim_x, -1), from_before(rim_bc, -1)
        gx = last_tokens(gx, gx_last, back_x)
        gbd = jnp.concatenate([last_tokens(gbc, gbc_last, back_bc), gdt[:, :hb].reshape(heads, rows).astype(BF16),
                               jnp.zeros((bd4.shape[1] - 2 * STATE - heads, rows), BF16)], axis=0)

        gbd_padded = jnp.pad(gbd, ((0, small_width - gbd.shape[0]), (0, 0)))
    lefts, later = [normed_by], [gx, grad_z]
    if ncols == 2:
        later += [x4, z4, bd4, hx, grad_out]
        gn_given, plain = (gain8, rstd8), None
        if fused:
            later += [rim_x, gx_last, bc, ubc, bdin, bctaps, gscores, gbct, gdt]
    else:
        grad_normed = turned_product(z4, grad_z) + turned_product(x4, gx) + turned_product(bd4, gbd)
        whole_rows = hx[:, Q:].astype(F32) * rstd_in
        gain_here = lax.dynamic_slice_in_dim(gain_full, col_index * cols_here, cols_here)[:, None]
        gn_given, plain = None, (jnp.sum(whole_rows * gain_full[:, None] * grad_normed, axis=0)[None], jnp.sum(whole_rows * grad_normed, axis=1)[None])
        gn_here = lax.psum_scatter(grad_normed.astype(BF16), "col", scatter_dimension=0, tiled=True).astype(F32)
    if not early:
        sources.append((1, 0, len(later)))
        lefts.append(grad_by)
        later.append(gated)
        pieces += [(3, at, each) for at in range(0, inner, each)]
    sums, state_out, small_out, stat_out, grad_in = close(
        sources, pieces, lefts, None if fused else gbd_padded, (lengths, gtaps, ggate, hsum) if fused else (gtaps, ggate, gbctaps, hsum),
        gn_given, plain, later, (nc, hb, len(later)) if fused else ())
    if ncols != 2:
        stat_total = jnp.sum(stat_out, axis=0)
        grad_in = (grad_out.astype(F32) + rstd_in * gain_here * gn_here - hidden_f * (rstd_in * rstd_in) * (stat_total / width)).astype(BF16)
    g_out = back_out[8] if early else sums[3][:, :inner]
    (g_norm_gain, g_inner, g_state, g_step, g_taps, g_bias, g_bc_taps, g_bc_bias, g_step_bias, g_decay, g_skip, g_gate) = last(
        sums[0], sums[1], state_out, small_out, [back_out[9], sums[2]] if early else [sums[2]], heads, inner)
    return (
        block_out,
        grad_in,
        g_norm_gain[0],
        jnp.transpose(g_inner, (2, 0, 1)),
        g_state,
        g_step,
        g_taps,
        g_bias[0],
        g_bc_taps,
        g_bc_bias[0],
        g_step_bias[0],
        g_decay[0],
        g_skip[0],
        g_gate[0],
        g_out.T,
    )


def solution(mesh):
    col, tokens, sums = P("col"), P("col", ("dp", "row")), P("col", ("dp", "row"))
    return jax.shard_map(
        per_device,
        mesh=mesh,
        in_specs=(tokens, tokens, P("dp", None), P(), P("col", None, "row"), P("row", None), P("col", "row"),
                  P(None, "col"), col, P(), P(), col, col, col, col, P("col", "row")),
        out_specs=(tokens, tokens, P(), P("col", None, ("dp", "row")), P(), sums, P(), P(), P(), P(), P(), P(), P(), P(), sums),
        check_vma=False,
    )
```

```python
import functools

import jax
import jax.numpy as jnp
from jax import lax
from jax.experimental import pallas as pl
from jax.experimental.pallas import tpu as pltpu
from jax.sharding import PartitionSpec as P

HEADDIM = 64
STATE = 128
CONV = 4
Q = 128
EPS = 1e-05
LOG2E = 1.4426950408889634
F32 = jnp.float32
BF16 = jnp.bfloat16
HIGHEST = lax.Precision.HIGHEST
MESH = pl.DeviceIdType.MESH
VMEM_LIMIT = 56 * 1024 * 1024
CUM, STEP, ENTRY, TAIL, DEC, SIG = range(6)


def nn(a, b, precision=None):
    return lax.dot_general(a, b, (((1,), (0,)), ((), ())), precision=precision, preferred_element_type=F32)


def nt(a, b, precision=None):
    return lax.dot_general(a, b, (((1,), (1,)), ((), ())), precision=precision, preferred_element_type=F32)


def tn(a, b, precision=None):
    return lax.dot_general(a, b, (((0,), (0,)), ((), ())), precision=precision, preferred_element_type=F32)


def halves(v):
    high = v.astype(BF16)
    return high, (v - high.astype(F32)).astype(BF16)


def nn3(a, b):
    (ah, al), (bh, bl) = halves(a), halves(b)
    return nn(jnp.concatenate([ah, ah, al], 1), jnp.concatenate([bh, bl, bh], 0))


def nt3(a, b):
    (ah, al), (bh, bl) = halves(a), halves(b)
    return nt(jnp.concatenate([ah, ah, al], 1), jnp.concatenate([bh, bl, bh], 1))


def sigm(v):
    return 0.5 + 0.5 * jnp.tanh(0.5 * v)


def iota(shape, dim):
    return lax.broadcasted_iota(jnp.int32, shape, dim)


def segment_of(place, ends):
    total = (place >= ends[0]).astype(jnp.int32)
    for end in ends[1:]:
        total = total + (place >= end).astype(jnp.int32)
    return jnp.where(place < 0, -1, total)


def chunk_of(c):
    return pl.ds(pl.multiple_of(c * Q, Q), Q)


def shift_masks(place, ends):
    segment = segment_of(place, ends)
    return [(segment_of(place - d, ends) == segment).astype(F32) for d in range(1, CONV)]


def shifted_right(now, earlier, d, lane):
    return pltpu.roll(jnp.where(lane >= Q - d, earlier, now), d, 1)


def shifted_left(now, later, d, lane):
    return pltpu.roll(jnp.where(lane < d, later, now), Q - d, 1)


def conv_tile(now, earlier, taps, masks, lane):
    total = taps(CONV) + taps(CONV - 1) * now
    for d in range(1, CONV):
        total = total + taps(CONV - 1 - d) * (shifted_right(now, earlier, d, lane) * masks[d - 1])
    return total


def spread(rows_ref, out):
    cols = jnp.transpose(rows_ref[...])
    for k in range(out.shape[0]):
        out[k] = jnp.broadcast_to(cols[:, k : k + 1], out.shape[1:])


def thirds(v):
    high, rest = v.astype(BF16), v
    rest = rest - high.astype(F32)
    middle = rest.astype(BF16)
    return jnp.concatenate([high, middle, (rest - middle.astype(F32)).astype(BF16)], -1)


def times_flags(v, flags):
    return nn(thirds(v), jnp.concatenate([flags.astype(BF16)] * 3, 0))


def stacked(v, count):
    return jnp.concatenate([v[:, c * Q : (c + 1) * Q] for c in range(count)], 0)


def scalars(lengths_ref, rows):
    ends = [lengths_ref[0, 0]]
    for k in range(1, lengths_ref.shape[1]):
        ends.append(ends[-1] + lengths_ref[0, k])
    return lax.axis_index("row") * rows, ends


def enter_kernel(nc, hb, place_ref, xin_ref, bcin_ref, dt_ref, heads_ref, taps8_ref, bctaps8_ref, wait_ref,
                 u_ref, ubc_ref, bc_ref, rows_ref, scores_ref, y_ref, fresh_ref, final_ref, pass_ref, hpar_ref, state, taps_ref, bctaps_ref):
    base, ends = scalars(place_ref, nc * Q)
    wide = iota((HEADDIM, Q), 1)
    block = pl.program_id(0)
    spread(taps8_ref, taps_ref)

    @pl.when(block == 0)
    def _():
        spread(bctaps8_ref, bctaps_ref)
        lane = iota((1, Q), 1)
        row, col = iota((Q, Q), 0), iota((Q, Q), 1)

        def body(c, _):
            masks = shift_masks(base + c * Q + lane, ends)
            for part in range(2 * STATE // HEADDIM):
                at = slice(part * HEADDIM, (part + 1) * HEADDIM)
                u = conv_tile(bcin_ref[at, chunk_of(c + 1)], bcin_ref[at, chunk_of(c)], lambda k: bctaps_ref[k, at, :], masks, wide)
                ubc_ref[at, chunk_of(c)] = u
                bc_ref[at, chunk_of(c)] = u * sigm(u)
            start = base + c * Q
            same = (segment_of(start + row, ends) == segment_of(start + col, ends)) & (row >= col)
            score = nn3(jnp.transpose(bc_ref[STATE:, chunk_of(c)]), bc_ref[:STATE, chunk_of(c)])
            scores_ref[c] = jnp.where(same, score, 0.0)
            return 0

        lax.fori_loop(0, nc, body, 0, unroll=2)

        nb = dt_ref.shape[0]
        by_head = jnp.transpose(heads_ref[...])[:, :8]
        for n in range(nb):
            own = by_head[n * hb : (n + 1) * hb]
            hpar_ref[n] = own if hb == 8 else jnp.concatenate([own, jnp.zeros((8 - hb, 8), F32)], 0)
        raw = jnp.concatenate([dt_ref[n] + hpar_ref[n, :, 0:1] for n in range(nb)], 0)
        rate = jnp.concatenate([-jnp.exp(hpar_ref[n, :, 1:2]) for n in range(nb)], 0)
        small = jnp.exp(-jnp.abs(raw))
        steps = jnp.maximum(raw, 0.0) + jnp.log1p(small)
        sig = jnp.where(raw >= 0, 1.0, small) / (1.0 + small)
        each = nb * 8
        cums = times_flags(stacked(steps * rate * LOG2E, nc), row <= col)
        whole_sum = jnp.zeros((each, 1), F32)
        for c in range(nc):
            at = slice(c * Q, (c + 1) * Q)
            start = base + c * Q
            segment = segment_of(start + lane, ends)
            before = segment_of(start - 1, ends)
            after = segment_of(start + Q - 1, ends)
            cum = cums[c * each : (c + 1) * each]
            last = cum[:, Q - 1 : Q]
            entry = jnp.exp2(cum) * (segment == before).astype(F32)
            tail = jnp.exp2(last - cum) * (segment == after).astype(F32)
            decay = jnp.broadcast_to(jnp.exp2(last), (each, Q)) * (before == after).astype(F32)
            for n in range(nb):
                part = slice(n * 8, (n + 1) * 8)
                rows_ref[n, CUM, :, at] = cum[part]
                rows_ref[n, STEP, :, at] = steps[part, at]
                rows_ref[n, ENTRY, :, at] = entry[part]
                rows_ref[n, TAIL, :, at] = tail[part]
                rows_ref[n, DEC, :, at] = decay[part]
                rows_ref[n, SIG, :, at] = sig[part, at]
            whole_sum = whole_sum + last
        end = segment_of(base + nc * Q - 1, ends)
        keep = jnp.broadcast_to(jnp.exp2(whole_sum), (each, Q)) * (segment_of(base - 1, ends) == end).astype(F32)
        for n in range(nb):
            pass_ref[n] = keep[n * 8 : (n + 1) * 8]

    state[...] = jnp.zeros_like(state)

    def chunk(c, _):
        now = chunk_of(c)
        masks = shift_masks(base + c * Q + iota((1, Q), 1), ends)
        cum8 = rows_ref[block, CUM, :, now]
        cols = jnp.transpose(cum8)
        weighted = []
        for h in range(hb):
            at = slice(h * HEADDIM, (h + 1) * HEADDIM)
            hr = slice(h, h + 1)
            u = conv_tile(xin_ref[at, chunk_of(c + 1)], xin_ref[at, now], lambda k: taps_ref[k, at, :], masks, wide)
            u_ref[at, now] = u
            x = u * sigm(u)
            moved = x * rows_ref[block, STEP, hr, now]
            decay = jnp.exp2(jnp.minimum(cols[:, hr] - cum8[hr, :], 0.0))
            mixing = (decay * scores_ref[c]).astype(BF16)
            y_ref[at, now] = nt(moved.astype(BF16), mixing) + hpar_ref[block, hr, 2:3] * x
            weighted.append((moved * rows_ref[block, TAIL, hr, now]).astype(BF16))
        fresh = nt(jnp.concatenate(weighted, 0), bc_ref[:STATE, now].astype(BF16))
        fresh_ref[c] = fresh
        for h in range(hb):
            at = slice(h * HEADDIM, (h + 1) * HEADDIM)
            state[at, :] = state[at, :] * rows_ref[block, DEC, h : h + 1, now] + fresh[at, :]
        return 0

    lax.fori_loop(0, nc, chunk, 0, unroll=2)
    final_ref[...] = state[...].astype(BF16)


def across_kernel(nc, hb, y_ref, fresh_ref, start_ref, bc_ref, rows_ref, z_ref, gg_ref, gate8_ref,
                  y_out, states_ref, stat_ref, state, gate_ref):
    first = pl.program_id(0) == 0

    @pl.when(first)
    def _():
        stat_ref[...] = jnp.zeros_like(stat_ref)

    state[...] = start_ref[...]
    spread(gate8_ref, gate_ref)

    def chunk(c, _):
        states_ref[c] = state[...]
        outer = nn3(state[...], bc_ref[STATE:, chunk_of(c)])
        square = jnp.zeros((8, Q), F32)
        cross = jnp.zeros((8, Q), F32)
        for h in range(hb):
            at = slice(h * HEADDIM, (h + 1) * HEADDIM)
            y = y_ref[at, chunk_of(c)] + outer[at, :] * rows_ref[0, ENTRY, h : h + 1, chunk_of(c)]
            y_out[at, chunk_of(c)] = y
            z = z_ref[at, chunk_of(c)]
            gz = y * (z * sigm(z))
            other = gz * gate_ref[0, at, :] * gg_ref[at, chunk_of(c)]
            squared = gz * gz
            for k in range(HEADDIM // 8):
                square = square + squared[k * 8 : (k + 1) * 8]
                cross = cross + other[k * 8 : (k + 1) * 8]
            state[at, :] = state[at, :] * rows_ref[0, DEC, h : h + 1, chunk_of(c)] + fresh_ref[c, at, :]
        stat_ref[0, :, chunk_of(c)] += square
        stat_ref[1, :, chunk_of(c)] += cross
        return 0

    lax.fori_loop(0, nc, chunk, 0, unroll=4)


def lane_sums(v):
    return nt(jnp.ones((8, 2 * Q), BF16), jnp.concatenate(halves(v), 1))


def gate_kernel(nc, hb, y_ref, z_ref, gg_ref, tok_ref, gate8_ref, bc_ref, rows_ref,
                gated_ref, gz_ref, gy_ref, adj_ref, first_ref, ggate_ref, adjoint, gsum, gate_ref):
    spread(gate8_ref, gate_ref)
    adjoint[...] = jnp.zeros_like(adjoint)
    gsum[...] = jnp.zeros_like(gsum)

    def chunk(k, _):
        c = nc - 1 - k
        rstd = tok_ref[0:1, chunk_of(c)]
        pull = tok_ref[1:2, chunk_of(c)]
        lifted = []
        for h in range(hb):
            at = slice(h * HEADDIM, (h + 1) * HEADDIM)
            y, z, gg = y_ref[at, chunk_of(c)], z_ref[at, chunk_of(c)], gg_ref[at, chunk_of(c)]
            s = sigm(z)
            silu = z * s
            gz = y * silu
            gate = gate_ref[0, at, :]
            gzr = gz * rstd
            gated_ref[at, chunk_of(c)] = (gzr * gate).astype(BF16)
            gsum[at, :] += gzr * gg
            ggz = rstd * (gate * gg) - gz * pull
            gy = ggz * silu
            gz_ref[at, chunk_of(c)] = (ggz * y * (s * (1.0 + z * (1.0 - s)))).astype(BF16)
            gy_ref[at, chunk_of(c)] = gy
            lifted.append(gy * rows_ref[0, ENTRY, h : h + 1, chunk_of(c)])
        adj = nt3(jnp.concatenate(lifted, 0), bc_ref[STATE:, chunk_of(c)])
        adj_ref[c] = adj
        for h in range(hb):
            at = slice(h * HEADDIM, (h + 1) * HEADDIM)
            adjoint[at, :] = adjoint[at, :] * rows_ref[0, DEC, h : h + 1, chunk_of(c)] + adj[at, :]
        return 0

    lax.fori_loop(0, nc, chunk, 0, unroll=4)
    first_ref[...] = adjoint[...].astype(BF16)
    ggate_ref[...] = lane_sums(gsum[...])


def conv_back(gu, later, taps, masks, lane):
    moved = [gu]
    total = taps(CONV - 1) * gu
    for d in range(1, CONV):
        part = shifted_left(gu * masks[d - 1], later * masks[CONV - 1 + d - 1], d, lane)
        moved.append(part)
        total = total + taps(CONV - 1 - d) * part
    return total, moved


def conv_rim(gu, taps, masks, lane, rim_in):
    total = jnp.zeros_like(gu)
    sums = []
    for d in range(1, CONV):
        part = pltpu.roll(jnp.where(lane < d, gu * masks[d - 1], 0.0), Q - d, 1)
        total = total + taps(CONV - 1 - d) * part
        sums.append(rim_in * part)
    return total, sums


def back_masks(base, c, ends):
    lane = iota((1, Q), 1)
    return shift_masks(base + c * Q + lane, ends) + shift_masks(base + (c + 1) * Q + lane, ends)


def total_rows(v):
    return jnp.sum(v, 0, keepdims=True)


def early_sums(early, n_dp, grads, outs, come1, come2, come3, sems):
    half = grads[0].shape[0] // 2
    views = []
    for k, (a, at, width) in enumerate(early["pieces"]):
        columns = pl.ds(at, width)
        views.append((grads[a].at[pl.ds(0, half), columns], grads[a].at[pl.ds(half, half), columns], come1.at[k], come2.at[k], come3.at[k],
                      outs[a].at[:, columns]))
    return RowSums(n_dp, views, sems)


def sent_sums(early, n_dp, grads, outs, *refs):
    sums = early_sums(early, n_dp, grads, outs, *refs)
    groups = early["groups"]
    for t in range(early["steps"]):
        @pl.when(pl.program_id(0) == t)
        def _():
            if t == 0:
                meet(sums.partners())
            for stage, lag in ((sums.along, 2), (sums.across, 1), (sums.pair, 0), (sums.finish, 3)):
                if 0 <= t - lag < len(groups):
                    for p in groups[t - lag]:
                        stage(p)


def end_sums(early, n_dp, grads, outs, *refs):
    sums = early_sums(early, n_dp, grads, outs, *refs)
    groups, steps = early["groups"], early["steps"]

    @pl.when(pl.program_id(0) == steps - 1)
    def _():
        for t in range(steps, len(groups) + 3):
            for stage, lag in ((sums.along, 2), (sums.across, 1), (sums.finish, 3)):
                if 0 <= t - lag < len(groups):
                    for p in groups[t - lag]:
                        stage(p)
        for p in range(len(early["pieces"])):
            sums.first(p).wait_send()
            sums.sent(p)


def back_kernel(nc, hb, heads, early, n_dp, place_ref, u_ref, xin_ref, gy_ref, y_ref, states_ref, adj_ref, start_ref, bc_ref, scores_ref,
                rows_ref, hpar_ref, taps8_ref, *refs):
    refs = list(refs)
    take = lambda count: [refs.pop(0) for _ in range(count)]
    arrays = 2 if early else 0
    grads = take(arrays)
    gx_ref, gxlast_ref, rim_ref, gtaps_ref, gdt_ref, gscores, gbct, hsum_ref = take(8)
    sums_out = take(arrays)
    adjoint, gnext, tapsum, hrow, taps_ref, ends_at = take(6)
    if early:
        sent_sums(early, n_dp, grads, sums_out, *refs)
    spread(taps8_ref, taps_ref)
    base, ends = scalars(place_ref, nc * Q)
    wide = iota((HEADDIM, Q), 1)
    block = pl.program_id(0)

    @pl.when(block == 0)
    def _():
        hsum_ref[...] = jnp.zeros_like(hsum_ref)
        gscores[...] = jnp.zeros_like(gscores)
        gbct[...] = jnp.zeros_like(gbct)
        hrow[...] = jnp.zeros_like(hrow)

    adjoint[...] = start_ref[...]
    gnext[...] = jnp.zeros_like(gnext)
    tapsum[...] = jnp.zeros_like(tapsum)

    def chunk(k, _):
        c = nc - 1 - k
        now = chunk_of(c)
        masks = back_masks(base, c, ends)
        from_later = nn(adjoint[...].astype(BF16), bc_ref[:STATE, now].astype(BF16))
        cum8 = rows_ref[0, CUM, :, now]
        cols = jnp.transpose(cum8)
        lifted, weighted = [], []
        for h in range(hb):
            at = slice(h * HEADDIM, (h + 1) * HEADDIM)
            hr = slice(h, h + 1)
            u = u_ref[at, now]
            gy = gy_ref[at, now]
            s = sigm(u)
            x = u * s
            step = rows_ref[0, STEP, hr, now]
            tail = rows_ref[0, TAIL, hr, now]
            moved = x * step
            moved_low = moved.astype(BF16)
            gy_low = gy.astype(BF16)
            decay = jnp.exp2(jnp.minimum(cols[:, hr] - cum8[hr, :], 0.0))
            gmix = tn(gy_low, moved_low)
            gscores[c] += gmix * decay
            gmoved = nn(gy_low, (decay * scores_ref[c]).astype(BF16))
            later = from_later[at, :] * tail
            lifted.append((gy * rows_ref[0, ENTRY, hr, now]).astype(BF16))
            weighted.append((moved * tail).astype(BF16))
            skip = hpar_ref[0, hr, 2:3]
            taken = gy_low.astype(F32) * (y_ref[at, now] - skip * x) - moved_low.astype(F32) * gmoved
            hrow[0, block, hr, now] = total_rows(taken)
            hrow[1, block, hr, now] = total_rows(moved * later)
            hrow[2, block, hr, now] = total_rows(adjoint[at, :] * states_ref[c, at, :]) * rows_ref[0, DEC, hr, now]
            gmoved = gmoved + later
            hrow[3, block, hr, now] = total_rows(x * gmoved)
            hrow[4, block, hr, now] = total_rows(x * gy)
            gx = gmoved * step + skip * gy
            gu = gx * (s * (1.0 + u * (1.0 - s)))
            gin, shifts = conv_back(gu, gnext[at, :], lambda k: taps_ref[k, at, :], masks, wide)
            gnext[at, :] = gu
            gx_ref[at, now] = gin.astype(BF16)

            ends_at[jnp.minimum(k, 1), at, :] = gin
            xin = xin_ref[at, chunk_of(c + 1)]
            for d in range(CONV):
                tapsum[d, at, :] += xin * shifts[d]
            tapsum[CONV, at, :] += gu
        gbct[STATE:, now] += tn(states_ref[c].astype(BF16), jnp.concatenate(lifted, 0))
        gbct[:STATE, now] += tn(adjoint[...].astype(BF16), jnp.concatenate(weighted, 0))
        for h in range(hb):
            at = slice(h * HEADDIM, (h + 1) * HEADDIM)
            adjoint[at, :] = adjoint[at, :] * rows_ref[0, DEC, h : h + 1, now] + adj_ref[c, at, :]
        return 0

    lax.fori_loop(0, nc, chunk, 0, unroll=2)

    gxlast_ref[...] = ends_at[0]
    masks = back_masks(base, 0, ends)
    for h in range(hb):
        at = slice(h * HEADDIM, (h + 1) * HEADDIM)
        rim, sums = conv_rim(gnext[at, :], lambda k: taps_ref[k, at, :], masks, wide, xin_ref[at, :Q])
        rim_ref[at, :] = rim.astype(BF16)
        for d in range(1, CONV):
            tapsum[d, at, :] += sums[d - 1]
    gtaps_ref[...] = jnp.concatenate([lane_sums(tapsum[d])[0:1] for d in range(CONV + 1)] + [jnp.zeros((7 - CONV, hb * HEADDIM), F32)], 0)

    row, col = iota((Q, Q), 0), iota((Q, Q), 1)
    glogs = (times_flags(stacked(hrow[0, block], nc), row >= col) + times_flags(stacked(hrow[1, block], nc), row < col)
             + times_flags(stacked(hrow[2, block], nc), row >= 0))
    rate = -jnp.exp(hpar_ref[0, :, 1:2])
    total = [jnp.zeros((8, Q), F32) for _ in range(3)]
    for c in range(nc):
        at = slice(c * Q, (c + 1) * Q)
        glog = glogs[c * 8 : (c + 1) * 8] * rate
        gdt = (hrow[3, block, :, at] + glog) * rows_ref[0, SIG, :, at]
        gdt_ref[0, :, at] = gdt
        total[0] = total[0] + gdt
        total[1] = total[1] + glog * rows_ref[0, STEP, :, at]
        total[2] = total[2] + hrow[4, block, :, at]
    sums = times_flags(jnp.concatenate(total, 0), row >= 0)
    first = lax.axis_index("col") * heads + block * hb
    lane = iota((1, Q), 1)
    for k in range(3):
        for h in range(hb):
            hsum_ref[k : k + 1, :] += jnp.where(lane == first + h, sums[k * 8 + h : k * 8 + h + 1, :], 0.0)

    if early:
        end_sums(early, n_dp, grads, sums_out, *refs)


def state_kernel(nc, place_ref, bc_ref, ubc_ref, bcin_ref, bctaps8_ref, gscores_in, gbct_in,
                 gbc_ref, gbclast_ref, bcrim_ref, gbctaps_ref, gnext, tapsum, bctaps_ref, ends_at):
    spread(bctaps8_ref, bctaps_ref)
    base, ends = scalars(place_ref, nc * Q)
    row, col = iota((Q, Q), 0), iota((Q, Q), 1)
    wide = iota((HEADDIM, Q), 1)
    gnext[...] = jnp.zeros_like(gnext)
    tapsum[...] = jnp.zeros_like(tapsum)
    tiles = [slice(k * HEADDIM, (k + 1) * HEADDIM) for k in range(2 * STATE // HEADDIM)]

    def body(k, _):
        c = nc - 1 - k
        now = chunk_of(c)
        start = base + c * Q
        same = (segment_of(start + row, ends) == segment_of(start + col, ends)) & (row >= col)
        gscore = jnp.where(same, gscores_in[c], 0.0)
        masks = back_masks(base, c, ends)
        inter = gbct_in[:, now]
        g_c = inter[STATE:] + nt3(bc_ref[:STATE, now], gscore)
        g_b = inter[:STATE] + nn3(bc_ref[STATE:, now], gscore)
        g_bc = jnp.concatenate([g_b, g_c], 0)
        for at in tiles:
            u = ubc_ref[at, now]
            s = sigm(u)
            gu = g_bc[at] * (s * (1.0 + u * (1.0 - s)))
            gin, shifts = conv_back(gu, gnext[at, :], lambda k: bctaps_ref[k, at, :], masks, wide)
            gnext[at, :] = gu
            gbc_ref[at, now] = gin.astype(BF16)

            ends_at[jnp.minimum(k, 1), at, :] = gin
            xin = bcin_ref[at, chunk_of(c + 1)]
            for d in range(CONV):
                tapsum[d, at, :] += xin * shifts[d]
            tapsum[CONV, at, :] += gu
        return 0

    lax.fori_loop(0, nc, body, 0)
    gbclast_ref[...] = ends_at[0]
    masks = back_masks(base, 0, ends)
    for at in tiles:
        rim, more = conv_rim(gnext[at, :], lambda k: bctaps_ref[k, at, :], masks, wide, bcin_ref[at, :Q])
        bcrim_ref[at, :] = rim.astype(BF16)
        for d in range(1, CONV):
            tapsum[d, at, :] += more[d - 1]
    for d in range(CONV + 1):
        gbctaps_ref[:, d * 2 * STATE : (d + 1) * 2 * STATE] = lane_sums(tapsum[d])


def whole(*shape):
    return pl.BlockSpec(shape, lambda n: (0,) * len(shape))


def params():
    return pltpu.CompilerParams(vmem_limit_bytes=VMEM_LIMIT)


SMEM = pl.BlockSpec(memory_space=pltpu.SMEM)


def shape(dtype, *dims):
    return jax.ShapeDtypeStruct(dims, dtype)


def after(value, *others):
    return lax.optimization_barrier((value,) + others)[0]


def moved(value, axis, steps):
    n = lax.axis_size(axis)
    return lax.ppermute(value, axis, [(k, (k + steps) % n) for k in range(n)])


def swapped(value, axis, bit):
    n = lax.axis_size(axis)
    return lax.ppermute(value, axis, [(k, k ^ bit) for k in range(n)])


def col_sum(value):
    if lax.axis_size("col") == 2:
        return value + swapped(value, "col", 1)
    return lax.psum(value, "col")


def from_before(value, steps):
    n = lax.axis_size("row")
    pairs = [(k, k + steps) for k in range(max(0, -steps), min(n, n - steps))]
    return lax.ppermute(value, "row", pairs)


def chained(state, keep, hb, direction):
    nb, inner = keep.shape[0], state.shape[0]
    flat = keep.reshape(nb * 8, Q)
    high, low = halves(flat)
    packed = jnp.concatenate([state, high, low], axis=0)
    total, decay = None, None
    for k in range(1, lax.axis_size("row")):
        part = from_before(packed, direction * k)
        passing = part[inner : inner + nb * 8].astype(F32) + part[inner + nb * 8 :].astype(F32)
        passing = jnp.repeat(passing.reshape(nb, 8, Q)[:, :hb].reshape(nb * hb, Q), HEADDIM, axis=0)
        part = part[:inner].astype(F32)
        total = part if total is None else total + decay * part
        decay = passing if decay is None else decay * passing
    return total


def sum_stages(n_row):
    order, bits = [0], []
    bit = n_row // 2
    while bit:
        order = [k + bit for k in order] + order
        bits.insert(0, bit)
        bit //= 2
    return order, bits


def far(source, target, sems, k, axis, place):
    return pltpu.make_async_remote_copy(
        src_ref=source, dst_ref=target, send_sem=sems.at[0, k], recv_sem=sems.at[1, k],
        device_id={axis: place}, device_id_type=MESH)


def meet(partners):
    barrier = pltpu.get_barrier_semaphore()
    for axis, place in partners:
        pl.semaphore_signal(barrier, inc=1, device_id={axis: place}, device_id_type=MESH)
    pl.semaphore_wait(barrier, len(partners))


class RowSums:
    def __init__(self, n_dp, pieces, sems):
        self.row, dp = lax.axis_index("row"), lax.axis_index("dp")
        self.n_dp, self.pieces, self.sems = n_dp, pieces, sems
        self.dps = [lax.rem(dp + k, n_dp) for k in range(n_dp)]
        self.quarter = pieces[0][3].shape[0]
        self.block = self.quarter // n_dp
        self.per = n_dp + 1

    def partners(self):
        return [("row", self.row ^ 1), ("row", self.row ^ 2)] + [("dp", d) for d in self.dps[1:]]

    def first(self, p):
        send, _, come1, _, _, _ = self.pieces[p]
        return far(send, come1, self.sems, p * self.per, "row", self.row ^ 1)

    def second(self, p):
        _, _, come1, come2, _, _ = self.pieces[p]
        return far(come1.at[pl.ds(0, self.quarter)], come2, self.sems, p * self.per + 1, "row", self.row ^ 2)

    def third(self, p):
        _, _, _, come2, come3, _ = self.pieces[p]
        block = self.block
        return [far(come2.at[pl.ds(k * block, block)], come3.at[pl.ds((k - 1) * block, block)], self.sems, p * self.per + 1 + k, "dp", self.dps[k])
                for k in range(self.n_dp - 1, 0, -1)]

    def pair(self, p):
        self.first(p).start()

    def across(self, p):
        _, kept, come1, _, _, _ = self.pieces[p]
        self.first(p).wait_recv()
        add_rows(come1, 0, kept, 0, self.quarter)
        self.second(p).start()
        add_rows(come1, self.quarter, kept, self.quarter, self.quarter)

    def along(self, p):
        _, _, come1, come2, _, _ = self.pieces[p]
        self.second(p).wait_recv()
        add_rows(come2, 0, come1, self.quarter, self.quarter)
        for copy in self.third(p):
            copy.start()

    def finish(self, p):
        _, _, _, come2, come3, out = self.pieces[p]
        for copy in self.third(p):
            copy.wait_recv()

        def body(i, _):
            at = i * 32
            total = come2[pl.ds(at, 32), :].astype(F32)
            for k in range(1, self.n_dp):
                total = total + come3[pl.ds((k - 1) * self.block + at, 32), :].astype(F32)
            out[pl.ds(at, 32), :] = total
            return 0

        lax.fori_loop(0, self.block // 32, body, 0, unroll=True)

    def sent(self, p):
        self.second(p).wait_send()
        for copy in self.third(p):
            copy.wait_send()


def add_rows(out, out_at, other, other_at, count):
    def body(i, _):
        at = i * 32
        out[pl.ds(out_at + at, 32), :] = out[pl.ds(out_at + at, 32), :] + other[pl.ds(other_at + at, 32), :]
        return 0

    lax.fori_loop(0, count // 32, body, 0, unroll=4)


def close_kernel(n_row, n_dp, n_col, sources, pieces, has_gn, fused, *refs):
    refs = list(refs)
    take = lambda count: [refs.pop(0) for _ in range(count)]
    lefts = take(1 + max(left for left, _, _ in sources))
    if fused:
        nc, hb, n_late = fused
        lengths_ref, = take(1)
        rows_given = take(3)
    else:
        gbd, = take(1)
        rows_given = take(4)
    if has_gn:
        gain8, rstd8 = take(2)
    else:
        stat, gain_row = take(2)
    later_given = take(n_late if fused else 2 + len(sources) - 3 + (5 if has_gn else 0))
    outs = take(len(sources))
    state_out, small_out, stat_out = take(3)
    if has_gn:
        grad_in, = take(1)
    come1, come2, come3 = take(len(sources)), take(len(sources)), take(len(sources))
    grad_slots, = take(1)
    later_held = take(len(later_given))
    small_a, small_b, small_c, state_a, state_b = take(5)
    sems_grad, sems_small, sems_state, sems_other, sems_local, small = take(6)
    if has_gn:
        gn_sum, gn, gn_come, gain, gsum, stat = take(6)
    if fused:
        gbd, gbctaps, gbclast, rim_bc, rims, gnext, tapsum, bctaps, ends_at, sems_rim = take(10)
        rows_given = rows_given[:2] + [gbctaps] + rows_given[2:]

    loads = [pltpu.make_async_copy(source, held, sems_local.at[k]) for k, (source, held) in enumerate(zip(later_given, later_held))]
    loading, loaded = set(), set()

    def fetch(*keys):
        for k in keys:
            if k not in loading:
                loads[k].start()
                loading.add(k)

    def held(k):
        fetch(k)
        if k not in loaded:
            loads[k].wait()
            loaded.add(k)
        return later_held[k]

    fetch(*((1, 7) if fused else range(len(loads))))

    row, dp, col = lax.axis_index("row"), lax.axis_index("dp"), lax.axis_index("col")
    dps = [lax.rem(dp + k, n_dp) for k in range(n_dp)]
    cols = [lax.rem(col + k, n_col) for k in range(n_col)]
    rows = lefts[0].shape[0]
    half, quarter = rows // 2, rows // 4
    block = quarter // n_dp
    count = len(pieces)
    slots = grad_slots.shape[0]
    views = []
    for p, (a, at, width) in enumerate(pieces):
        columns, mine = pl.ds(at, width), grad_slots.at[p % slots, :, pl.ds(0, width)]
        views.append((mine.at[pl.ds(0, half)], mine.at[pl.ds(half, half)], come1[a].at[:, columns], come2[a].at[:, columns],
                      come3[a].at[:, columns], outs[a].at[:, columns]))
    sums = RowSums(n_dp, views, sems_grad)
    ahead, behind = lax.rem(row + 1, n_row), lax.rem(row + n_row - 1, n_row)
    meet(sums.partners() + [("col", c) for c in cols[1:]] + ([("row", ahead), ("row", behind)] if fused else []))
    started = []

    def start(copy):
        copy.start()
        started.append(copy)
        return copy

    def make(p):
        a, at, width = pieces[p]
        left, first_row, right = sources[a]
        if p >= slots:
            sums.first(p - slots).wait_send()
        right = gbd if right is None else held(right)
        value = right[first_row + at : min(first_row + at + width, right.shape[0]), :]
        if value.shape[0] < width:
            value = jnp.concatenate([value, jnp.zeros((width - value.shape[0], value.shape[1]), BF16)], 0)
        for part in range(2):
            rows_here = slice(part * half, (part + 1) * half)
            grad_slots[p % slots, rows_here, :width] = nt(lefts[left][rows_here, :], value).astype(BF16)
            if part == 0:
                sums.pair(p)

    group = lambda r: pl.ds(pl.multiple_of(r * (n_dp * block), 16), n_dp * block)
    here = pl.ds(pl.multiple_of((row * n_dp + dp) * block, 16), block)
    n0 = n_col - 1
    n1 = n0 + n_dp - 1
    later = {"others": []}

    def send_rim():
        later["rim"] = start(far(held(7), rims.at[pl.ds(0, held(7).shape[0])], sems_rim, 0, "row", behind))

    def add_rim(target, last, at, count):
        tokens = target.shape[1]
        come = jnp.where(row < n_row - 1, rims[at : at + count, :].astype(F32), 0.0)
        target[:count, tokens - Q :] = (last[...] + come).astype(BF16)

    def take_rim():
        later["rim"].wait_recv()
        add_rim(held(0), held(8), 0, held(8).shape[0])

    def state_back():
        bc, ubc, bcin, bctaps8, gscores, gbct, gdt = (held(k) for k in range(9, 16))
        state_kernel(nc, lengths_ref, bc, ubc, bcin, bctaps8, gscores, gbct, gbd, gbclast, rim_bc, gbctaps, gnext, tapsum, bctaps, ends_at)
        channels = held(8).shape[0]
        later["rim_bc"] = start(far(rim_bc, rims.at[pl.ds(channels, 2 * STATE)], sems_rim, 1, "row", behind))
        steps = [gdt[n, :hb, :] for n in range(gdt.shape[0])]
        rest = gbd.shape[0] - 2 * STATE - hb * gdt.shape[0]
        gbd[2 * STATE :, :] = jnp.concatenate(steps + [jnp.zeros((rest, gdt.shape[2]), F32)], 0).astype(BF16)

    def take_rim_bc():
        later["rim_bc"].wait_recv()
        add_rim(gbd, gbclast, held(8).shape[0], 2 * STATE)

    def product(place, which):
        value, w4 = held(which), held(2 + which)
        weights = lambda w4: jnp.concatenate([w4[place * (n_row // 2) + k] for k in range(n_row // 2)], 1)
        part = tn(weights(w4), value[...])
        if which:
            gn_sum[...] = part
        else:
            bd4 = held(4)
            gn_sum[...] += part + tn(weights(bd4), gbd[: bd4.shape[1], :])

    def prepare(k, place):
        hx = held(5)
        width = gn_sum.shape[0]
        rstd = rstd8[0:1, :]

        def body(i, total):
            at = pl.ds(i * 16, 16)
            there = pl.ds(pl.multiple_of(place * width + i * 16, 16), 16)
            pushed = gn_sum[at, :]
            if k == 0:
                gn[at, :] = pushed.astype(BF16)
            product = hx[there, Q:].astype(F32) * pushed
            scaled = product * rstd
            summed = scaled[:, :128]
            for tile in range(1, scaled.shape[1] // 128):
                summed = summed + scaled[:, tile * 128 : (tile + 1) * 128]
            gsum[at, :] = summed
            product = product * gain[0, there, 0:1]
            return total + product[:8] + product[8:]

        total = lax.fori_loop(0, width // 16, body, jnp.zeros((8, rstd.shape[1]), F32), unroll=2)
        total = rstd * total_rows(total)
        stat[...] = total if k == 0 else stat[...] + total
        small[6:7, pl.ds(pl.multiple_of(place * width, 128), width)] = lane_sums(gsum[...])[0:1]

    def begin_rows():
        channels = rows_given[0].shape[1]
        small[0 : CONV + 1, :channels] = rows_given[0][0 : CONV + 1, :]
        small[CONV + 1 : CONV + 2, :channels] = rows_given[1][0:1, :]
        small[7:8, : rows_given[2].shape[1]] = rows_given[2][0:1, :]
        for k in range(3):
            small[8:9, k * 128 : (k + 1) * 128] = rows_given[3][k : k + 1, :]

    def begin():
        small[...] = jnp.zeros_like(small)
        if has_gn:
            spread(gain8, gain)
        else:
            small[6:7, : gain_row.shape[1]] = gain_row[...]
        if not fused:
            begin_rows()

    def send_norm():
        if fused:
            begin()
        prepare(0, 1 - col)
        later["others"].append(start(far(gn, gn_come, sems_other, 0, "col", cols[1])))

    def send_small():
        if fused:
            begin_rows()
        if has_gn:
            prepare(1, col)
        later["small1"] = start(far(small, small_a.at[0], sems_small, 0, "row", row ^ 1))
        later["others"] += [start(far(stat, stat_out.at[col], sems_other, k, "col", cols[k])) for k in range(1, n_col)]
        stat_out[col] = stat[...]

    def small_pair():
        later["small1"].wait_recv()
        small_a[1] = small[...] + small_a[0]
        later["small2"] = start(far(small_a.at[1], small_b.at[0], sems_small, 1, "row", row ^ 2))

    def small_dp():
        later["small2"].wait_recv()
        small_b[1] = small_a[1] + small_b[0]
        later["small3"] = [start(far(small_b.at[1], small_c.at[k], sems_small, 1 + k, "dp", dps[k])) for k in range(1, n_dp)]

    def small_col():
        for copy in later["small3"]:
            copy.wait_recv()
        total = small_b[1]
        for k in range(1, n_dp):
            total = total + small_c[k]
        small_out[col] = total
        later["small4"] = [start(far(small_out.at[col], small_out.at[col], sems_small, n_dp + k, "col", cols[k])) for k in range(1, n_col)]

    def state_col():
        state_a[0] = outs[0][:, : state_a.shape[2]]
        later["state1"] = [start(far(state_a.at[0], state_a.at[k], sems_state, k - 1, "col", cols[k])) for k in range(1, n_col)]

    def state_dp():
        for copy in later["state1"]:
            copy.wait_recv()
        total = state_a[0]
        for k in range(1, n_col):
            total = total + state_a[k]
        state_b[...] = total.astype(state_b.dtype)
        state_out[here, :] = state_b[...]
        later["state2"] = [start(far(state_b, state_out.at[here], sems_state, n0 + k - 1, "dp", dps[k])) for k in range(1, n_dp)]

    def state_row():
        for copy in later["state2"]:
            copy.wait_recv()
        later["state3"] = start(far(state_out.at[group(row)], state_out.at[group(row)], sems_state, n1, "row", row ^ 2))

    def state_pair():
        later["state3"].wait_recv()
        later["state4"] = [start(far(state_out.at[group(r)], state_out.at[group(r)], sems_state, n1 + 1 + k, "row", row ^ 1))
                           for k, r in enumerate((row, row ^ 2))]

    def norm_back():
        for copy in later["others"]:
            copy.wait_recv()
        if not has_gn:
            return
        hx, grad_out = held(5), held(6)
        rstd = rstd8[0:1, :]
        total = stat_out[0]
        for k in range(1, n_col):
            total = total + stat_out[k]
        own = gn_sum.shape[0]
        width = n_col * own
        pull = (rstd * rstd) * (total / width)

        def body(i, _):
            at = pl.ds(i * 16, 16)
            there = pl.ds(pl.multiple_of(col * own + i * 16, 16), 16)
            pushed = gn_sum[at, :] + gn_come[at, :].astype(F32)
            grad_in[at, :] = (grad_out[at, :].astype(F32) + (rstd * gain[0, there, 0:1]) * pushed
                              - hx[there, Q:].astype(F32) * pull).astype(BF16)
            return 0

        lax.fori_loop(0, own // 16, body, 0, unroll=2)

    ahead_of = {}
    if fused:
        ahead_of = {4: [take_rim_bc], 6: [take_rim]}
        extra = {0: [send_rim], 2: [state_back], 4: [lambda: product(1 - col, 1)], 7: [lambda: product(1 - col, 0), send_norm],
                 8: [lambda: product(col, 1)], 10: [lambda: product(col, 0), send_small, state_col], 12: [state_dp, small_pair],
                 13: [state_row, small_dp], 14: [state_pair, small_col], 15: [norm_back]}
    elif has_gn:
        extra = {1: [lambda: product(1 - col, 1)], 2: [lambda: product(1 - col, 0), send_norm], 4: [lambda: product(col, 1)],
                 6: [lambda: product(col, 0), send_small], 8: [state_col, small_pair], 10: [state_dp, small_dp], 11: [state_row],
                 12: [small_col], 13: [state_pair, norm_back]}
    else:
        extra = {1: [send_small], 3: [small_pair], 4: [small_dp], 5: [small_col], 8: [state_col], 9: [state_dp, state_row],
                 10: [state_pair], 11: [norm_back]}
    for step in extra.get(0, ()):
        step()
    make(0)
    if fused:
        fetch(*range(9, 16), 3, 0, 8, 2, 4, 5, 6)
    else:
        begin()
    for t in range(1, max(count + 7, 17)):
        for step in ahead_of.get(t, ()):
            step()
        if t < count:
            make(t)
        if 0 <= t - 2 < count:
            sums.across(t - 2)
        if 0 <= t - 4 < count:
            sums.along(t - 4)
        if 0 <= t - 6 < count:
            sums.finish(t - 6)
        for step in extra.get(t, ()):
            step()
    for copy in later["small4"] + later["state4"]:
        copy.wait_recv()
    for k in range(len(loads)):
        held(k)
    for copy in started:
        copy.wait_send()
    for p in range(count):
        if p + slots >= count:
            sums.first(p).wait_send()
        sums.sent(p)


def close(sources, pieces, lefts, gbd, given, gn, plain, later, fused=()):
    n_row, n_dp, n_col = (lax.axis_size(axis) for axis in ("row", "dp", "col"))
    assert n_row == 4
    rows, tokens = lefts[0].shape
    widths = [max(at + width for a, at, width in pieces if a == k) for k in range(len(sources))]
    half, quarter, block = rows // 2, rows // 4, rows // 4 // n_dp
    vmem, anywhere = pl.BlockSpec(memory_space=pltpu.VMEM), pl.BlockSpec(memory_space=pl.ANY)
    has_gn = gn is not None
    here = rows // n_col
    given = list(given)
    small = (16, max(rows, given[1 if fused else 0].shape[1]))
    channels = given[1].shape[1]
    extra = list(gn) if has_gn else list(plain)
    out = pl.pallas_call(
        functools.partial(close_kernel, n_row, n_dp, n_col, sources, pieces, has_gn, fused),
        in_specs=[vmem] * len(lefts) + ([SMEM] + [vmem] * 3 if fused else [vmem] * 5) + [vmem] * len(extra) + [anywhere] * len(later),
        out_specs=[vmem] * (len(sources) + 3 + has_gn),
        out_shape=[shape(F32, block, width) for width in widths]
        + [shape(BF16, rows, 2 * STATE), shape(F32, n_col, *small), shape(F32, n_col, 1, tokens)] + [shape(BF16, here, tokens)] * has_gn,
        scratch_shapes=[pltpu.VMEM((half, width), BF16) for width in widths] + [pltpu.VMEM((quarter, width), BF16) for width in widths]
        + [pltpu.VMEM(((n_dp - 1) * block, width), BF16) for width in widths]
        + [pltpu.VMEM((min(3 if fused else 4, len(pieces)), rows, max(width for _, _, width in pieces)), BF16)]
        + [pltpu.VMEM(value.shape, value.dtype) for value in later]
        + [pltpu.VMEM((2,) + small, F32), pltpu.VMEM((2,) + small, F32), pltpu.VMEM((n_dp,) + small, F32),
           pltpu.VMEM((n_col, block, 2 * STATE), F32), pltpu.VMEM((block, 2 * STATE), BF16),
           pltpu.SemaphoreType.DMA((2, len(pieces) * (n_dp + 1))), pltpu.SemaphoreType.DMA((2, n_dp + n_col)),
           pltpu.SemaphoreType.DMA((2, n_col + n_dp + 2)), pltpu.SemaphoreType.DMA((2, n_col)),
           pltpu.SemaphoreType.DMA((len(later),)), pltpu.VMEM(small, F32)]
        + ([pltpu.VMEM((here, tokens), F32), pltpu.VMEM((here, tokens), BF16), pltpu.VMEM((here, tokens), BF16), pltpu.VMEM((1, rows, 128), F32),
            pltpu.VMEM((here, 128), F32), pltpu.VMEM((1, tokens), F32)] if has_gn else [])
        + ([pltpu.VMEM((widths[0], tokens), BF16), pltpu.VMEM((8, (CONV + 1) * 2 * STATE), F32), pltpu.VMEM((2 * STATE, Q), F32),
            pltpu.VMEM((2 * STATE, Q), BF16), pltpu.VMEM((channels + 2 * STATE, Q), BF16), pltpu.VMEM((2 * STATE, Q), F32),
            pltpu.VMEM((CONV + 1, 2 * STATE, Q), F32), pltpu.VMEM((CONV + 1, 2 * STATE, Q), F32), pltpu.VMEM((2, 2 * STATE, Q), F32),
            pltpu.SemaphoreType.DMA((2, 2))] if fused else []),
        compiler_params=pltpu.CompilerParams(vmem_limit_bytes=61 * 1024 * 1024, collective_id=1, has_side_effects=True),
        cost_estimate=pl.CostEstimate(flops=10**6, bytes_accessed=10**8, transcendentals=0),
        name="close",
    )(*lefts, *([] if fused else [gbd]), *given, *extra, *later)
    count = len(sources)
    return out[:count], out[count], out[count + 1], out[count + 2], out[count + 3] if has_gn else None


def last_kernel(n_row, n_dp, n_col, heads, n_z, bd, x, state, small, *refs):
    refs = list(refs)
    take = lambda count: [refs.pop(0) for _ in range(count)]
    z_parts = take(n_z)
    norm_gain, inner, state_out, step, taps, bias, bc_taps, bc_bias, step_bias, decay, skip, gate = refs
    block = x.shape[0]
    at, channels = 0, inner.shape[2]
    for part in z_parts:
        count = min(part.shape[1], channels - at)
        inner[0, :, at : at + count] = part[:, :count]
        at += count
    inner[1] = x[:, :channels]
    for r in range(n_row):
        for d in range(n_dp):
            state_out[(d * n_row + r) * block : (d * n_row + r + 1) * block, :] = state[
                (r * n_dp + d) * block : (r * n_dp + d + 1) * block, :].astype(F32)
    step[...] = jnp.transpose(bd[:, 2 * STATE :])[:heads]
    by_col = lambda k: jnp.concatenate([small[c, k : k + 1, :channels] for c in range(n_col)], 1)
    for k in range(CONV):
        taps[k : k + 1, :] = by_col(CONV - 1 - k)
    bias[...] = by_col(CONV)
    gate[...] = by_col(CONV + 1)
    over = lambda k, at, count: sum(small[c, k : k + 1, at : at + count] for c in range(n_col))
    norm_gain[...] = over(6, 0, norm_gain.shape[1])
    for k in range(CONV):
        bc_taps[k : k + 1, :] = over(7, (CONV - 1 - k) * 2 * STATE, 2 * STATE)
    bc_bias[...] = over(7, CONV * 2 * STATE, 2 * STATE)
    for k, target in enumerate((step_bias, decay, skip)):
        target[...] = over(8, k * 128, 128)[:, : target.shape[1]]


def last(bd, x, state, small, z_parts, heads, channels):
    n_row, n_dp, n_col = (lax.axis_size(axis) for axis in ("row", "dp", "col"))
    block = x.shape[0]
    width = state.shape[0]
    row = lambda count: shape(F32, 1, count)
    return pl.pallas_call(
        functools.partial(last_kernel, n_row, n_dp, n_col, heads, len(z_parts)),
        out_shape=[row(width), shape(F32, 2, block, channels), shape(F32, width, 2 * STATE), shape(F32, heads, block),
                   shape(F32, CONV, n_col * channels), row(n_col * channels), shape(F32, CONV, 2 * STATE), row(2 * STATE),
                   row(n_col * heads), row(n_col * heads), row(n_col * heads), row(n_col * channels)],
        compiler_params=params(),
        cost_estimate=pl.CostEstimate(flops=10**6, bytes_accessed=10**7, transcendentals=0),
        name="last",
    )(bd, x, state, small, *z_parts)


def open_kernel(n_row, n_col, parts, hidden, inner, state_w, step_w, hx, x4, z_w, bd4, sems):
    row, col = lax.axis_index("row"), lax.axis_index("col")
    cols = [lax.rem(col + k, n_col) for k in range(n_col)]
    ahead, behind = lax.rem(row + 1, n_row), lax.rem(row + n_row - 1, n_row)
    partners = [("row", row ^ 1), ("row", row ^ 2), ("row", ahead), ("row", behind)] + [("col", c) for c in cols[1:]]
    meet(partners)
    width, tokens = hidden.shape
    each = inner.shape[0] // parts
    heads = step_w.shape[0]
    mine = pl.ds(pl.multiple_of(col * width, 16), width)
    counter = [0]
    started = []

    def start(source, target, axis, place):
        copy = far(source, target, sems, counter[0], axis, place)
        counter[0] += 1
        copy.start()
        started.append(copy)
        return copy

    rim = start(hidden.at[:, pl.ds(tokens - Q, Q)], hx.at[mine, pl.ds(0, Q)], "row", ahead)
    wide = [start(hidden, hx.at[mine, pl.ds(Q, tokens)], "col", cols[k]) for k in range(1, n_col)]
    part = lambda p: pl.ds(p * each, each)
    send = lambda p: start(x4.at[row, part(p)], x4.at[row, part(p)], "row", row ^ 2)

    def split(p):
        def body(i, _):
            at = pl.ds(p * each + i * 16, 16)
            x4[row, at, :] = inner[at, 1, :]
            z_w[at, :] = inner[at, 0, :]
            return 0

        lax.fori_loop(0, each // 16, body, 0, unroll=2)

    split(0)
    over = [send(0)]
    bd4[row, : 2 * STATE, :] = jnp.transpose(state_w[...].astype(F32)).astype(BF16)
    rest = bd4.shape[1] - 2 * STATE - heads
    bd4[row, 2 * STATE :, :] = jnp.concatenate([step_w[...], jnp.zeros((rest, step_w.shape[1]), BF16)], 0)
    bd_over = start(bd4.at[row], bd4.at[row], "row", row ^ 2)
    near = [start(bd4.at[row], bd4.at[row], "row", row ^ 1)]
    for p in range(1, parts):
        split(p)
        if p == 1:
            over.append(send(1))
    near.append(start(x4.at[row], x4.at[row], "row", row ^ 1))

    def keep_hidden(i, _):
        hx[pl.ds(pl.multiple_of(col * width + i * 16, 16), 16), pl.ds(Q, tokens)] = hidden[pl.ds(i * 16, 16), :]
        return 0

    lax.fori_loop(0, width // 16, keep_hidden, 0)
    rim.wait_recv()
    wide += [start(hx.at[mine, pl.ds(0, Q)], hx.at[mine, pl.ds(0, Q)], "col", cols[k]) for k in range(1, n_col)]
    bd_over.wait_recv()
    near.append(start(bd4.at[row ^ 2], bd4.at[row ^ 2], "row", row ^ 1))
    waited = []
    for p in range(parts):
        over[p].wait_recv()
        near.append(start(x4.at[row ^ 2, part(p)], x4.at[row ^ 2, part(p)], "row", row ^ 1))
        if p + 2 < parts:
            over[p].wait_send()
            waited.append(id(over[p]))
            over.append(send(p + 2))
    for copy in wide + near:
        copy.wait_recv()
    for copy in started:
        if id(copy) not in waited:
            copy.wait_send()


def open_up(hidden, inner, state_w, step_w):
    n_row, n_col = lax.axis_size("row"), lax.axis_size("col")
    assert n_row == 4
    channels, _, block = inner.shape
    heads = step_w.shape[0]
    parts = 4 if channels % 64 == 0 else 1
    vmem = pl.BlockSpec(memory_space=pltpu.VMEM)
    return pl.pallas_call(
        functools.partial(open_kernel, n_row, n_col, parts),
        in_specs=[vmem] * 4,
        out_specs=[vmem] * 4,
        out_shape=[shape(BF16, hidden.shape[0] * n_col, Q + hidden.shape[1]), shape(BF16, n_row, channels, block), shape(BF16, channels, block),
                   shape(BF16, n_row, 2 * STATE + heads + -heads % 32, block)],
        scratch_shapes=[pltpu.SemaphoreType.DMA((2, 5 + 2 * parts + 2 * (n_col - 1)))],
        compiler_params=pltpu.CompilerParams(vmem_limit_bytes=VMEM_LIMIT, collective_id=2, has_side_effects=True),
        cost_estimate=pl.CostEstimate(flops=0, bytes_accessed=10**8, transcendentals=0),
        name="open",
    )(hidden, inner, state_w, step_w)


def joined(w4_ref):
    return jnp.concatenate([w4_ref[j] for j in range(w4_ref.shape[0])], 1)


def by_distance(n_row, n_dp):
    row, dp = lax.axis_index("row"), lax.axis_index("dp")
    return [lax.rem(dp + k, n_dp) * n_row + (row ^ place) for place in sum_stages(n_row)[0] for k in range(n_dp)]


def put_by_distance(n_row, n_dp, source, target, skip):
    each = target.shape[0] // (n_row * n_dp)
    for k, place in enumerate(by_distance(n_row, n_dp)):
        target[k * each : (k + 1) * each, :] = source[pl.ds(pl.multiple_of(place * each, 32), each), skip:]


def project_kernel(n_row, n_dp, hb, lengths_ref, hx_ref, gain8_ref, x4_ref, bd4_ref, normed_ref, by_ref, rstd_ref, live_ref, xin_ref, bd_ref, dt_ref, gain_ref):
    @pl.when(pl.program_id(0) == 0)
    def _():
        spread(gain8_ref, gain_ref)
        width, count = hx_ref.shape

        def square(i, total):
            v = hx_ref[pl.ds(i * 16, 16), :].astype(F32)
            v = v * v
            return total + v[:8] + v[8:]

        total = lax.fori_loop(0, width // 16, square, jnp.zeros((8, count), F32), unroll=4)
        rstd = lax.rsqrt(jnp.sum(total, 0, keepdims=True) / width + EPS)
        rstd_ref[...] = jnp.broadcast_to(rstd[:, Q:], rstd_ref.shape)
        base, ends = scalars(lengths_ref, count - Q)
        live_ref[...] = (base + iota(live_ref.shape, 1) < ends[-1]).astype(F32)

        def norm(i, _):
            at = pl.ds(i * 16, 16)
            normed_ref[at, :] = (hx_ref[at, :].astype(F32) * rstd * gain_ref[0, at, 0:1]).astype(BF16)
            return 0

        lax.fori_loop(0, width // 16, norm, 0, unroll=4)
        put_by_distance(n_row, n_dp, normed_ref, by_ref, Q)
        bd = nn(joined(bd4_ref), normed_ref[...])
        bd_ref[...] = bd[: 2 * STATE]
        dt_ref[...] = jnp.zeros_like(dt_ref)
        for n in range(dt_ref.shape[0]):
            dt_ref[n, :hb, :] = bd[2 * STATE + n * hb : 2 * STATE + (n + 1) * hb, Q:]

    xin_ref[...] = nn(joined(x4_ref), normed_ref[...])


def second_kernel(n_row, n_dp, steps, hb, given, *refs):
    refs = list(refs)
    take = lambda count: [refs.pop(0) for _ in range(count)]
    far_refs = [take(2), take(2)]
    near_refs = [take(2), take(2)]
    normed, = take(1)
    grads = take(2 if given else 1)
    live, final, keep = take(3)
    z4, z, out4, gg, state_in, grad_by = take(6)
    whole_grad, come, came, kept, sems, sems_state = take(6)
    row, col = lax.axis_index("row"), lax.axis_index("col")
    n = pl.program_id(0)
    each = z4.shape[1]

    def piece(side, which, s):
        rows = pl.ds(s * each, each)
        return far(far_refs[side][which].at[rows], come.at[side, which, rows], sems, (side * 2 + which) * steps + s, "row", row ^ 1)

    def pieces(at):
        return [piece(at // steps, which, at % steps) for which in range(2)]

    def states():
        copies = []
        for k in range(1, n_row):
            there = lax.rem(row + k, n_row)
            copies.append(far(final, came.at[k - 1], sems_state, 2 * k - 2, "row", there))
            copies.append(far(keep, kept.at[k - 1], sems_state, 2 * k - 1, "row", there))
        return copies

    @pl.when(n == 0)
    def _():
        meet([("row", lax.rem(row + k, n_row)) for k in range(1, n_row)])
        for copy in states() + pieces(0) + pieces(1):
            copy.start()

    @pl.when(n == 0)
    def _():
        width = grads[0].shape[0]
        for place, source in zip((col, 1 - col) if given else (0,), grads):
            def body(i, _):
                at = pl.ds(pl.multiple_of(place * width + i * 16, 16), 16)
                whole_grad[at, :] = (source[pl.ds(i * 16, 16), :].astype(F32) * live[0:1, :]).astype(BF16)
                return 0

            lax.fori_loop(0, width // 16, body, 0, unroll=4)
        put_by_distance(n_row, n_dp, whole_grad, grad_by, 0)

    for at in range(2 * steps):
        @pl.when(n == at)
        def _():
            side = at // steps
            if at + 2 < 2 * steps:
                for copy in pieces(at + 2):
                    copy.start()
            for copy in pieces(at):
                copy.wait_recv()
            rows = slice(at % steps * each, (at % steps + 1) * each)
            w4, out = ((z4, z), (out4, gg))[side]
            w4[row] = near_refs[side][0][...]
            w4[row ^ 2] = near_refs[side][1][...]
            w4[row ^ 1] = come[side, 0, rows, :]
            w4[row ^ 3] = come[side, 1, rows, :]
            value = normed[:, Q:] if side == 0 else whole_grad[...]
            out[...] = nn(joined(w4), value)

    @pl.when(n == 2 * steps - 1)
    def _():
        for copy in states():
            copy.wait_recv()
        for head in range(final.shape[0] // HEADDIM):
            at = slice(head * HEADDIM, (head + 1) * HEADDIM)
            total, decay = None, None
            for k in range(1, n_row):
                part = jnp.where(row >= k, came[k - 1, at, :].astype(F32), 0.0)
                total = part if total is None else total + decay * part
                passing = kept[k - 1, head // hb, head % hb : head % hb + 1, :]
                decay = passing if decay is None else decay * passing
            state_in[at, :] = total
        for copy in states():
            copy.wait_send()
        for at in range(2 * steps):
            for copy in pieces(at):
                copy.wait_send()


def placed(value, index, count):
    out = jnp.zeros((count,) + value.shape, F32)
    return lax.dynamic_update_slice(out, value[None], (index,) + (0,) * value.ndim)


def turned(value, axis):
    return lax.all_gather(value, axis, axis=0, tiled=True)


def per_device(hidden_in, grad_out, lengths, norm_gain, inner_proj, state_proj, step_proj, conv_inner, conv_inner_bias,
               conv_state, conv_state_bias, step_bias, decay_log, skip_gain, gate_gain, out_proj):
    cols_here, rows = hidden_in.shape
    ncols = lax.axis_size("col")
    nrow = lax.axis_size("row")
    width = cols_here * ncols
    inner = inner_proj.shape[0]
    heads = step_proj.shape[0]
    col_index = lax.axis_index("col")
    nc = rows // Q
    hb = max(k for k in (1, 2, 3, 4) if heads % k == 0)
    nb = heads // hb
    bh = hb * HEADDIM


    gain_full = norm_gain.astype(F32)
    gain8 = jnp.broadcast_to(gain_full[None], (8, width))
    hx, x4, z_w, bd4 = open_up(hidden_in, inner_proj, state_proj, step_proj)
    out_w, grad_now, hx = lax.optimization_barrier((out_proj, grad_out, hx))
    z_far = swapped(z_w, "row", 2)
    z_far, out_w = lax.optimization_barrier((z_far, out_w))
    out_far = swapped(out_w, "row", 2)
    if ncols == 2:
        grads = [grad_now, swapped(grad_now, "col", 1)]
    else:
        grads = [lax.all_gather(grad_now, "col", axis=0, tiled=True)]

    bm = 2 * bh if nb % 2 == 0 else bh
    part4 = pl.BlockSpec((nrow, bm, width // nrow), lambda n: (0, n, 0))
    ext = rows + Q
    normed_ext, normed_by, rstd8, live8, xin, bdin, dt = pl.pallas_call(
        functools.partial(project_kernel, nrow, lax.axis_size("dp"), hb),
        grid=(inner // bm,),
        in_specs=[SMEM, whole(width, ext), whole(8, width), part4, whole(*bd4.shape)],
        out_specs=[whole(width, ext), whole(width, rows), whole(8, rows), whole(8, rows), pl.BlockSpec((bm, ext), lambda n: (n, 0)), whole(2 * STATE, ext), whole(nb, 8, rows)],
        out_shape=[shape(BF16, width, ext), shape(BF16, width, rows), shape(F32, 8, rows), shape(F32, 8, rows), shape(F32, inner, ext), shape(F32, 2 * STATE, ext), shape(F32, nb, 8, rows)],
        compiler_params=params(),
        scratch_shapes=[pltpu.VMEM((1, width, Q), F32)],
        cost_estimate=pl.CostEstimate(flops=8 * 10**9, bytes_accessed=20 * 10**6, transcendentals=0),
        name="project",
    )(lengths, hx, gain8, x4, bd4)
    rstd_in = rstd8[:1]
    by_head = jnp.pad(jnp.stack([step_bias, decay_log, skip_gain]), ((0, 5), (0, 128 - heads)))

    def taps_of(taps, bias):
        return jnp.pad(jnp.concatenate([taps, bias[None]], axis=0).astype(F32), ((0, 7 - CONV), (0, 0)))

    taps = taps_of(conv_inner, conv_inner_bias)
    bctaps = taps_of(conv_state, conv_state_bias)
    gate = jnp.broadcast_to(gate_gain.astype(F32)[None], (8, inner))

    tok = pl.BlockSpec((bh, rows), lambda n: (n, 0))
    tok_ext = pl.BlockSpec((bh, rows + Q), lambda n: (n, 0))
    eight = pl.BlockSpec((8, bh), lambda n: (0, n))
    bc_ext = pl.BlockSpec((2 * STATE, rows + Q), lambda n: (0, 0))
    state_spec = pl.BlockSpec((bh, STATE), lambda n: (n, 0))
    chunks = pl.BlockSpec((nc, bh, STATE), lambda n: (0, n, 0))
    rows_spec = pl.BlockSpec((1, 6, 8, rows), lambda n: (n, 0, 0, 0))
    head_tok = pl.BlockSpec((1, 8, rows), lambda n: (n, 0, 0))
    head_q = pl.BlockSpec((1, 8, Q), lambda n: (n, 0, 0))
    head8 = pl.BlockSpec((1, 8, 8), lambda n: (n, 0, 0))

    u, ubc, bc, rowpack, scores, y_in, fresh, final, keep, hpar = pl.pallas_call(
        functools.partial(enter_kernel, nc, hb),
        grid=(nb,),
        in_specs=[SMEM, tok_ext, bc_ext, whole(nb, 8, rows), whole(8, 128), eight, whole(8, 2 * STATE),
                  pl.BlockSpec(memory_space=pl.ANY)],
        out_specs=[tok, whole(2 * STATE, rows), whole(2 * STATE, rows), whole(nb, 6, 8, rows), whole(nc, Q, Q), tok, chunks,
                   state_spec, whole(nb, 8, Q), whole(nb, 8, 8)],
        out_shape=[shape(F32, inner, rows), shape(F32, 2 * STATE, rows), shape(F32, 2 * STATE, rows),
                   shape(F32, nb, 6, 8, rows), shape(F32, nc, Q, Q), shape(F32, inner, rows), shape(F32, nc, inner, STATE),
                   shape(BF16, inner, STATE), shape(F32, nb, 8, Q), shape(F32, nb, 8, 8)],
        scratch_shapes=[pltpu.VMEM((bh, STATE), F32), pltpu.VMEM((CONV + 1, bh, Q), F32), pltpu.VMEM((CONV + 1, 2 * STATE, Q), F32)],
        compiler_params=params(),
        cost_estimate=pl.CostEstimate(flops=3 * 10**10, bytes_accessed=40 * 10**6, transcendentals=0),
        name="enter",
    )(lengths, xin, bdin, dt, by_head, taps, bctaps, z_far)

    steps = inner // bm
    block = pl.BlockSpec((bm, width // nrow), lambda n: (jnp.minimum(n, steps - 1), 0))
    block_after = pl.BlockSpec((bm, width // nrow), lambda n: (jnp.maximum(n - steps, 0), 0))
    anywhere = pl.BlockSpec(memory_space=pl.ANY)
    second = pl.pallas_call(
        functools.partial(second_kernel, nrow, lax.axis_size("dp"), steps, hb, ncols == 2),
        grid=(2 * steps,),
        in_specs=[anywhere] * 4 + [block] * 2 + [block_after] * 2 + [whole(width, ext)] + [whole(*value.shape) for value in grads]
        + [whole(8, rows), whole(inner, STATE), whole(nb, 8, Q)],
        out_specs=[pl.BlockSpec((nrow, bm, width // nrow), lambda n: (0, jnp.minimum(n, steps - 1), 0)),
                   pl.BlockSpec((bm, rows), lambda n: (jnp.minimum(n, steps - 1), 0)),
                   pl.BlockSpec((nrow, bm, width // nrow), lambda n: (0, jnp.maximum(n - steps, 0), 0)),
                   pl.BlockSpec((bm, rows), lambda n: (jnp.maximum(n - steps, 0), 0)),
                   whole(inner, STATE), whole(width, rows)],
        out_shape=[shape(BF16, nrow, inner, width // nrow), shape(F32, inner, rows)] * 2 + [shape(F32, inner, STATE), shape(BF16, width, rows)],
        scratch_shapes=[pltpu.VMEM((width, rows), BF16), pltpu.VMEM((2, 2, inner, width // nrow), BF16), pltpu.VMEM((nrow - 1, inner, STATE), BF16),
                        pltpu.VMEM((nrow - 1, nb, 8, Q), F32), pltpu.SemaphoreType.DMA((2, 4 * steps)),
                        pltpu.SemaphoreType.DMA((2, 2 * (nrow - 1)))],
        compiler_params=pltpu.CompilerParams(vmem_limit_bytes=VMEM_LIMIT, collective_id=3, has_side_effects=True),
        cost_estimate=pl.CostEstimate(flops=10**10, bytes_accessed=30 * 10**6, transcendentals=0),
        name="second",
    )(z_w, z_far, out_w, out_far, z_w, z_far, out_w, out_far, normed_ext, *grads, live8, final, keep)
    z4, z, out4, grad_gated, state_in, grad_by = second

    y, states, stats = pl.pallas_call(
        functools.partial(across_kernel, nc, hb),
        grid=(nb,),
        in_specs=[tok, chunks, state_spec, whole(2 * STATE, rows), rows_spec, tok, tok, eight],
        out_specs=[tok, chunks, whole(2, 8, rows)],
        out_shape=[shape(F32, inner, rows), shape(F32, nc, inner, STATE), shape(F32, 2, 8, rows)],
        scratch_shapes=[pltpu.VMEM((bh, STATE), F32), pltpu.VMEM((1, bh, Q), F32)],
        compiler_params=params(),
        cost_estimate=pl.CostEstimate(flops=10**10, bytes_accessed=35 * 10**6, transcendentals=0),
        name="across",
    )(y_in, fresh, state_in, bc, rowpack, z, grad_gated, gate)

    sums = col_sum(jnp.sum(stats, axis=1))
    inner_width = inner * ncols
    rstd_gate = lax.rsqrt(sums[0] / inner_width + EPS)
    pull = rstd_gate * rstd_gate * rstd_gate * (sums[1] / inner_width)
    token_rows = jnp.concatenate([rstd_gate[None], pull[None], jnp.zeros((6, rows), F32)], axis=0)

    gated, grad_z, grad_y, adj, adj_first, ggate = pl.pallas_call(
        functools.partial(gate_kernel, nc, hb),
        grid=(nb,),
        in_specs=[tok, tok, tok, whole(8, rows), eight, whole(2 * STATE, rows), rows_spec],
        out_specs=[tok, tok, tok, chunks, state_spec, eight],
        out_shape=[shape(BF16, inner, rows), shape(BF16, inner, rows), shape(F32, inner, rows),
                   shape(F32, nc, inner, STATE), shape(BF16, inner, STATE), shape(F32, 8, inner)],
        scratch_shapes=[pltpu.VMEM((bh, STATE), F32), pltpu.VMEM((bh, Q), F32), pltpu.VMEM((1, bh, Q), F32)],
        compiler_params=params(),
        cost_estimate=pl.CostEstimate(flops=10**10, bytes_accessed=40 * 10**6, transcendentals=0),
        name="gate",
    )(y, z, grad_gated, token_rows, gate, bc, rowpack)

    adj_in = chained(adj_first, keep, hb, -1)
    def turned_product(w4, value):
        return lax.dot_general(w4, value, (((1,), (0,)), ((), ())), preferred_element_type=F32).reshape(-1, rows)

    def halves_of_features(products):
        return [sum(turned_product(lax.dynamic_slice_in_dim(w4, at * (nrow // 2), nrow // 2, 0), value) for w4, value in products)
                for at in (1 - col_index, col_index)]

    if ncols == 2:
        mixed_other, mixed = halves_of_features([(out4, gated)])
        mixed_come = swapped(mixed_other.astype(BF16), "col", 1)

    n_dp = lax.axis_size("dp")
    early, grads_early, first_z = {}, [], 0
    if nb >= 5 and inner % 768 == 0:
        first_z = inner // 3
        grads_early = [nt(grad_by, gated).astype(BF16), nt(normed_by, grad_z[:first_z]).astype(BF16)]
        each = inner // 6
        places = [(0, k * each, each) for k in range(6)] + [(1, k * each, each) for k in range(2)]
        early = {"pieces": places, "groups": [(2 * k, 2 * k + 1) for k in range(4)], "steps": nb}
    quarter = width // 4
    once = pl.Buffered(1)
    held = pl.BlockSpec(memory_space=pltpu.VMEM)
    back_out = pl.pallas_call(
        functools.partial(back_kernel, nc, hb, heads, early, n_dp),
        grid=(nb,),
        in_specs=[SMEM, tok, tok_ext, tok, tok, chunks, chunks, state_spec, whole(2 * STATE, rows), whole(nc, Q, Q), rows_spec, head8, eight]
        + [pl.BlockSpec(value.shape, lambda n: (0, 0), pipeline_mode=once) for value in grads_early],
        out_specs=[tok, pl.BlockSpec((bh, Q), lambda n: (n, 0)), pl.BlockSpec((bh, Q), lambda n: (n, 0)), eight, head_tok,
                   whole(nc, Q, Q), whole(2 * STATE, rows), whole(8, Q)] + [whole(quarter // n_dp, value.shape[1]) for value in grads_early],
        out_shape=[shape(BF16, inner, rows), shape(F32, inner, Q), shape(BF16, inner, Q), shape(F32, 8, inner), shape(F32, nb, 8, rows),
                   shape(F32, nc, Q, Q), shape(F32, 2 * STATE, rows), shape(F32, 8, Q)]
        + [shape(F32, quarter // n_dp, value.shape[1]) for value in grads_early],
        scratch_shapes=[pltpu.VMEM((bh, STATE), F32), pltpu.VMEM((bh, Q), F32), pltpu.VMEM((CONV + 1, bh, Q), F32),
                        pltpu.VMEM((5, nb, 8, rows), F32), pltpu.VMEM((CONV + 1, bh, Q), F32), pltpu.VMEM((2, bh, Q), F32)]
        + ([pltpu.VMEM((8, 2 * quarter, each), BF16), pltpu.VMEM((8, quarter, each), BF16),
            pltpu.VMEM((8, quarter // n_dp * (n_dp - 1), each), BF16), pltpu.SemaphoreType.DMA((2, 8 * (n_dp + 1)))] if early else []),
        compiler_params=pltpu.CompilerParams(vmem_limit_bytes=VMEM_LIMIT, collective_id=4, has_side_effects=True) if early else params(),
        cost_estimate=pl.CostEstimate(flops=6 * 10**10, bytes_accessed=50 * 10**6, transcendentals=0),
        name="back",
    )(lengths, u, xin, grad_y, y, states, adj, adj_in, bc, scores, rowpack, hpar, taps, *grads_early)
    gx, gx_last, rim_x, gtaps, gdt, gscores, gbct, hsum = back_out[:8]
    if ncols == 2:
        mixed_come, gx = lax.optimization_barrier((mixed_come, gx))

    if ncols == 2:
        mixed = mixed + mixed_come.astype(F32)
    else:
        mixed = lax.psum_scatter(turned_product(out4, gated).astype(BF16), "col", scatter_dimension=0, tiled=True).astype(F32)
    hidden_f = hidden_in.astype(F32)
    block_out = (hidden_f + live8[:1] * mixed).astype(BF16)

    small_width = -(-(2 * STATE + heads) // 128) * 128
    fused = ncols == 2 and bool(early)
    each = inner // 6 if inner % 768 == 0 else inner + -inner % 128
    sources = [(0, 0, None), (0, 0, 0), (0, first_z, 1)]
    pieces = [(0, 0, 2 * STATE), (0, 2 * STATE, small_width - 2 * STATE)]
    z_pieces = [(2, at, each) for at in range(0, inner - first_z, each)]
    x_pieces = [(1, at, each) for at in range(0, inner, each)]
    if inner % 768 == 0:
        x_pieces[-1:] = [(1, inner - each, each // 2), (1, inner - each // 2, each // 2)]
    pieces = z_pieces + pieces + x_pieces if fused else pieces + z_pieces + x_pieces
    gbd = None
    if not fused:
        vmem = pl.BlockSpec(memory_space=pltpu.VMEM)
        gbc, gbc_last, rim_bc, gbctaps = pl.pallas_call(
            functools.partial(state_kernel, nc),
            grid=(1,),
            out_shape=[shape(BF16, 2 * STATE, rows), shape(F32, 2 * STATE, Q), shape(BF16, 2 * STATE, Q),
                       shape(F32, 8, (CONV + 1) * 2 * STATE)],
            in_specs=[SMEM, vmem, vmem, bc_ext, vmem, vmem, vmem],
            out_specs=[vmem] * 4,
            scratch_shapes=[pltpu.VMEM((2 * STATE, Q), F32), pltpu.VMEM((CONV + 1, 2 * STATE, Q), F32),
                            pltpu.VMEM((CONV + 1, 2 * STATE, Q), F32), pltpu.VMEM((2, 2 * STATE, Q), F32)],
            compiler_params=params(),
            cost_estimate=pl.CostEstimate(flops=10**9, bytes_accessed=6 * 10**6, transcendentals=0),
            name="state",
        )(lengths, bc, ubc, bdin, bctaps, gscores, gbct)

        def last_tokens(value, last, rim):
            return lax.dynamic_update_slice(value, (last + rim.astype(F32)).astype(BF16), (0, rows - Q))

        back_x, back_bc = from_before(rim_x, -1), from_before(rim_bc, -1)
        gx = last_tokens(gx, gx_last, back_x)
        gbd = jnp.concatenate([last_tokens(gbc, gbc_last, back_bc), gdt[:, :hb].reshape(heads, rows).astype(BF16),
                               jnp.zeros((bd4.shape[1] - 2 * STATE - heads, rows), BF16)], axis=0)

        gbd_padded = jnp.pad(gbd, ((0, small_width - gbd.shape[0]), (0, 0)))
    lefts, later = [normed_by], [gx, grad_z]
    if ncols == 2:
        later += [x4, z4, bd4, hx, grad_out]
        gn_given, plain = (gain8, rstd8), None
        if fused:
            later += [rim_x, gx_last, bc, ubc, bdin, bctaps, gscores, gbct, gdt]
    else:
        grad_normed = turned_product(z4, grad_z) + turned_product(x4, gx) + turned_product(bd4, gbd)
        whole_rows = hx[:, Q:].astype(F32) * rstd_in
        gain_here = lax.dynamic_slice_in_dim(gain_full, col_index * cols_here, cols_here)[:, None]
        gn_given, plain = None, (jnp.sum(whole_rows * gain_full[:, None] * grad_normed, axis=0)[None], jnp.sum(whole_rows * grad_normed, axis=1)[None])
        gn_here = lax.psum_scatter(grad_normed.astype(BF16), "col", scatter_dimension=0, tiled=True).astype(F32)
    if not early:
        sources.append((1, 0, len(later)))
        lefts.append(grad_by)
        later.append(gated)
        pieces += [(3, at, each) for at in range(0, inner, each)]
    sums, state_out, small_out, stat_out, grad_in = close(
        sources, pieces, lefts, None if fused else gbd_padded, (lengths, gtaps, ggate, hsum) if fused else (gtaps, ggate, gbctaps, hsum),
        gn_given, plain, later, (nc, hb, len(later)) if fused else ())
    if ncols != 2:
        stat_total = jnp.sum(stat_out, axis=0)
        grad_in = (grad_out.astype(F32) + rstd_in * gain_here * gn_here - hidden_f * (rstd_in * rstd_in) * (stat_total / width)).astype(BF16)
    g_out = back_out[8] if early else sums[3][:, :inner]
    (g_norm_gain, g_inner, g_state, g_step, g_taps, g_bias, g_bc_taps, g_bc_bias, g_step_bias, g_decay, g_skip, g_gate) = last(
        sums[0], sums[1], state_out, small_out, [back_out[9], sums[2]] if early else [sums[2]], heads, inner)
    return (
        block_out,
        grad_in,
        g_norm_gain[0],
        jnp.transpose(g_inner, (2, 0, 1)),
        g_state,
        g_step,
        g_taps,
        g_bias[0],
        g_bc_taps,
        g_bc_bias[0],
        g_step_bias[0],
        g_decay[0],
        g_skip[0],
        g_gate[0],
        g_out.T,
    )


def solution(mesh):
    col, tokens, sums = P("col"), P("col", ("dp", "row")), P("col", ("dp", "row"))
    return jax.shard_map(
        per_device,
        mesh=mesh,
        in_specs=(tokens, tokens, P("dp", None), P(), P("col", None, "row"), P("row", None), P("col", "row"),
                  P(None, "col"), col, P(), P(), col, col, col, col, P("col", "row")),
        out_specs=(tokens, tokens, P(), P("col", None, ("dp", "row")), P(), sums, P(), P(), P(), P(), P(), P(), P(), P(), sums),
        check_vma=False,
    )
```
